32 devices in a mesh: dp: 8 (over y, x, core), tensor: 4 (over z).
Axes of the slice: x: 2, y: 2, z: 4, core: 2. Of those that a mesh axis runs over, the one named last changes fastest.
Arguments:
- inputs: bfloat16 [8, 4096, 1024], P('dp', 'tensor'), may hold values from -6 to 6
- skip_input: bfloat16 [8, 4096, 1024], P('dp', 'tensor'), may hold values from -6 to 6
- lengths: int32 [8, 4], P('dp'), may hold values from 1 to 2048, 4096 in all within a row
- time_steps: int32 [8, 4], P('dp'), may hold values from 0 to 999
- w_skip_in: bfloat16 [1024, 1024], replicated, may hold values from -0.125 to 0.125
- w_skip_res: bfloat16 [1024, 1024], replicated, may hold values from -0.125 to 0.125
- w_ada: bfloat16 [256, 4096], replicated, may hold values from -0.375 to 0.375
- w_qkv: bfloat16 [3, 1024, 1024], P(None, None, 'tensor'), may hold values from -0.1875 to 0.1875
- w_out: bfloat16 [1024, 1024], P('tensor'), may hold values from -1.5 to 1.5
- w_up: bfloat16 [1024, 4096], P(None, 'tensor'), may hold values from -0.1875 to 0.1875
- w_down: bfloat16 [4096, 1024], P('tensor'), may hold values from -0.09375 to 0.09375
- cotangent: bfloat16 [8, 4096, 1024], P('dp', 'tensor'), may hold values from -6 to 6
Outputs:
- block_out: float32 [8, 4096, 1024], P('dp', 'tensor')
- grad_inputs: float32 [8, 4096, 1024], P('dp', 'tensor')
- grad_skips: float32 [8, 4096, 1024], P('dp', 'tensor')
- grad_skip_in: float32 [1024, 1024], replicated
- grad_skip_res: float32 [1024, 1024], replicated
- grad_ada: float32 [256, 4096], replicated
- grad_qkv: float32 [3, 1024, 1024], P(None, None, 'tensor')
- grad_out_proj: float32 [1024, 1024], P('tensor')
- grad_up: float32 [1024, 4096], P(None, 'tensor')
- grad_down: float32 [4096, 1024], P('tensor')
The draws below stay inside these ranges and needn't reach their ends.
Inputs may be any that keep to these rules, and one draw needn't show every extreme that they name: The 4 lengths of each row add up to 4096, and the longest of each row has exactly 2048 frames.
All inputs are finite; a program needn't handle non-finite values.
Results may differ from the reference program's by a relative error of at most 0.018.
Values may be sent and summed in bfloat16 or wider, within the bound.
A program may use at most 384 MiB of HBM per device.

```python
import math
import jax
import jax.numpy as jnp
import numpy as np
from jax import lax

D = 1024
HEADS = 16
HEAD_DIM = 64
FF = 4096
TIME_DIM = 256
ROW_LEN = 4096
UTT = 4
ROWS = 8


def with_ends(entries, stream_key, low, top_value):
    dims = entries.shape
    index_at = [jax.random.randint(jax.random.fold_in(stream_key, axis), (), 0, dims[axis]) for axis in range(len(dims))]
    entries = entries.at[tuple(index_at)].set(low)
    longest = dims.index(max(dims))
    index_at[longest] = (index_at[longest] + 1) % dims[longest]
    return entries.at[tuple(index_at)].set(top_value)


def block_levels(stream_key, shape, cuts, smallest, largest):
    factor_of = 1.0
    for axis_at, blocks in cuts:
        steps = jax.random.uniform(jax.random.fold_in(jax.random.fold_in(stream_key, 6), axis_at), (blocks,), jnp.float32, smallest / len(cuts), largest / len(cuts))
        factor_of = factor_of * jnp.repeat(jnp.exp(steps), shape[axis_at] // blocks).reshape((-1,) + (1,) * (len(shape) - 1 - axis_at))
    return factor_of


def length_profile(count, total, bound, skew):
    loads = [(1 << 20) // math.isqrt(rank ** skew) + 1 for rank in range(2, count + 1)]
    spare, holding = total - bound - (count - 1), [1] * (count - 1)
    while spare > 0:
        movable = [i for i in range(count - 1) if holding[i] < bound]
        pool, budget = sum([loads[i] for i in movable]), spare
        for i in movable:
            extra = min(bound - holding[i], max(1, budget * loads[i] // pool), spare)
            holding[i] = holding[i] + extra
            spare = spare - extra
    return np.array([bound] + holding)


def uneven(key, amount, total, bound, slope):
    if amount == 2:
        one = jax.random.randint(key, (), max(1, total - bound), min(bound, total - 1) + 1)
        return jnp.stack([one, total - one])
    sizes = jnp.asarray(length_profile(amount, total, bound, slope), jnp.int32)
    twos = (amount - 1) // 2
    source_of, taker = sizes[1:1 + 2 * twos:2], sizes[2:2 + 2 * twos:2]
    margin = jnp.minimum(source_of - 1, bound - taker)
    moved = jax.random.randint(jax.random.fold_in(key, 1), (twos,), 0, 1 << 20) % (margin + 1)
    sizes = sizes.at[1:1 + 2 * twos:2].set(source_of - moved).at[2:2 + 2 * twos:2].set(taker + moved)
    return sizes[jax.random.permutation(jax.random.fold_in(key, 2), amount)]


def noise(stream_key, shape, deviation, most, cuts=(), held_as=jnp.bfloat16):
    entries = jax.random.normal(stream_key, shape, jnp.float32) * deviation
    if len(cuts) > 0:
        entries = block_levels(stream_key, shape, cuts, -0.22, 0.18) * entries
    return jnp.clip(entries, min=-most, max=most).astype(held_as)


def setup_inputs(seed: int = 0) -> dict:
    arg_keys = jax.random.split(jax.random.key(seed), 13)
    return {
        "inputs": noise(arg_keys[0], (ROWS, ROW_LEN, D), 1.0, 6.0, ((0, 8), (1, 4))),
        "skip_input": noise(arg_keys[1], (ROWS, ROW_LEN, D), 1.0, 6.0, ((0, 8), (1, 4))),
        "lengths": jax.vmap(lambda own: uneven(own, UTT, ROW_LEN, ROW_LEN // 2, 1))(jax.random.split(arg_keys[2], ROWS)).reshape((ROWS, UTT)).astype(jnp.int32),
        "time_steps": with_ends(jax.random.randint(arg_keys[3], (ROWS, UTT), 0, 1000), jax.random.fold_in(arg_keys[3], 1), 0, 999).astype(jnp.int32),
        "w_skip_in": noise(arg_keys[4], (D, D), (2 * D) ** -0.5, 0.125),
        "w_skip_res": noise(arg_keys[5], (D, D), (2 * D) ** -0.5, 0.125),
        "w_ada": noise(arg_keys[6], (TIME_DIM, 4 * D), TIME_DIM ** -0.5, 0.375),
        "w_qkv": noise(arg_keys[7], (3, D, D), D ** -0.5, 0.1875, ((2, 4),)),
        "w_out": noise(arg_keys[8], (D, D), (D // 64) ** -0.5, 1.5, ((0, 4),)),
        "w_up": noise(arg_keys[9], (D, FF), D ** -0.5, 0.1875, ((1, 4),)),
        "w_down": noise(arg_keys[10], (FF, D), FF ** -0.5, 0.09375, ((0, 4),)),
        "cotangent": noise(arg_keys[11], (ROWS, ROW_LEN, D), 1.0, 6.0, ((0, 8), (1, 4))),
    }


@jax.custom_vjp
def low(v):
    return lax.optimization_barrier(v.astype(jnp.bfloat16)).astype(jnp.float32)

@jax.custom_vjp
def low_back(v):
    return v

def low_keep(v):
    return (low(v), None)

def low_pass(kept, grad):
    return (grad,)

def back_keep(v):
    return (v, None)

def back_low(kept, grad):
    return (low(grad),)
low.defvjp(low_keep, low_pass)
low_back.defvjp(back_keep, back_low)

def highest(pattern, left_side, right_side):
    return jnp.einsum(pattern, left_side, right_side, precision=lax.Precision.HIGHEST)

def modulated_norm(hidden, shift_part, scale_part):
    center = hidden - lax.optimization_barrier(jnp.mean(hidden, axis=-1, keepdims=True))
    spread = lax.optimization_barrier(jnp.mean(center * center, axis=-1, keepdims=True))
    return center * lax.rsqrt(spread + 1e-06) * (1.0 + scale_part) + shift_part

def rotate_heads(values, cosine_table, sine_table):
    half_width = values.shape[-1] // 2
    first_half = values[..., :half_width]
    second_half = values[..., half_width:]
    return jnp.concatenate([first_half * cosine_table - second_half * sine_table, second_half * cosine_table + first_half * sine_table], axis=-1)

def row_layout(lengths_row, steps_row):
    ends_at = jnp.cumsum(lengths_row, dtype=jnp.int32)
    starts_at = ends_at - lengths_row
    positions = jnp.arange(ROW_LEN, dtype=jnp.int32)
    segment = lax.optimization_barrier(jnp.sum((positions[:, None] >= ends_at[None, :]).astype(jnp.int32), axis=1, dtype=jnp.int32))
    member = segment[:, None] == jnp.arange(UTT, dtype=jnp.int32)[None, :]
    offsets = lax.optimization_barrier(jnp.sum(jnp.where(member, starts_at[None, :], 0), axis=1, dtype=jnp.int32))
    places = (positions - offsets).astype(jnp.float32)
    rotary_rate = jnp.exp(-math.log(10000.0) * (2.0 * jnp.arange(HEAD_DIM // 2, dtype=jnp.float32) / HEAD_DIM))
    angles = places[:, None, None] * rotary_rate
    time_rate = jnp.exp(-math.log(10000.0) * (jnp.arange(TIME_DIM // 2, dtype=jnp.float32) / (TIME_DIM // 2)))
    phases = steps_row.astype(jnp.float32)[:, None] * time_rate
    embedding = jnp.concatenate([jnp.sin(phases), jnp.cos(phases)], axis=-1)
    return (segment, jnp.cos(angles), jnp.sin(angles), embedding)

def attention(query_rot, key_rot, value_low, segment):
    block_rows = min(512, ROW_LEN // 2)
    scale_value = HEAD_DIM ** (-0.5)

    def one_block(block_index):
        block_start = block_index * block_rows
        query_block = lax.dynamic_slice_in_dim(query_rot, block_start, block_rows, 0)
        segment_block = lax.dynamic_slice_in_dim(segment, block_start, block_rows, 0)
        scores = low_back(highest('qhe,khe->hqk', query_block, key_rot) * scale_value)
        allowed = (segment_block[:, None] == segment[None, :])[None]
        masked = jnp.where(allowed, scores, -1e+30)
        row_peak = lax.optimization_barrier(jnp.max(masked, axis=-1, keepdims=True))
        weights = jnp.exp(masked - row_peak)
        prob_rows = weights / lax.optimization_barrier(jnp.sum(weights, axis=-1, keepdims=True))
        return highest('hqk,khe->qhe', low(prob_rows), value_low)
    blocks = lax.map(jax.checkpoint(one_block), jnp.arange(ROW_LEN // block_rows, dtype=jnp.int32))
    return blocks.reshape(ROW_LEN, HEADS * HEAD_DIM)

def row_forward(inputs_wide, skips_wide, matrices, segment, cosine_table, sine_table, embedding):
    w_skip_in, w_skip_res, w_ada, w_qkv, w_out, w_up, w_down = matrices
    base_stream = low_back(highest('ld,de->le', inputs_wide, w_skip_in) + highest('ld,de->le', skips_wide, w_skip_res))
    per_utterance = highest('ut,tm->um', low(jax.nn.silu(embedding)), w_ada)
    shift_one, scale_one, shift_two, scale_two = jnp.split(per_utterance[segment], 4, axis=-1)
    normed = low(modulated_norm(base_stream, shift_one, scale_one))
    projected = highest('ld,kde->kle', normed, w_qkv)
    head_shape = (ROW_LEN, HEADS, HEAD_DIM)
    query_rot = low(rotate_heads(low_back(projected[0]).reshape(head_shape), cosine_table, sine_table))
    key_rot = low(rotate_heads(low_back(projected[1]).reshape(head_shape), cosine_table, sine_table))
    value_low = low(low_back(projected[2])).reshape(head_shape)
    context = low(low_back(attention(query_rot, key_rot, value_low, segment)))
    hidden_one = base_stream + low_back(highest('le,ed->ld', context, w_out))
    ffn_in = low(modulated_norm(hidden_one, shift_two, scale_two))
    before = low_back(highest('ld,df->lf', ffn_in, w_up))
    activated = low(jax.nn.gelu(before, approximate=True))
    return hidden_one + highest('lf,fd->ld', activated, w_down)

def reference(inputs, skip_input, lengths, time_steps, w_skip_in, w_skip_res, w_ada, w_qkv, w_out, w_up, w_down, cotangent):
    weights = tuple((matrix.astype(jnp.float32) for matrix in (w_skip_in, w_skip_res, w_ada, w_qkv, w_out, w_up, w_down)))

    def one_row(totals, row_data):
        inputs_row, skips_row, lengths_row, steps_row, cot_row = row_data
        segment, cosine_table, sine_table, embedding = row_layout(lengths_row, steps_row)

        def forward(inputs_wide, skips_wide, matrices):
            return row_forward(inputs_wide, skips_wide, matrices, segment, cosine_table, sine_table, embedding)
        row_out, pull_back = jax.vjp(forward, inputs_row.astype(jnp.float32), skips_row.astype(jnp.float32), weights)
        grad_in, grad_skip, grad_mats = pull_back(cot_row.astype(jnp.float32))
        totals = tuple((total_now + grad_now for total_now, grad_now in zip(totals, grad_mats)))
        return (totals, (row_out, grad_in, grad_skip))
    zero_sums = tuple((jnp.zeros(matrix.shape, jnp.float32) for matrix in weights))
    totals, (block_out, grad_inputs, grad_skips) = lax.scan(one_row, zero_sums, (inputs, skip_input, lengths, time_steps, cotangent))
    return (block_out, grad_inputs, grad_skips, totals[0], totals[1], totals[2], totals[3], totals[4], totals[5], totals[6])
```

```python
import functools
import math

import jax
import jax.numpy as jnp
from jax import lax
from jax.experimental import pallas as pl
from jax.experimental.pallas import tpu as pltpu
from jax.sharding import PartitionSpec as P

HEAD_DIM = 64
LANES = 128
MASKED = -1e30
LOG2E = math.log2(math.e)
MIB = 2**20
BF = jnp.bfloat16
F32 = jnp.float32
norm_epsilon = 1e-06
NT = (((1,), (1,)), ((), ()))
TN = (((0,), (0,)), ((), ()))


def stored_block(block, own, per_part):
    shift = per_part.bit_length() - 1
    part = lax.shift_right_logical(block, shift)
    return ((part ^ own) << shift) | (block & (per_part - 1))


def swap_halves(values):
    lane = lax.broadcasted_iota(jnp.int32, values.shape, 1)
    return jnp.where(lane % 64 < 32, pltpu.roll(values, 96, 1), pltpu.roll(values, 32, 1))


def project_kernel(normed_ref, weight_ref, cos_ref, sin_ref, out_ref, *, pairs):
    normed = normed_ref[...]
    cosine = cos_ref[...]
    sine = sin_ref[...]
    width = pairs * LANES
    for kind in range(3):
        weight = weight_ref[kind * width : (kind + 1) * width, :]
        part = lax.dot_general(normed, weight, NT, preferred_element_type=F32)
        for pair in range(pairs):
            cut = part[:, pair * LANES : (pair + 1) * LANES]
            if kind < 2:
                cut = cut * cosine + swap_halves(cut) * sine
            if kind == 0:
                cut = cut * (LOG2E * HEAD_DIM**-0.5)
            out_ref[pair * 3 + kind] = cut.astype(BF)


def project(normed_all, weight, cosine, sine, pairs):
    length, depth = normed_all.shape
    rows = 512
    return pl.pallas_call(
        functools.partial(project_kernel, pairs=pairs),
        grid=(length // rows,),
        in_specs=[
            pl.BlockSpec((rows, depth), lambda i: (i, 0)),
            pl.BlockSpec(weight.shape, lambda i: (0, 0)),
            pl.BlockSpec((rows, LANES), lambda i: (i, 0)),
            pl.BlockSpec((rows, LANES), lambda i: (i, 0)),
        ],
        out_specs=pl.BlockSpec((3 * pairs, rows, LANES), lambda i: (0, i, 0)),
        out_shape=jax.ShapeDtypeStruct((3 * pairs, length, LANES), BF),
        compiler_params=pltpu.CompilerParams(vmem_limit_bytes=40 * MIB),
        name="project",
    )(normed_all, weight, cosine, sine)


def attend_kernel(
    own_ref, low_ref, high_ref, q_ref, k_ref, v_ref, qmark_ref, kmark_ref, ctx_ref, lse_ref, keys, vals,
    *, bq, bk, per_part,
):
    step = pl.program_id(0)
    length = kmark_ref.shape[0]
    own = own_ref[0]

    @pl.when(step == 0)
    def _():
        lane = lax.broadcasted_iota(jnp.int32, (512, LANES), 1)

        @pl.loop(0, length // 512)
        def _(i):
            rows = pl.ds(pl.multiple_of(i * 512, 512), 512)
            keys[rows, :LANES] = k_ref[0, rows, :]
            keys[rows, LANES:] = kmark_ref[rows, :]
            v = v_ref[0, rows, :]
            one = jnp.ones_like(v)
            vals[0, rows, :] = jnp.where(lane < 64, v, one)
            vals[1, rows, :] = jnp.where(lane < 64, one, v)

    first = lax.broadcasted_iota(jnp.int32, (bq, LANES), 1) < 64
    q = q_ref[0]
    mark = qmark_ref[...]
    zero = jnp.zeros_like(q)
    queries = (
        jnp.concatenate([jnp.where(first, q, zero), mark], axis=1),
        jnp.concatenate([jnp.where(first, zero, q), mark], axis=1),
    )

    def body(j, carry):
        rows = pl.ds(pl.multiple_of(stored_block(j, own, per_part // bk) * bk, bk), bk)
        block = keys[rows, :]
        new = []
        for head in range(2):
            peak, total = carry[head]
            scores = lax.dot_general(queries[head], block, NT, preferred_element_type=F32)
            higher = jnp.maximum(peak, jnp.max(scores, axis=1, keepdims=True))
            weights = jnp.exp2(scores - higher).astype(BF)
            total = total * jnp.exp2(peak - higher) + jnp.dot(
                weights, vals[head, rows, :], preferred_element_type=F32
            )
            new.append((higher, total))
        return tuple(new)

    init = (jnp.full((bq, 1), -3e38, F32), jnp.zeros((bq, LANES), F32))
    (peak_a, sum_a), (peak_b, sum_b) = lax.fori_loop(low_ref[step], high_ref[step], body, (init, init))
    weight_sum = pltpu.roll(jnp.where(first, sum_b, sum_a), 64, 1)
    ctx_ref[0] = (jnp.where(first, sum_a, sum_b) / weight_sum).astype(BF)
    lse_ref[...] = jnp.where(first, peak_a, peak_b) + jnp.log2(weight_sum)


def attend(qkv, pair, qmark, kmark, own, low, high, bq, bk, per_part):
    length = qmark.shape[0]
    row = lambda i, *_: (i, 0)
    whole = lambda i, *_: (0, 0)
    return pl.pallas_call(
        functools.partial(attend_kernel, bq=bq, bk=bk, per_part=per_part),
        grid_spec=pltpu.PrefetchScalarGridSpec(
            num_scalar_prefetch=3,
            grid=(length // bq,),
            in_specs=[
                pl.BlockSpec((1, bq, LANES), lambda i, *_: (3 * pair, i, 0)),
                pl.BlockSpec((1, length, LANES), lambda i, *_: (3 * pair + 1, 0, 0)),
                pl.BlockSpec((1, length, LANES), lambda i, *_: (3 * pair + 2, 0, 0)),
                pl.BlockSpec((bq, LANES), row),
                pl.BlockSpec((length, LANES), whole),
            ],
            out_specs=[
                pl.BlockSpec((1, bq, LANES), lambda i, *_: (i // (per_part // bq), i % (per_part // bq), 0)),
                pl.BlockSpec((bq, LANES), row),
            ],
            scratch_shapes=[pltpu.VMEM((length, 2 * LANES), BF), pltpu.VMEM((2, length, LANES), BF)],
        ),
        out_shape=[
            jax.ShapeDtypeStruct((length // per_part, per_part, LANES), BF),
            jax.ShapeDtypeStruct((length, LANES), F32),
        ],
        compiler_params=pltpu.CompilerParams(
            dimension_semantics=("arbitrary",), vmem_limit_bytes=48 * MIB
        ),
        cost_estimate=pl.CostEstimate(
            flops=int(0.9 * 4 * length * length * LANES), bytes_accessed=8 * length * LANES, transcendentals=length * length
        ),
        name="attend",
    )(own, low, high, qkv, qkv, qkv, qmark, kmark)


def three_parts(value):
    high = value.astype(BF).astype(F32)
    rest = value - high
    middle = rest.astype(BF).astype(F32)
    return high, middle, (rest - middle).astype(BF).astype(F32)


def attend_back_kernel(
    own_ref, low_ref, high_ref, q_ref, k_ref, v_ref, do_ref, ctx_ref, lse_ref, qmark_ref, kmark_ref, cos_ref,
    sin_ref, out_ref, keys, vals, key_heads, query_heads, grad_heads, dq_sum,
    *, bq, bk, utt, per_part,
):
    length = kmark_ref.shape[0]
    own = own_ref[0]
    pb = 512
    lane = lax.broadcasted_iota(jnp.int32, (pb, LANES), 1)
    first = lane < 64

    @pl.loop(0, length // pb)
    def _(i):
        rows = pl.ds(pl.multiple_of(i * pb, pb), pb)
        at, within = i // (per_part // pb), pl.ds(pl.multiple_of(i % (per_part // pb) * pb, pb), pb)
        k = k_ref[0, rows, :]
        zero = jnp.zeros_like(k)
        mark = kmark_ref[rows, :]
        keys[rows, :LANES] = k
        keys[rows, LANES:] = mark
        vals[rows, :LANES] = v_ref[0, rows, :]
        vals[rows, LANES:] = mark
        q = q_ref[0, rows, :]
        grad = do_ref[at, within, :]
        qmark = qmark_ref[rows, :].astype(F32)
        lse = lse_ref[rows, :]
        product = grad.astype(F32) * ctx_ref[at, within, :].astype(F32)
        for head in range(2):
            mine = first if head == 0 else jnp.logical_not(first)
            key_heads[head, rows, :] = jnp.where(mine, k, zero)
            query_heads[head, rows, :LANES] = jnp.where(mine, q, zero)
            grad_heads[head, rows, :LANES] = jnp.where(mine, grad, zero)
            high, middle, low = three_parts(-lse[:, 64 * head : 64 * head + 1])
            query_heads[head, rows, LANES:] = jnp.where(
                lane == utt, high, jnp.where(lane == utt + 1, middle, jnp.where(lane == utt + 2, low, qmark))
            ).astype(BF)
            delta = jnp.sum(jnp.where(mine, product, 0.0), axis=1, keepdims=True)
            high, middle, low = three_parts(-delta)
            grad_heads[head, rows, LANES:] = jnp.where(
                lane == utt, high, jnp.where(lane == utt + 1, middle, jnp.where(lane == utt + 2, low, 0.0))
            ).astype(BF)
        dq_sum[rows, :] = jnp.zeros((pb, LANES), F32)

    @pl.loop(0, length // bk)
    def _(j):
        key_rows = pl.ds(pl.multiple_of(j * bk, bk), bk)
        key_block = keys[key_rows, :]
        value_block = vals[key_rows, :]

        def body(i, carry):
            dk, dv = carry
            rows = pl.ds(pl.multiple_of(stored_block(i, own, per_part // bq) * bq, bq), bq)
            dq = dq_sum[rows, :]
            for head in range(2):
                query = query_heads[head, rows, :]
                grad = grad_heads[head, rows, :]
                probs = jnp.exp2(lax.dot_general(key_block, query, NT, preferred_element_type=F32))
                pulled = lax.dot_general(value_block, grad, NT, preferred_element_type=F32)
                grad_scores = (probs * pulled).astype(BF)
                dv = dv + jnp.dot(probs.astype(BF), grad[:, :LANES], preferred_element_type=F32)
                dk = dk + jnp.dot(grad_scores, query[:, :LANES], preferred_element_type=F32)
                dq = dq + lax.dot_general(
                    grad_scores, key_heads[head, key_rows, :], TN, preferred_element_type=F32
                )
            dq_sum[rows, :] = dq
            return dk, dv

        zero = jnp.zeros((bk, LANES), F32)
        dk, dv = lax.fori_loop(low_ref[j], high_ref[j], body, (zero, zero))
        at, within = j // (per_part // bk), pl.ds(pl.multiple_of(j % (per_part // bk) * bk, bk), bk)
        out_ref[at, 2, within, :] = dv.astype(BF)
        dk = dk * (1.0 / LOG2E)
        out_ref[at, 1, within, :] = (dk * cos_ref[key_rows, :] - swap_halves(dk) * sin_ref[key_rows, :]).astype(BF)

    @pl.loop(0, length // pb)
    def _(i):
        rows = pl.ds(pl.multiple_of(i * pb, pb), pb)
        at, within = i // (per_part // pb), pl.ds(pl.multiple_of(i % (per_part // pb) * pb, pb), pb)
        dq = dq_sum[rows, :] * HEAD_DIM**-0.5
        out_ref[at, 0, within, :] = (dq * cos_ref[rows, :] - swap_halves(dq) * sin_ref[rows, :]).astype(BF)


def attend_back(
    qkv, pair, grad, ctx, lse, qmark, kmark, cosine, sine, own, low, high, bq, bk, utt, per_part
):
    length = qmark.shape[0]
    in_smem = pl.BlockSpec(memory_space=pltpu.SMEM)
    whole = pl.BlockSpec((length, LANES), lambda i: (0, 0))
    parts = length // per_part
    by_part = pl.BlockSpec((parts, per_part, LANES), lambda i: (0, 0, 0))
    cut = lambda kind: pl.BlockSpec((1, length, LANES), lambda i: (3 * pair + kind, 0, 0))
    wide = pltpu.VMEM((length, 2 * LANES), BF)
    return pl.pallas_call(
        functools.partial(attend_back_kernel, bq=bq, bk=bk, utt=utt, per_part=per_part),
        grid=(1,),
        in_specs=[in_smem] * 3 + [cut(0), cut(1), cut(2)] + [by_part] * 2 + [whole] * 5,
        out_specs=pl.BlockSpec((parts, 3, per_part, LANES), lambda i: (0, 0, 0, 0)),
        out_shape=jax.ShapeDtypeStruct((parts, 3, per_part, LANES), BF),
        scratch_shapes=[
            wide,
            wide,
            pltpu.VMEM((2, length, LANES), BF),
            pltpu.VMEM((2, length, 2 * LANES), BF),
            pltpu.VMEM((2, length, 2 * LANES), BF),
            pltpu.VMEM((length, LANES), F32),
        ],
        compiler_params=pltpu.CompilerParams(vmem_limit_bytes=56 * MIB),
        cost_estimate=pl.CostEstimate(
            flops=int(0.9 * 10 * length * length * LANES), bytes_accessed=30 * length * LANES, transcendentals=length * length
        ),
        name="attend_back",
    )(own, low, high, qkv, qkv, qkv, grad, ctx, lse, qmark, kmark, cosine, sine)


def frame_marks(lengths, places, utt):
    ends = jnp.cumsum(lengths)
    starts = ends - lengths
    segment = jnp.sum((places[:, None] >= ends[None, :]).astype(jnp.int32), axis=1, dtype=jnp.int32)
    member = segment[:, None] == jnp.arange(utt, dtype=jnp.int32)[None, :]
    offsets = jnp.sum(jnp.where(member, starts[None, :], 0), axis=1, dtype=jnp.int32)
    return segment, member, offsets


def block_ranges(lengths, blocks, size, other):
    ends = jnp.cumsum(lengths)
    starts = ends - lengths
    at_first = blocks * size
    at_last = at_first + (size - 1)
    index = jnp.arange(lengths.shape[0], dtype=jnp.int32)
    seg_first = jnp.sum((at_first[:, None] >= ends[None]).astype(jnp.int32), axis=1)
    seg_last = jnp.sum((at_last[:, None] >= ends[None]).astype(jnp.int32), axis=1)
    low = jnp.sum(jnp.where(index[None] == seg_first[:, None], starts[None], 0), axis=1)
    high = jnp.sum(jnp.where(index[None] == seg_last[:, None], ends[None], 0), axis=1)
    return (low // other).astype(jnp.int32), ((high + other - 1) // other).astype(jnp.int32)


def feed_kernel(
    x_own_ref, x_other_ref, cot_own_ref, cot_other_ref, up_ref, down_ref,
    out_own_ref, out_other_ref, gin_own_ref, gin_other_ref, gup_ref, gdown_ref, out_sum, gin_sum,
):
    step = pl.program_id(0)
    last = pl.num_programs(0) - 1
    up = up_ref[...]
    down = down_ref[...]
    root = math.sqrt(2.0 / math.pi)
    gup = gdown = None
    for side, (x_ref, cot_ref) in enumerate(((x_own_ref, cot_own_ref), (x_other_ref, cot_other_ref))):
        x = x_ref[...]
        cot = cot_ref[...]
        before = lax.dot_general(x, up, NT, preferred_element_type=F32)
        grad_act = lax.dot_general(cot, down, NT, preferred_element_type=F32)
        square = before * before
        bend = jnp.tanh(root * before * (1.0 + 0.044715 * square))
        half = 0.5 * (1.0 + bend)
        activated = (before * half).astype(BF)
        slope = half + 0.5 * before * (1.0 - bend * bend) * (root + (3.0 * 0.044715 * root) * square)
        grad_before = (grad_act * slope).astype(BF)
        out = jnp.dot(activated, down, preferred_element_type=F32)
        gin = jnp.dot(grad_before, up, preferred_element_type=F32)
        gd = lax.dot_general(activated, cot, TN, preferred_element_type=F32)
        gu = lax.dot_general(grad_before, x, TN, preferred_element_type=F32)
        gup = gu if side == 0 else gup + gu
        gdown = gd if side == 0 else gdown + gd

        @pl.when(step == 0)
        def _():
            out_sum[side] = out
            gin_sum[side] = gin

        @pl.when(step > 0)
        def _():
            out_sum[side] += out
            gin_sum[side] += gin

    gup_ref[...] = gup.astype(BF)
    gdown_ref[...] = gdown.astype(BF)

    @pl.when(step == last)
    def _():
        out_own_ref[...] = out_sum[0]
        out_other_ref[...] = out_sum[1].astype(BF)
        gin_own_ref[...] = gin_sum[0]
        gin_other_ref[...] = gin_sum[1].astype(BF)


def feed(x_own, x_other, cot_own, cot_other, up, down):
    frames, depth = x_own.shape
    units = up.shape[0]
    chunk = 256
    whole = pl.BlockSpec((frames, depth), lambda j: (0, 0))
    cut = pl.BlockSpec((chunk, depth), lambda j: (j, 0))
    shape = lambda *s: jax.ShapeDtypeStruct(*s)
    return pl.pallas_call(
        feed_kernel,
        grid=(units // chunk,),
        in_specs=[whole] * 4 + [cut] * 2,
        out_specs=[whole] * 4 + [cut] * 2,
        out_shape=[
            shape((frames, depth), F32),
            shape((frames, depth), BF),
            shape((frames, depth), F32),
            shape((frames, depth), BF),
            shape((units, depth), BF),
            shape((units, depth), BF),
        ],
        scratch_shapes=[pltpu.VMEM((2, frames, depth), F32), pltpu.VMEM((2, frames, depth), F32)],
        compiler_params=pltpu.CompilerParams(
            dimension_semantics=("arbitrary",), vmem_limit_bytes=60 * MIB
        ),
        cost_estimate=pl.CostEstimate(
            flops=24 * frames * depth * units, bytes_accessed=40 * frames * depth, transcendentals=2 * frames * units
        ),
        name="feed",
    )(x_own, x_other, cot_own, cot_other, up, down)


SUM_WIDTH = 256


def sum_kernel(x_ref, out_ref, held, first_in, half_in, sems, *, rows_all, parts):
    d = lax.axis_index("dp")
    z = lax.axis_index("tensor")
    total = x_ref.shape[0]
    half = total // 2
    core = d % 2
    dp_bits = [1 << k for k in range(1, rows_all.bit_length() - 1)]
    z_bits = [1 << k for k in reversed(range(parts.bit_length() - 1))]
    steps = [
        [("dp", bit) for bit in dp_bits] + [("tensor", bit) for bit in z_bits],
        [("dp", bit) for bit in reversed(dp_bits)] + [("tensor", bit) for bit in z_bits],
    ]

    def device(axis, bit):
        return (d ^ bit, z) if axis == "dp" else (d, z ^ bit)

    barrier = pltpu.get_barrier_semaphore()
    everyone = [("dp", 1)] + steps[0]
    for axis, bit in everyone:
        pl.semaphore_signal(barrier, inc=1, device_id=device(axis, bit), device_id_type=pl.DeviceIdType.MESH)
    pl.semaphore_wait(barrier, len(everyone))

    def rows(start, size):
        return pl.ds(pl.multiple_of(start, 16), size)

    def send(source, target, at, axis, bit):
        copy = pltpu.make_async_remote_copy(
            src_ref=source,
            dst_ref=target,
            send_sem=sems.at[2 * at],
            recv_sem=sems.at[2 * at + 1],
            device_id=device(axis, bit),
            device_id_type=pl.DeviceIdType.MESH,
        )
        copy.start()
        return copy

    def add_into(target, start, one, one_at, two, size):
        step = min(size, 128)

        @pl.loop(0, size // step)
        def _(i):
            a = one[rows(one_at + i * step, step), :].astype(F32)
            b = two[pl.ds(pl.multiple_of(i * step, step), step), :].astype(F32)
            target[rows(start + i * step, step), :] = (a + b).astype(BF)

    at = 0
    copy = send(x_ref.at[rows((1 - core) * half, half), :], first_in, at, "dp", 1)
    copy.wait()
    add_into(held, 0, x_ref, core * half, first_in, half)
    at += 1

    quarter = half // 2
    starts = [0, quarter]
    size = quarter
    begin = [0, quarter]
    kept = []
    for step in range(len(steps[0])):
        size //= 2
        copies = []
        for side in range(2):
            axis, bit = steps[side][step]
            upper = ((d if axis == "dp" else z) // bit) % 2
            keep = starts[side] + upper * size
            away = starts[side] + (1 - upper) * size
            target = half_in.at[pl.ds(begin[side], size), :]
            copies.append(send(held.at[rows(away, size), :], target, at, axis, bit))
            starts[side] = keep
            at += 1
        for side in range(2):
            copies[side].wait()
            add_into(held, starts[side], held, starts[side], half_in.at[pl.ds(begin[side], size), :], size)
            begin[side] += size
        kept.append((list(starts), size))

    def settle(start, n):
        out_ref[rows(core * half + start, n), :] = held[rows(start, n), :]

    for side in range(2):
        settle(starts[side], size)
    for step in reversed(range(len(steps[0]))):
        copies = []
        for side in range(2):
            axis, bit = steps[side][step]
            mine = out_ref.at[rows(core * half + starts[side], size), :]
            copies.append(send(mine, mine, at, axis, bit))
            at += 1
        for side in range(2):
            copies[side].wait()
        starts = kept[step - 1][0] if step > 0 else [0, quarter]
        size *= 2
    mine = out_ref.at[rows(core * half, half), :]
    send(mine, mine, at, "dp", 1).wait()


def sum_everywhere(value, rows_all, parts):
    total, width = value.shape
    stages = rows_all.bit_length() + parts.bit_length() - 3
    whole = pl.BlockSpec(memory_space=pltpu.VMEM)
    return pl.pallas_call(
        functools.partial(sum_kernel, rows_all=rows_all, parts=parts),
        in_specs=[whole],
        out_specs=whole,
        out_shape=jax.ShapeDtypeStruct(value.shape, BF),
        scratch_shapes=[
            pltpu.VMEM((total // 2, width), BF),
            pltpu.VMEM((total // 2, width), BF),
            pltpu.VMEM((total // 2, width), BF),
            pltpu.SemaphoreType.DMA((2 * (2 + 4 * stages),)),
        ],
        compiler_params=pltpu.CompilerParams(
            collective_id=0, has_side_effects=True, vmem_limit_bytes=32 * MIB
        ),
        name="sum_everywhere",
    )(value)


def norm_parts(hidden):
    center = hidden - jnp.mean(hidden, axis=-1, keepdims=True)
    inverse = lax.rsqrt(jnp.mean(center * center, axis=-1, keepdims=True) + norm_epsilon)
    return center * inverse, inverse


def norm_pull(unit, inverse, grad, scale):
    pulled = grad * (1.0 + scale)
    return (
        pulled
        - jnp.mean(pulled, axis=-1, keepdims=True)
        - unit * jnp.mean(pulled * unit, axis=-1, keepdims=True)
    ) * inverse


def dot(a, b, dims=(((1,), (0,)), ((), ()))):
    return lax.dot_general(a, b, dims, preferred_element_type=F32)


def exact(pattern, a, b):
    return jnp.einsum(pattern, a, b, precision=lax.Precision.HIGHEST)


def on_device(
    inputs, skip_input, lengths, time_steps, w_skip_in, w_skip_res, w_ada, w_qkv, w_out, w_up, w_down, cotangent
):
    parts = lax.axis_size("tensor")
    rows_all = lax.axis_size("dp")
    half = parts // 2
    columns = rows_all // 2
    d = lax.axis_index("dp")
    z = lax.axis_index("tensor")
    core, column = d % 2, d // 2
    stays = z // half == core
    part = core * half + z % half
    inputs, skip_input, cotangent = inputs[0], skip_input[0], cotangent[0]
    frames, depth = inputs.shape
    length = frames * parts
    heads_here = w_out.shape[0] // HEAD_DIM
    pairs = heads_here * HEAD_DIM // LANES
    utt = lengths.shape[1]
    both = ("dp", "tensor")

    def relocate(value):
        pattern = [
            (i * parts + j, ((i // 2) * 2 + j // half) * parts + (i % 2) * half + j % half)
            for i in range(rows_all)
            for j in range(parts)
            if i % 2 != j // half
        ]
        return jnp.where(stays, value, lax.ppermute(value, both, pattern))

    def partner(value, b):
        pattern = [
            (i * parts + j, (i ^ (b // half)) * parts + (j // half) * half + ((j % half) ^ (b % half)))
            for i in range(rows_all)
            for j in range(parts)
        ]
        return lax.ppermute(value, both, pattern)

    def exchange(blocks):
        return [blocks[0]] + [partner(blocks[b], b) for b in range(1, parts)]

    same_core = [[2 * i + k for i in range(columns)] for k in range(2)]

    ws = w_qkv.shape[2]
    qkv_rows = jnp.transpose(w_qkv, (0, 2, 1)).reshape(3 * ws, depth)
    per_q, per_o = 3 * ws // rows_all, ws // rows_all
    slice_head = jnp.concatenate(
        [
            lax.dynamic_slice_in_dim(qkv_rows, d * per_q, per_q, 0),
            lax.dynamic_slice_in_dim(w_out, d * per_o, per_o, 0),
        ]
    )
    head_rows = lax.all_gather(lax.all_gather(slice_head, "tensor"), "dp")
    head_rows = jnp.transpose(head_rows, (1, 0, 2, 3))
    order = part ^ jnp.arange(parts, dtype=jnp.int32)
    head_rows = jnp.take(head_rows, order, axis=0)
    w_heads = head_rows[:, :, :per_q].reshape(parts, 3 * ws, depth)
    w_out_all = head_rows[:, :, per_q:].reshape(parts, ws, depth)

    units = w_down.shape[0]
    per_u = units // rows_all
    at = core * (units // 2) + column * per_u
    slice_feed = jnp.stack(
        [
            jnp.transpose(lax.dynamic_slice_in_dim(w_up, at, per_u, 1)),
            lax.dynamic_slice_in_dim(w_down, at, per_u, 0),
        ]
    )
    feed_rows = lax.all_gather(lax.all_gather(slice_feed, "tensor", axis=1), "dp", axis=1, axis_index_groups=same_core)
    feed_rows = feed_rows.reshape(2, columns * parts * per_u, depth)

    other_lengths = partner(lengths, half)
    other_steps = partner(time_steps, half)
    lengths_work = jnp.where(stays, lengths, other_lengths)[0]
    steps_work = jnp.where(stays, time_steps, other_steps)[0]

    time_rate = jnp.exp(
        -math.log(10000.0) * (jnp.arange(w_ada.shape[0] // 2, dtype=F32) / (w_ada.shape[0] // 2))
    )

    def embed(steps):
        phases = steps.astype(F32)[:, None] * time_rate
        return jax.nn.silu(jnp.concatenate([jnp.sin(phases), jnp.cos(phases)], axis=-1)).astype(BF)

    def modulation(silu_low, member, at, wide):
        per_utterance = dot(silu_low, w_ada[:, at : at + wide])
        return exact("lu,um->lm", member.astype(F32), per_utterance)

    spot = jnp.arange(frames, dtype=jnp.int32)
    _, member_home, _ = frame_marks(lengths[0], z * frames + spot, utt)
    shift_one, scale_one = jnp.split(modulation(embed(time_steps[0]), member_home, 0, 2 * depth), 2, axis=-1)
    base_home = dot(inputs, w_skip_in) + dot(skip_input, w_skip_res)
    unit_home, _ = norm_parts(base_home)
    normed = relocate((unit_home * (1.0 + scale_one) + shift_one).astype(BF))
    base = relocate(base_home.astype(BF))
    cot = relocate(cotangent)

    silu_low = embed(steps_work)
    _, member, _ = frame_marks(lengths_work, part * frames + spot, utt)
    mods = jnp.split(modulation(silu_low, member, 0, 4 * depth), 4, axis=-1)
    across = [normed] + [partner(normed, b) for b in range(1, half)]
    blocks = across + [partner(value, half) for value in across]
    normed_all = jnp.concatenate(blocks)

    index = jnp.arange(length, dtype=jnp.int32)
    places = (part ^ (index // frames)) * frames + index % frames
    segment, _, offsets = frame_marks(lengths_work, places, utt)
    rotary_rate = jnp.exp(-math.log(10000.0) * (2.0 * jnp.arange(HEAD_DIM // 2, dtype=F32) / HEAD_DIM))
    angles = (places - offsets).astype(F32)[:, None] * rotary_rate
    cosine = jnp.tile(jnp.cos(angles), (1, 4))
    sine_half = jnp.sin(angles)
    sine = jnp.tile(jnp.concatenate([-sine_half, sine_half], axis=1), (1, 2))
    lane = jnp.arange(LANES, dtype=jnp.int32)[None, :]
    same = segment[:, None] == lane
    qmark = jnp.where((lane < utt) & jnp.logical_not(same), MASKED, 0.0).astype(BF)
    kmark = (same | ((lane >= utt) & (lane < utt + 3))).astype(BF)

    qkv = project(normed_all, w_heads[0], cosine, sine, pairs)

    def ranges(size, other):
        per = frames // size
        stored = jnp.arange(length // size, dtype=jnp.int32)
        natural = (part ^ (stored // per)) * per + stored % per
        return block_ranges(lengths_work, natural, size, other)

    own = part.astype(jnp.int32)[None]
    bq, bk = 512, 512
    low, high = ranges(bq, bk)
    low_back, high_back = ranges(bk, bq)
    ctx_pairs, lse_pairs, ctx_mine = [], [], []
    for pair in range(pairs):
        ctx, lse = attend(qkv, pair, qmark, kmark, own, low, high, bq, bk, frames)
        ctx_pairs.append(ctx)
        lse_pairs.append(lse)
        ctx_mine.append(exchange([ctx[b] for b in range(parts)]))
    context = jnp.concatenate(
        [ctx_mine[pair][b] for b in range(parts) for pair in range(pairs)], axis=1
    )
    w_out_work = w_out_all.reshape(parts * ws, depth)
    hidden = base.astype(F32) + dot(context, w_out_work)
    unit_two, inverse_two = norm_parts(hidden)
    ffn_in = (unit_two * (1.0 + mods[3]) + mods[2]).astype(BF)

    ffn_other = partner(ffn_in, half)
    cot_other = partner(cot, half)
    out_own, out_send, gin_own, gin_send, gup, gdown = feed(
        ffn_in, ffn_other, cot, cot_other, feed_rows[0], feed_rows[1]
    )
    grad_ffn_in = gin_own + partner(gin_send, half).astype(F32)
    block_out = hidden + out_own + partner(out_send, half).astype(F32)
    block_out = relocate(block_out.astype(BF)).astype(F32)

    grad_hidden = cot.astype(F32) + norm_pull(unit_two, inverse_two, grad_ffn_in, mods[3])
    grad_hidden_low = grad_hidden.astype(BF)
    grad_context = dot(grad_hidden_low, w_out_work, NT).astype(BF)
    grad_out = dot(context, grad_hidden_low, TN).astype(BF)
    member_wide = member.astype(F32)
    sums_two = exact("lu,lm->um", member_wide, jnp.concatenate([grad_ffn_in, grad_ffn_in * unit_two], axis=1))

    grad_out = jnp.take(grad_out.reshape(parts, 2, ws // 2, depth), order, axis=0)
    mine = lax.dynamic_slice_in_dim(grad_out, core, 1, 1)[:, 0]
    theirs = lax.dynamic_slice_in_dim(grad_out, 1 - core, 1, 1)[:, 0]
    grad_out = (mine.astype(F32) + partner(theirs, half).astype(F32)).astype(BF)

    grad_out = jnp.transpose(grad_out.reshape(parts, columns, per_o, depth), (1, 0, 2, 3))
    grad_feed = jnp.concatenate(
        [gup.reshape(columns, parts, per_u, depth), gdown.reshape(columns, parts, per_u, depth), grad_out], axis=2
    )
    grad_feed = lax.psum_scatter(grad_feed, "dp", scatter_dimension=0, axis_index_groups=same_core)
    grad_feed = lax.psum_scatter(grad_feed, "tensor", scatter_dimension=0)
    grad_feed = lax.all_gather(grad_feed, "dp", axis=0)
    grad_feed = jnp.transpose(grad_feed.reshape(columns, 2, 2 * per_u + per_o, depth), (1, 0, 2, 3)).astype(F32)
    grad_up = jnp.transpose(grad_feed[:, :, :per_u].reshape(units, depth))
    grad_down = grad_feed[:, :, per_u : 2 * per_u].reshape(units, depth)
    grad_out = grad_feed[:, :, 2 * per_u :].reshape(ws, depth)

    grad_mine = []
    for pair in range(pairs):
        cut = [
            grad_context[:, b * ws + pair * LANES : b * ws + (pair + 1) * LANES] for b in range(parts)
        ]
        grad = jnp.stack(exchange(cut))
        grads = attend_back(
            qkv, pair, grad, ctx_pairs[pair], lse_pairs[pair], qmark, kmark, cosine, sine, own,
            low_back, high_back, bq, bk, utt, frames,
        )
        grad_mine.append(grads)
    grad_heads = jnp.concatenate(
        [grad_mine[pair][:, kind].reshape(length, LANES) for kind in range(3) for pair in range(pairs)], axis=1
    )
    grad_qkv = relocate(dot(normed_all, grad_heads, TN).astype(BF))
    grad_qkv = lax.psum(grad_qkv, "dp").astype(F32).reshape(depth, 3, ws)
    grad_qkv = jnp.transpose(grad_qkv, (1, 0, 2))

    returned = [exchange([grads[b] for b in range(parts)]) for grads in grad_mine]
    grad_rows = jnp.concatenate(
        [returned[pair][b][kind] for b in range(parts) for kind in range(3) for pair in range(pairs)], axis=1
    )
    grad_normed = dot(grad_rows, w_heads.reshape(parts * 3 * ws, depth))
    unit_one, inverse_one = norm_parts(base.astype(F32))
    grad_base = (grad_hidden + norm_pull(unit_one, inverse_one, grad_normed, mods[1])).astype(BF)
    sums_one = exact("lu,lm->um", member_wide, jnp.concatenate([grad_normed, grad_normed * unit_one], axis=1))

    inputs_work = relocate(inputs)
    skips_work = relocate(skip_input)
    grad_skip = jnp.concatenate(
        [
            dot(frames_in, grad_base, TN).astype(BF)[:, k * SUM_WIDTH : (k + 1) * SUM_WIDTH]
            for frames_in in (inputs_work, skips_work)
            for k in range(depth // SUM_WIDTH)
        ]
    )
    grad_skip = sum_everywhere(grad_skip, rows_all, parts).reshape(2, depth // SUM_WIDTH, depth, SUM_WIDTH)
    grad_skip = jnp.transpose(grad_skip, (0, 2, 1, 3)).reshape(2, depth, depth).astype(F32)

    grad_base_home = relocate(grad_base)
    grad_inputs = dot(grad_base_home, w_skip_in, NT)
    grad_skips = dot(grad_base_home, w_skip_res, NT)

    steps_all = lax.all_gather(time_steps[0], "dp")
    silu_all = embed(steps_all.reshape(-1)).astype(F32)
    row_work = column * 2 + z // half
    sums = jnp.concatenate([sums_one, sums_two], axis=1)
    slots = jnp.arange(rows_all, dtype=jnp.int32)[:, None, None] == row_work
    sums_all = lax.psum(jnp.where(slots, sums[None], 0.0), both).reshape(rows_all * utt, 4 * depth)
    grad_ada = exact("ut,um->tm", silu_all, sums_all)

    return (
        block_out[None],
        grad_inputs[None],
        grad_skips[None],
        grad_skip[0],
        grad_skip[1],
        grad_ada,
        grad_qkv,
        grad_out,
        grad_up,
        grad_down,
    )


def solution(mesh):
    placed = (
        P("dp", "tensor", None),
        P("dp", "tensor", None),
        P("dp", None),
        P("dp", None),
        P(),
        P(),
        P(),
        P(None, None, "tensor"),
        P("tensor", None),
        P(None, "tensor"),
        P("tensor", None),
        P("dp", "tensor", None),
    )
    return jax.shard_map(
        on_device,
        mesh=mesh,
        in_specs=placed,
        out_specs=(
            P("dp", "tensor", None),
            P("dp", "tensor", None),
            P("dp", "tensor", None),
            P(),
            P(),
            P(),
            P(None, None, "tensor"),
            P("tensor", None),
            P(None, "tensor"),
            P("tensor", None),
        ),
        check_vma=False,
    )
```

```python
import functools
import math

import jax
import jax.numpy as jnp
from jax import lax
from jax.experimental import pallas as pl
from jax.experimental.pallas import tpu as pltpu
from jax.sharding import PartitionSpec as P

HEAD_DIM = 64
LANES = 128
MASKED = -1e30
LOG2E = math.log2(math.e)
MIB = 2**20
BF = jnp.bfloat16
F32 = jnp.float32
norm_epsilon = 1e-06
NT = (((1,), (1,)), ((), ()))
TN = (((0,), (0,)), ((), ()))


def cost(microseconds):
    return pl.CostEstimate(flops=int(microseconds * 1.1e9), bytes_accessed=0, transcendentals=0)


def stored_block(block, own, per_part):
    shift = per_part.bit_length() - 1
    part = lax.shift_right_logical(block, shift)
    return ((part ^ own) << shift) | (block & (per_part - 1))


def swap_halves(values):
    lane = lax.broadcasted_iota(jnp.int32, values.shape, 1)
    return jnp.where(lane % 64 < 32, pltpu.roll(values, 96, 1), pltpu.roll(values, 32, 1))


def mesh_spot(parts):
    d = lax.axis_index("dp")
    z = lax.axis_index("tensor")
    return d, z, d % 2, parts // 2


def partner_of(d, z, b, half):
    return d ^ (b // half), z ^ (b % half)


def remote_copy(source, target, sems, at, device):
    return pltpu.make_async_remote_copy(
        src_ref=source,
        dst_ref=target,
        send_sem=sems.at[2 * at],
        recv_sem=sems.at[2 * at + 1],
        device_id=device,
        device_id_type=pl.DeviceIdType.MESH,
    )


PIECES = 4


def in_pieces(source, target, sems, at, device, pieces=range(PIECES)):
    rows = source.shape[0] // PIECES
    return [
        remote_copy(
            source.at[k * rows : (k + 1) * rows, :], target.at[k * rows : (k + 1) * rows, :], sems, at + k, device
        )
        for k in pieces
    ]


def remote(source, target, sems, at, device):
    copy = remote_copy(source, target, sems, at, device)
    copy.start()
    return copy


def greet(devices):
    barrier = pltpu.get_barrier_semaphore()
    for device in devices:
        pl.semaphore_signal(barrier, inc=1, device_id=device, device_id_type=pl.DeviceIdType.MESH)
    pl.semaphore_wait(barrier, len(devices))


def project_kernel(normed_ref, weight_ref, cos_ref, sin_ref, out_ref, *, pairs):
    normed = normed_ref[...]
    cosine = cos_ref[...]
    sine = sin_ref[...]
    width = pairs * LANES
    for kind in range(3):
        weight = weight_ref[kind * width : (kind + 1) * width, :]
        part = lax.dot_general(normed, weight, NT, preferred_element_type=F32)
        for pair in range(pairs):
            cut = part[:, pair * LANES : (pair + 1) * LANES]
            if kind < 2:
                cut = cut * cosine + swap_halves(cut) * sine
            if kind == 0:
                cut = cut * (LOG2E * HEAD_DIM**-0.5)
            out_ref[pair * 3 + kind] = cut.astype(BF)


def project(normed_all, weight, cosine, sine, pairs):
    length, depth = normed_all.shape
    rows = 512
    return pl.pallas_call(
        functools.partial(project_kernel, pairs=pairs),
        grid=(length // rows,),
        in_specs=[
            pl.BlockSpec((rows, depth), lambda i: (i, 0)),
            pl.BlockSpec(weight.shape, lambda i: (0, 0)),
            pl.BlockSpec((rows, LANES), lambda i: (i, 0)),
            pl.BlockSpec((rows, LANES), lambda i: (i, 0)),
        ],
        out_specs=pl.BlockSpec((3 * pairs, rows, LANES), lambda i: (0, i, 0)),
        out_shape=jax.ShapeDtypeStruct((3 * pairs, length, LANES), BF),
        compiler_params=pltpu.CompilerParams(vmem_limit_bytes=40 * MIB),
        cost_estimate=cost(11),
        name="project",
    )(normed_all, weight, cosine, sine)


def attend_kernel(
    own_ref, low_ref, high_ref, q_ref, k_ref, v_ref, qmark_ref, kmark_ref, ctx_ref, lse_ref, keys, vals,
    *, bq, bk, per_part,
):
    step = pl.program_id(0)
    length = kmark_ref.shape[0]
    own = own_ref[0]

    @pl.when(step == 0)
    def _():
        lane = lax.broadcasted_iota(jnp.int32, (512, LANES), 1)

        @pl.loop(0, length // 512)
        def _(i):
            rows = pl.ds(pl.multiple_of(i * 512, 512), 512)
            keys[rows, :LANES] = k_ref[0, rows, :]
            keys[rows, LANES:] = kmark_ref[rows, :]
            v = v_ref[0, rows, :]
            one = jnp.ones_like(v)
            vals[0, rows, :] = jnp.where(lane < 64, v, one)
            vals[1, rows, :] = jnp.where(lane < 64, one, v)

    first = lax.broadcasted_iota(jnp.int32, (bq, LANES), 1) < 64
    q = q_ref[0]
    mark = qmark_ref[...]
    zero = jnp.zeros_like(q)
    queries = (
        jnp.concatenate([jnp.where(first, q, zero), mark], axis=1),
        jnp.concatenate([jnp.where(first, zero, q), mark], axis=1),
    )

    def body(j, carry):
        rows = pl.ds(pl.multiple_of(stored_block(j, own, per_part // bk) * bk, bk), bk)
        block = keys[rows, :]
        new = []
        for head in range(2):
            peak, total = carry[head]
            scores = lax.dot_general(queries[head], block, NT, preferred_element_type=F32)
            higher = jnp.maximum(peak, jnp.max(scores, axis=1, keepdims=True))
            weights = jnp.exp2(scores - higher).astype(BF)
            total = total * jnp.exp2(peak - higher) + jnp.dot(
                weights, vals[head, rows, :], preferred_element_type=F32
            )
            new.append((higher, total))
        return tuple(new)

    init = (jnp.full((bq, 1), -3e38, F32), jnp.zeros((bq, LANES), F32))
    (peak_a, sum_a), (peak_b, sum_b) = lax.fori_loop(low_ref[step], high_ref[step], body, (init, init))
    weight_sum = pltpu.roll(jnp.where(first, sum_b, sum_a), 64, 1)
    ctx_ref[0] = (jnp.where(first, sum_a, sum_b) / weight_sum).astype(BF)
    lse_ref[...] = jnp.where(first, peak_a, peak_b) + jnp.log2(weight_sum)


def attend(qkv, pair, qmark, kmark, own, low, high, bq, bk, per_part):
    length = qmark.shape[0]
    row = lambda i, *_: (i, 0)
    whole = lambda i, *_: (0, 0)
    return pl.pallas_call(
        functools.partial(attend_kernel, bq=bq, bk=bk, per_part=per_part),
        grid_spec=pltpu.PrefetchScalarGridSpec(
            num_scalar_prefetch=3,
            grid=(length // bq,),
            in_specs=[
                pl.BlockSpec((1, bq, LANES), lambda i, *_: (3 * pair, i, 0)),
                pl.BlockSpec((1, length, LANES), lambda i, *_: (3 * pair + 1, 0, 0)),
                pl.BlockSpec((1, length, LANES), lambda i, *_: (3 * pair + 2, 0, 0)),
                pl.BlockSpec((bq, LANES), row),
                pl.BlockSpec((length, LANES), whole),
            ],
            out_specs=[
                pl.BlockSpec((1, bq, LANES), lambda i, *_: (i // (per_part // bq), i % (per_part // bq), 0)),
                pl.BlockSpec((bq, LANES), row),
            ],
            scratch_shapes=[pltpu.VMEM((length, 2 * LANES), BF), pltpu.VMEM((2, length, LANES), BF)],
        ),
        out_shape=[
            jax.ShapeDtypeStruct((length // per_part, per_part, LANES), BF),
            jax.ShapeDtypeStruct((length, LANES), F32),
        ],
        compiler_params=pltpu.CompilerParams(
            dimension_semantics=("arbitrary",), vmem_limit_bytes=48 * MIB
        ),
        cost_estimate=cost(37),
        name="attend",
    )(own, low, high, qkv, qkv, qkv, qmark, kmark)


def three_parts(value):
    high = value.astype(BF).astype(F32)
    rest = value - high
    middle = rest.astype(BF).astype(F32)
    return high, middle, (rest - middle).astype(BF).astype(F32)


def attend_back_kernel(
    own_ref, low_ref, high_ref, q_ref, k_ref, v_ref, do_ref, ctx_ref, lse_ref, qmark_ref, kmark_ref, cos_ref,
    sin_ref, out_ref, keys, vals, key_heads, query_heads, grad_heads, dq_sum,
    *, bq, bk, utt, per_part,
):
    length = kmark_ref.shape[0]
    own = own_ref[0]
    pb = 512
    lane = lax.broadcasted_iota(jnp.int32, (pb, LANES), 1)
    first = lane < 64

    @pl.loop(0, length // pb)
    def _(i):
        rows = pl.ds(pl.multiple_of(i * pb, pb), pb)
        at, within = i // (per_part // pb), pl.ds(pl.multiple_of(i % (per_part // pb) * pb, pb), pb)
        k = k_ref[0, rows, :]
        zero = jnp.zeros_like(k)
        mark = kmark_ref[rows, :]
        keys[rows, :LANES] = k
        keys[rows, LANES:] = mark
        vals[rows, :LANES] = v_ref[0, rows, :]
        vals[rows, LANES:] = mark
        q = q_ref[0, rows, :]
        grad = do_ref[at, within, :]
        qmark = qmark_ref[rows, :].astype(F32)
        lse = lse_ref[rows, :]
        product = grad.astype(F32) * ctx_ref[at, within, :].astype(F32)
        for head in range(2):
            mine = first if head == 0 else jnp.logical_not(first)
            key_heads[head, rows, :] = jnp.where(mine, k, zero)
            query_heads[head, rows, :LANES] = jnp.where(mine, q, zero)
            grad_heads[head, rows, :LANES] = jnp.where(mine, grad, zero)
            high, middle, low = three_parts(-lse[:, 64 * head : 64 * head + 1])
            query_heads[head, rows, LANES:] = jnp.where(
                lane == utt, high, jnp.where(lane == utt + 1, middle, jnp.where(lane == utt + 2, low, qmark))
            ).astype(BF)
            delta = jnp.sum(jnp.where(mine, product, 0.0), axis=1, keepdims=True)
            high, middle, low = three_parts(-delta)
            grad_heads[head, rows, LANES:] = jnp.where(
                lane == utt, high, jnp.where(lane == utt + 1, middle, jnp.where(lane == utt + 2, low, 0.0))
            ).astype(BF)
        dq_sum[rows, :] = jnp.zeros((pb, LANES), F32)

    @pl.loop(0, length // bk)
    def _(j):
        key_rows = pl.ds(pl.multiple_of(j * bk, bk), bk)
        key_block = keys[key_rows, :]
        value_block = vals[key_rows, :]

        def body(i, carry):
            dk, dv = carry
            rows = pl.ds(pl.multiple_of(stored_block(i, own, per_part // bq) * bq, bq), bq)
            dq = dq_sum[rows, :]
            for head in range(2):
                query = query_heads[head, rows, :]
                grad = grad_heads[head, rows, :]
                probs = jnp.exp2(lax.dot_general(key_block, query, NT, preferred_element_type=F32))
                pulled = lax.dot_general(value_block, grad, NT, preferred_element_type=F32)
                grad_scores = (probs * pulled).astype(BF)
                dv = dv + jnp.dot(probs.astype(BF), grad[:, :LANES], preferred_element_type=F32)
                dk = dk + jnp.dot(grad_scores, query[:, :LANES], preferred_element_type=F32)
                dq = dq + lax.dot_general(
                    grad_scores, key_heads[head, key_rows, :], TN, preferred_element_type=F32
                )
            dq_sum[rows, :] = dq
            return dk, dv

        zero = jnp.zeros((bk, LANES), F32)
        dk, dv = lax.fori_loop(low_ref[j], high_ref[j], body, (zero, zero))
        at, within = j // (per_part // bk), pl.ds(pl.multiple_of(j % (per_part // bk) * bk, bk), bk)
        out_ref[at, 2, within, :] = dv.astype(BF)
        dk = dk * (1.0 / LOG2E)
        out_ref[at, 1, within, :] = (dk * cos_ref[key_rows, :] - swap_halves(dk) * sin_ref[key_rows, :]).astype(BF)

    @pl.loop(0, length // pb)
    def _(i):
        rows = pl.ds(pl.multiple_of(i * pb, pb), pb)
        at, within = i // (per_part // pb), pl.ds(pl.multiple_of(i % (per_part // pb) * pb, pb), pb)
        dq = dq_sum[rows, :] * HEAD_DIM**-0.5
        out_ref[at, 0, within, :] = (dq * cos_ref[rows, :] - swap_halves(dq) * sin_ref[rows, :]).astype(BF)


def attend_back(
    qkv, pair, grad, ctx, lse, qmark, kmark, cosine, sine, own, low, high, bq, bk, utt, per_part
):
    length = qmark.shape[0]
    in_smem = pl.BlockSpec(memory_space=pltpu.SMEM)
    whole = pl.BlockSpec((length, LANES), lambda i: (0, 0))
    parts = length // per_part
    by_part = pl.BlockSpec((parts, per_part, LANES), lambda i: (0, 0, 0))
    cut = lambda kind: pl.BlockSpec((1, length, LANES), lambda i: (3 * pair + kind, 0, 0))
    wide = pltpu.VMEM((length, 2 * LANES), BF)
    return pl.pallas_call(
        functools.partial(attend_back_kernel, bq=bq, bk=bk, utt=utt, per_part=per_part),
        grid=(1,),
        in_specs=[in_smem] * 3 + [cut(0), cut(1), cut(2)] + [by_part] * 2 + [whole] * 5,
        out_specs=pl.BlockSpec((parts, 3, per_part, LANES), lambda i: (0, 0, 0, 0)),
        out_shape=jax.ShapeDtypeStruct((parts, 3, per_part, LANES), BF),
        scratch_shapes=[
            wide,
            wide,
            pltpu.VMEM((2, length, LANES), BF),
            pltpu.VMEM((2, length, 2 * LANES), BF),
            pltpu.VMEM((2, length, 2 * LANES), BF),
            pltpu.VMEM((length, LANES), F32),
        ],
        compiler_params=pltpu.CompilerParams(vmem_limit_bytes=56 * MIB),
        cost_estimate=cost(66),
        name="attend_back",
    )(own, low, high, qkv, qkv, qkv, grad, ctx, lse, qmark, kmark, cosine, sine)


def frame_marks(lengths, places, utt):
    ends = jnp.cumsum(lengths)
    starts = ends - lengths
    segment = jnp.sum((places[:, None] >= ends[None, :]).astype(jnp.int32), axis=1, dtype=jnp.int32)
    member = segment[:, None] == jnp.arange(utt, dtype=jnp.int32)[None, :]
    offsets = jnp.sum(jnp.where(member, starts[None, :], 0), axis=1, dtype=jnp.int32)
    return segment, member, offsets


def block_ranges(lengths, blocks, size, other):
    ends = jnp.cumsum(lengths)
    starts = ends - lengths
    at_first = blocks * size
    at_last = at_first + (size - 1)
    index = jnp.arange(lengths.shape[0], dtype=jnp.int32)
    seg_first = jnp.sum((at_first[:, None] >= ends[None]).astype(jnp.int32), axis=1)
    seg_last = jnp.sum((at_last[:, None] >= ends[None]).astype(jnp.int32), axis=1)
    low = jnp.sum(jnp.where(index[None] == seg_first[:, None], starts[None], 0), axis=1)
    high = jnp.sum(jnp.where(index[None] == seg_last[:, None], ends[None], 0), axis=1)
    return (low // other).astype(jnp.int32), ((high + other - 1) // other).astype(jnp.int32)


def feed_kernel(
    x_own_ref, cot_own_ref, cot_other_ref, weights_ref, inputs_hbm, heads_hbm,
    out_own_ref, out_other_ref, gin_own_ref, gin_other_ref, grads_ref, inputs_in_hbm, heads_out_hbm,
    x_other_ref, out_sum, gin_sum, local, sems, *, parts,
):
    step = pl.program_id(0)
    last = pl.num_programs(0) - 1
    d, z, core, half = mesh_spot(parts)
    leaves = z // half != core
    there = ((d - core) + z // half, core * half + z % half)
    beside = partner_of(d, z, half, half)

    def copies():
        return in_pieces(inputs_hbm, inputs_in_hbm, sems, 1, there)

    eighth = d // 2 % 4 + 4 * core

    def heads_part(k):
        if k < parts:
            cut = heads_out_hbm.at[eighth, z]
            return remote_copy(cut, cut, sems, PIECES + k, (d, z ^ k))
        size = 1 << (k - parts)
        cut = heads_out_hbm.at[pl.ds(eighth // size * size, size)]
        return remote_copy(cut, cut, sems, PIECES + k, (d ^ (2, 4)[k - parts], z))

    @pl.when(step == 0)
    def _():
        barrier = pltpu.get_barrier_semaphore()
        near = [(d ^ bit, z) for bit in (1, 2, 4)] + [(d, z ^ k) for k in range(1, parts)]
        for device in near:
            pl.semaphore_signal(barrier, inc=1, device_id=device, device_id_type=pl.DeviceIdType.MESH)

        @pl.when(leaves)
        def _():
            pl.semaphore_signal(barrier, inc=1, device_id=there, device_id_type=pl.DeviceIdType.MESH)
            pl.semaphore_wait(barrier, len(near) + 1)

        @pl.when(jnp.logical_not(leaves))
        def _():
            pl.semaphore_wait(barrier, len(near))

        remote_copy(x_own_ref, x_other_ref, sems, 0, beside).start()
        copy = pltpu.make_async_copy(heads_hbm.at[:, eighth], heads_out_hbm.at[eighth, z], local)
        copy.start()
        copy.wait()
        for k in range(1, parts):
            heads_part(k).start()

    @pl.when(step == 1)
    def _():
        @pl.when(leaves)
        def _():
            for copy in copies():
                copy.start()

    @pl.when(step == 2)
    def _():
        for k in range(1, parts):
            heads_part(k).wait()
        heads_part(parts).start()

    @pl.when(step == 4)
    def _():
        heads_part(parts).wait()
        heads_part(parts + 1).start()

    chunk, depth = weights_ref.shape[0] * weights_ref.shape[2], weights_ref.shape[3]
    up = weights_ref[:, 0].reshape(chunk, depth)
    down = weights_ref[:, 1].reshape(chunk, depth)
    root = math.sqrt(2.0 / math.pi)
    gup = gdown = None
    for side, (x_ref, cot_ref) in enumerate(((x_own_ref, cot_own_ref), (x_other_ref, cot_other_ref))):
        if side == 1:

            @pl.when(step == 0)
            def _():
                remote_copy(x_own_ref, x_other_ref, sems, 0, beside).wait()

        x = x_ref[...]
        cot = cot_ref[...]
        before = lax.dot_general(x, up, NT, preferred_element_type=F32)
        grad_act = lax.dot_general(cot, down, NT, preferred_element_type=F32)
        square = before * before
        bend = jnp.tanh(root * before * (1.0 + 0.044715 * square))
        half = 0.5 * (1.0 + bend)
        activated = (before * half).astype(BF)
        slope = half + 0.5 * before * (1.0 - bend * bend) * (root + (3.0 * 0.044715 * root) * square)
        grad_before = (grad_act * slope).astype(BF)
        out = jnp.dot(activated, down, preferred_element_type=F32)
        gin = jnp.dot(grad_before, up, preferred_element_type=F32)
        gd = lax.dot_general(activated, cot, TN, preferred_element_type=F32)
        gu = lax.dot_general(grad_before, x, TN, preferred_element_type=F32)
        gup = gu if side == 0 else gup + gu
        gdown = gd if side == 0 else gdown + gd

        @pl.when(step == 0)
        def _():
            out_sum[side] = out
            gin_sum[side] = gin

        @pl.when(step > 0)
        def _():
            out_sum[side] += out
            gin_sum[side] += gin

    per = weights_ref.shape[2]
    grads_ref[:, :per] = gup.astype(BF).reshape(-1, per, depth)
    grads_ref[:, per : 2 * per] = gdown.astype(BF).reshape(-1, per, depth)
    grads_ref[:, 2 * per :] = jnp.zeros(grads_ref[:, 2 * per :].shape, BF)

    @pl.when(step == last)
    def _():
        out_own_ref[...] = out_sum[0]
        out_other_ref[...] = out_sum[1].astype(BF)
        gin_own_ref[...] = gin_sum[0]
        gin_other_ref[...] = gin_sum[1].astype(BF)

        heads_part(parts + 1).wait()

        @pl.when(leaves)
        def _():
            for copy in copies():
                copy.wait()


def feed(x_own, cot_own, cot_other, weights, inputs, heads, spare, parts):
    frames, depth = x_own.shape
    groups, _, per, _ = weights.shape
    chunk = 256
    whole = pl.BlockSpec((frames, depth), lambda j: (0, 0))
    cut = pl.BlockSpec((chunk // per, 2, per, depth), lambda j: (j, 0, 0, 0))
    grads = pl.BlockSpec((chunk // per, 2 * per + spare, depth), lambda j: (j, 0, 0))
    shape = lambda *s: jax.ShapeDtypeStruct(*s)
    anywhere = pl.BlockSpec(memory_space=pl.ANY)
    return pl.pallas_call(
        functools.partial(feed_kernel, parts=parts),
        grid=(groups * per // chunk,),
        in_specs=[whole] * 3 + [cut] + [anywhere] * 2,
        out_specs=[whole] * 4 + [grads] + [anywhere] * 2,
        out_shape=[
            shape((frames, depth), F32),
            shape((frames, depth), BF),
            shape((frames, depth), F32),
            shape((frames, depth), BF),
            shape((groups, 2 * per + spare, depth), BF),
            shape((frames, depth), BF),
            shape((8, parts) + heads.shape[:1] + heads.shape[2:], BF),
        ],
        scratch_shapes=[
            pltpu.VMEM((frames, depth), BF),
            pltpu.VMEM((2, frames, depth), F32),
            pltpu.VMEM((2, frames, depth), F32),
            pltpu.SemaphoreType.DMA,
            pltpu.SemaphoreType.DMA((2 * (PIECES + parts + 3),)),
        ],
        compiler_params=pltpu.CompilerParams(
            dimension_semantics=("arbitrary",), vmem_limit_bytes=60 * MIB, collective_id=3, has_side_effects=True
        ),
        cost_estimate=cost(84),
        name="feed",
    )(x_own, cot_own, cot_other, weights, inputs, heads)


def spread(segment, table):
    masks = [segment == u for u in range(1, table.shape[0])]
    columns = []
    for k in range(table.shape[1] // LANES):
        cut = table[:, k * LANES : (k + 1) * LANES]
        out = jnp.broadcast_to(cut[0:1], segment.shape)
        for u, mask in enumerate(masks):
            out = jnp.where(mask, cut[u + 1 : u + 2], out)
        columns.append(out)
    return jnp.concatenate(columns, axis=1)


def collect(segment, values, utt):
    rows = []
    for u in range(utt):
        mask = segment == u
        rows.append(
            jnp.concatenate(
                [
                    jnp.sum(jnp.where(mask, values[:, k * LANES : (k + 1) * LANES], 0.0), axis=0, keepdims=True)
                    for k in range(values.shape[1] // LANES)
                ],
                axis=1,
            )
        )
    return jnp.concatenate(rows, axis=0)


def unit_norm(hidden):
    center = hidden - jnp.mean(hidden, axis=-1, keepdims=True)
    inverse = lax.rsqrt(jnp.mean(center * center, axis=-1, keepdims=True) + norm_epsilon)
    return center * inverse, inverse


def pull_norm(unit, inverse, grad, gain):
    pulled = grad * gain
    return (
        pulled
        - jnp.mean(pulled, axis=-1, keepdims=True)
        - unit * jnp.mean(pulled * unit, axis=-1, keepdims=True)
    ) * inverse


def join_kernel(own_ref, *refs, pairs, parts):
    ctx_refs = refs[: pairs * parts]
    w_out_ref, base_ref, base_in_ref, segment_ref, shift_ref, scale_ref, hidden_ref, normed_ref = refs[pairs * parts :]
    own = own_ref[0]
    hidden = jnp.where(own_ref[1] == 1, base_ref[...], base_in_ref[...]).astype(F32)
    for b in range(parts):
        context = jnp.concatenate([ctx_refs[pair * parts + b][...] for pair in range(pairs)], axis=1)
        hidden = hidden + jnp.dot(context, w_out_ref[:, own ^ b].reshape(pairs * LANES, -1), preferred_element_type=F32)
    hidden_ref[...] = hidden
    unit, _ = unit_norm(hidden)
    segment = segment_ref[...]
    normed_ref[...] = (unit * (1.0 + spread(segment, scale_ref[...])) + spread(segment, shift_ref[...])).astype(BF)


def join(own, ctx_blocks, w_out, base, base_in, segment, shift, scale, pairs, parts):
    frames, depth = base.shape
    rows = 256
    row = lambda i, *_: (i, 0)
    wide = pl.BlockSpec((rows, depth), row)
    table = pl.BlockSpec(shift.shape, lambda i, *_: (0, 0))
    return pl.pallas_call(
        functools.partial(join_kernel, pairs=pairs, parts=parts),
        grid_spec=pltpu.PrefetchScalarGridSpec(
            num_scalar_prefetch=1,
            grid=(frames // rows,),
            in_specs=[pl.BlockSpec((rows, LANES), row)] * (pairs * parts)
            + [pl.BlockSpec(w_out.shape, lambda i, *_: (0, 0, 0, 0)), wide, wide, pl.BlockSpec((rows, LANES), row)]
            + [table] * 2,
            out_specs=[wide, wide],
        ),
        out_shape=[jax.ShapeDtypeStruct((frames, depth), F32), jax.ShapeDtypeStruct((frames, depth), BF)],
        compiler_params=pltpu.CompilerParams(vmem_limit_bytes=40 * MIB),
        cost_estimate=cost(8),
        name="join",
    )(own, *ctx_blocks, w_out, base, base_in, segment, shift, scale)


def turn_kernel(
    own_ref, gin_own_ref, gin_in_ref, out_own_ref, out_in_ref, hidden_ref, cot_ref, skips_ref, segment_ref, scale_ref,
    w_out_ref, grad_hidden_ref, low_ref, block_out_ref, sums_ref, *grad_context_refs, pairs, parts, utt,
):
    own = own_ref[0]
    hidden = hidden_ref[...]
    unit, inverse = unit_norm(hidden)
    segment = segment_ref[...]
    block_out_ref[0] = (hidden + out_own_ref[...] + out_in_ref[...].astype(F32)).astype(BF)
    block_out_ref[1] = skips_ref[...]
    grad = gin_own_ref[...] + gin_in_ref[...].astype(F32)
    grad_hidden = cot_ref[...].astype(F32) + pull_norm(unit, inverse, grad, 1.0 + spread(segment, scale_ref[...]))
    grad_hidden_ref[...] = grad_hidden
    low = grad_hidden.astype(BF)
    low_ref[...] = low
    for b in range(parts):
        part = lax.dot_general(low, w_out_ref[:, own ^ b].reshape(pairs * LANES, -1), NT, preferred_element_type=F32).astype(BF)
        for pair in range(pairs):
            grad_context_refs[pair * parts + b][...] = part[:, pair * LANES : (pair + 1) * LANES]
    sums = jnp.concatenate([collect(segment, grad, utt), collect(segment, grad * unit, utt)], axis=0)

    @pl.when(pl.program_id(0) == 0)
    def _():
        sums_ref[...] = sums

    @pl.when(pl.program_id(0) > 0)
    def _():
        sums_ref[...] += sums


def turn(own, gin_own, gin_in, out_own, out_in, hidden, cot, skips, segment, scale, w_out, pairs, parts):
    frames, depth = hidden.shape
    utt = scale.shape[0]
    rows = 256
    row = lambda i, *_: (i, 0)
    wide = pl.BlockSpec((rows, depth), row)
    thin = pl.BlockSpec((rows, LANES), row)
    shape = lambda *s: jax.ShapeDtypeStruct(*s)
    return pl.pallas_call(
        functools.partial(turn_kernel, pairs=pairs, parts=parts, utt=utt),
        grid_spec=pltpu.PrefetchScalarGridSpec(
            num_scalar_prefetch=1,
            grid=(frames // rows,),
            in_specs=[wide] * 7
            + [thin, pl.BlockSpec(scale.shape, lambda i, *_: (0, 0)), pl.BlockSpec(w_out.shape, lambda i, *_: (0, 0, 0, 0))],
            out_specs=[wide] * 2
            + [pl.BlockSpec((2, rows, depth), lambda i, *_: (0, i, 0)), pl.BlockSpec((2 * utt, depth), lambda i, *_: (0, 0))]
            + [thin] * (pairs * parts),
        ),
        out_shape=[
            shape((frames, depth), F32),
            shape((frames, depth), BF),
            shape((2, frames, depth), BF),
            shape((2 * utt, depth), F32),
        ]
        + [shape((frames, LANES), BF)] * (pairs * parts),
        compiler_params=pltpu.CompilerParams(
            dimension_semantics=("arbitrary",), vmem_limit_bytes=48 * MIB
        ),
        cost_estimate=cost(15),
        name="turn",
    )(own, gin_own, gin_in, out_own, out_in, hidden, cot, skips, segment, scale, w_out)


def out_grad_kernel(*refs, pairs, parts, columns, at_row):
    low_ref, ctx_refs, (_, out_hbm, held, landing, local, sems) = refs[0], refs[1:-6], refs[-6:]
    d, z, core, half = mesh_spot(parts)
    part = core * half + z % half
    beside = partner_of(d, z, half, half)
    per = pairs * LANES // (2 * columns)
    greet([beside])
    if per < held.shape[3]:
        held[...] = jnp.zeros_like(held)
    low = low_ref[...]
    for b in range(parts):
        for pair in range(pairs):
            grad = lax.dot_general(ctx_refs[pair * parts + b][...], low, TN, preferred_element_type=F32)
            for k in range(LANES // per):
                spot = pair * (LANES // per) + k
                held[spot % 2, spot // 2, part ^ b, :per, :] = grad[k * per : (k + 1) * per].astype(BF)
    remote(held.at[1 - core], landing, sems, 0, beside).wait()

    @pl.loop(0, columns)
    def _(i):
        held[core, i] = (held[core, i].astype(F32) + landing[i].astype(F32)).astype(BF)

    copies = []
    for i in range(columns):
        copy = pltpu.make_async_copy(
            held.at[core, i], out_hbm.at[i * parts : (i + 1) * parts, at_row:, :], local.at[i]
        )
        copy.start()
        copies.append(copy)
    for copy in copies:
        copy.wait()


def out_grad(low, ctx_blocks, grad_feed, at_row, pairs, parts, columns):
    depth = low.shape[1]
    spare = grad_feed.shape[1] - at_row
    vmem = pl.BlockSpec(memory_space=pltpu.VMEM)
    anywhere = pl.BlockSpec(memory_space=pl.ANY)
    return pl.pallas_call(
        functools.partial(out_grad_kernel, pairs=pairs, parts=parts, columns=columns, at_row=at_row),
        in_specs=[vmem] * (1 + pairs * parts) + [anywhere],
        out_specs=anywhere,
        out_shape=jax.ShapeDtypeStruct(grad_feed.shape, BF),
        scratch_shapes=[
            pltpu.VMEM((2, columns, parts, spare, depth), BF),
            pltpu.VMEM((columns, parts, spare, depth), BF),
            pltpu.SemaphoreType.DMA((columns,)),
            pltpu.SemaphoreType.DMA((2,)),
        ],
        input_output_aliases={1 + pairs * parts: 0},
        compiler_params=pltpu.CompilerParams(
            collective_id=4, has_side_effects=True, vmem_limit_bytes=32 * MIB
        ),
        cost_estimate=cost(9),
        name="out_grad",
    )(low, *ctx_blocks, grad_feed)


class Sender:
    def __init__(self, sems, used=0):
        self.sems, self.used = sems, used
        self.d, self.z = lax.axis_index("dp"), lax.axis_index("tensor")

    def device(self, axis, bit):
        return (self.d ^ bit, self.z) if axis == "dp" else (self.d, self.z ^ bit)

    def side(self, axis, bit):
        return ((self.d if axis == "dp" else self.z) // bit) % 2

    def take(self, count):
        self.used += count
        return self.used - count

    def send(self, source, target, axis, bit):
        return remote(source, target, self.sems, self.take(1), self.device(axis, bit))


def rows_at(start, size):
    return pl.ds(pl.multiple_of(start, 16), size)


def few_rows(size):
    while size > 128:
        size //= 2
    return size


def add_rows(target, start, landing, landing_at, size):
    step = few_rows(size)

    @pl.loop(0, size // step)
    def _(i):
        here = rows_at(start + i * step, step)
        there = landing[rows_at(landing_at + i * step, step), :].astype(F32)
        target[here, :] = (target[here, :].astype(F32) + there).astype(target.dtype)


def sum_tree(sender, buffer, landing, down, turn_round, up, out, offset):
    size = buffer.shape[0] // 2
    starts, begin, kept = [0, size], [0, size], []
    for step in range(len(down[0])):
        kept.append(list(starts))
        size //= 2
        copies = []
        for side in range(2):
            axis, bit = down[side][step]
            upper = sender.side(axis, bit)
            lose = starts[side] + (1 - upper) * size
            copies.append(
                sender.send(buffer.at[rows_at(lose, size), :], landing.at[rows_at(begin[side], size), :], axis, bit)
            )
            starts[side] = starts[side] + upper * size
        yield
        for side in range(2):
            copies[side].wait()
            add_rows(buffer, starts[side], landing, begin[side], size)
            begin[side] += size
    yield from turn_round(starts, size)
    for step in reversed(range(len(down[0]))):
        copies = []
        for side in range(2):
            mine = out.at[rows_at(offset + starts[side], size), :]
            copies.append(sender.send(mine, mine, *up[side][step]))
        yield
        for side in range(2):
            copies[side].wait()
        starts = kept[step]
        size *= 2


def spread_sums(sender, own, held, out, parts):
    half = parts // 2
    slot = (sender.d // 2) * 2 + sender.z // half
    held[0] = own
    group = [("dp", 1)] + [("tensor", 1 << k) for k in range(parts.bit_length() - 2)]
    for at, (axis, bit) in enumerate(group):
        copy = sender.send(held.at[2 * at], held.at[2 * at + 1], axis, bit)
        yield
        copy.wait()
        held[2 * at + 2] = held[2 * at] + held[2 * at + 1]
    out[pl.ds(slot, 1)] = held[pl.ds(2 * len(group), 1)]
    size = 1
    rows_all = out.shape[0]
    for axis, bit in [("tensor", half)] + [("dp", 1 << k) for k in range(1, rows_all.bit_length() - 1)]:
        mine = out.at[pl.ds(slot // size * size, size)]
        copy = sender.send(mine, mine, axis, bit)
        yield
        copy.wait()
        size *= 2


def run_all(running):
    for work in list(running):
        try:
            next(work)
        except StopIteration:
            running.remove(work)


def bits_of(rows_all, parts):
    dp_bits = [1 << k for k in range(1, rows_all.bit_length() - 1)]
    return dp_bits, [1 << k for k in reversed(range(parts.bit_length() - 1))]


def finish_kernel(*refs, pairs, parts, utt, rows_all):
    cut = (pairs - 1) * parts
    prev_hbm, refs = refs[:cut], refs[cut:]
    own_hbm, refs = refs[:pairs], refs[pairs:]
    (
        normed_hbm, weight_hbm, base_hbm, base_in_hbm, grad_hbm, segment_ref, scale_ref,
        grad_base_ref, qkv_ref, sums_ref,
        prev, own, normed, weight, base, grad_hidden, arrived, total, qkv_held, qkv_in, loads, sems,
    ) = refs
    d, z, core, half = mesh_spot(parts)
    part = core * half + z % half
    stays = z // half == core
    frames = normed.shape[1]
    width = pairs * LANES

    there = ((d - core) + z // half, core * half + z % half)
    dp_bits, _ = bits_of(rows_all, parts)
    near = [partner_of(d, z, b, half) for b in range(1, parts)] + [(d, z ^ half)] + [(d ^ bit, z) for bit in dp_bits]
    barrier = pltpu.get_barrier_semaphore()
    for device in near:
        pl.semaphore_signal(barrier, inc=1, device_id=device, device_id_type=pl.DeviceIdType.MESH)

    @pl.when(jnp.logical_not(stays))
    def _():
        pl.semaphore_signal(barrier, inc=1, device_id=there, device_id_type=pl.DeviceIdType.MESH)
        pl.semaphore_wait(barrier, len(near) + 1)

    @pl.when(stays)
    def _():
        pl.semaphore_wait(barrier, len(near))

    sends = []
    order = [b for b in range(1, parts) if b % half] + [b for b in range(1, parts) if b % half == 0]
    for b in order:
        sends.append(
            (b, remote(own_hbm[-1].at[b], arrived.at[b - 1], sems, b - 1, partner_of(d, z, b, half)))
        )

    def load(at, source, target):
        copy = pltpu.make_async_copy(source, target, loads.at[at])
        copy.start()
        return copy

    first = [load(0, normed_hbm, normed)]
    for pair in range(pairs):
        first.append(load(1 + pair, own_hbm[pair], own.at[pair]))
    at = 1 + pairs
    four = pl.ds(core * 4, 4)
    second = [
        load(at, weight_hbm.at[four], weight.at[four]),
        remote(weight_hbm.at[four], weight.at[four], sems, parts - 1, (d ^ 1, z)),
    ]
    for k in range(cut):
        second.append(load(at + 1 + k, prev_hbm[k], prev.at[k]))
    at += 1 + cut
    third = [load(at, grad_hbm, grad_hidden)]

    @pl.when(stays)
    def _():
        pltpu.make_async_copy(base_hbm, base, loads.at[at + 1]).start()

    @pl.when(jnp.logical_not(stays))
    def _():
        pltpu.make_async_copy(base_in_hbm, base, loads.at[at + 1]).start()

    for copy in first:
        copy.wait()
    for kind in range(3):
        for pair in range(pairs):

            def gather(b, carry):
                return carry + lax.dot_general(own[pair, b, kind], normed[b], TN, preferred_element_type=F32)

            grad = lax.fori_loop(0, parts, gather, jnp.zeros((LANES, normed.shape[2]), F32)).astype(BF)
            wide = qkv_held.shape[1]
            for k in range(normed.shape[2] // wide):
                at_row = k * 3 * width + kind * width + pair * LANES
                qkv_held[at_row : at_row + LANES, :] = grad[:, k * wide : (k + 1) * wide]

    sender = Sender(sems, parts)
    down = [
        [("dp", bit) for bit in dp_bits] + [("tensor", half)],
        [("dp", bit) for bit in reversed(dp_bits)] + [("tensor", half)],
    ]

    def go_home(starts, size):
        at_sem = sender.take(2)

        def copies():
            return [
                remote_copy(
                    qkv_held.at[rows_at(starts[side], size), :],
                    qkv_ref.at[rows_at(starts[side], size), :],
                    sems,
                    at_sem + side,
                    there,
                )
                for side in range(2)
            ]

        @pl.when(stays)
        def _():
            for side in range(2):
                here = rows_at(starts[side], size)
                qkv_ref[here, :] = qkv_held[here, :]

        @pl.when(jnp.logical_not(stays))
        def _():
            for copy in copies():
                copy.start()

        yield

        @pl.when(jnp.logical_not(stays))
        def _():
            for copy in copies():
                copy.wait()

        for side in range(2):
            starts[side] = starts[side] + (core - z // half) * size

    up = [line[:-1] + [("dp", 1)] for line in down]
    running = [sum_tree(sender, qkv_held, qkv_in, down, go_home, up, qkv_ref, 0)]
    run_all(running)

    for copy in second:
        copy.wait()
    rows = 256

    def add_block(source, b, pair, fresh):
        weights = jnp.concatenate(
            [weight[:, part ^ b, kind * pairs + pair].reshape(LANES, -1) for kind in range(3)],
            axis=0,
        )

        @pl.loop(0, frames // rows)
        def _(i):
            here = pl.ds(pl.multiple_of(i * rows, rows), rows)
            block = jnp.concatenate([source[kind, here, :] for kind in range(3)], axis=1)
            term = jnp.dot(block, weights, preferred_element_type=F32)
            if fresh:
                total[here, :] = term
            else:
                total[here, :] += term

    add_block(own.at[pairs - 1, 0], 0, pairs - 1, True)
    run_all(running)
    for pair in range(pairs - 1):
        for b in range(parts):
            add_block(prev.at[pair * parts + b], b, pair, False)
            if b % 2:
                run_all(running)
    for b, copy in sorted(sends, key=lambda item: (item[0] % half, item[0])):
        copy.wait()
        add_block(arrived.at[b - 1], b, pairs - 1, False)
        run_all(running)

    for copy in third:
        copy.wait()
    pltpu.make_async_copy(base_hbm, base, loads.at[at + 1]).wait()
    sums_ref[...] = jnp.zeros_like(sums_ref)

    @pl.loop(0, frames // rows)
    def _(i):
        here = pl.ds(pl.multiple_of(i * rows, rows), rows)
        unit, inverse = unit_norm(base[here, :].astype(F32))
        grad = total[here, :]
        segment = segment_ref[here, :]
        pulled = pull_norm(unit, inverse, grad, 1.0 + spread(segment, scale_ref[...]))
        grad_base_ref[here, :] = (grad_hidden[here, :] + pulled).astype(BF)
        sums_ref[...] += jnp.concatenate([collect(segment, grad, utt), collect(segment, grad * unit, utt)], axis=0)

    while running:
        run_all(running)


def finish(
    prev, own, normed_all, weight, base, base_in, grad_hidden, segment, scale, pairs, parts, rows_all
):
    frames, depth = base.shape
    utt = scale.shape[0]
    units = 3 * pairs * LANES
    wide = depth
    while units * depth // wide % (16 * rows_all * 2):
        wide //= 2
    qkv_shape = (units * depth // wide, wide)
    copies = parts + 2 + 5 * rows_all.bit_length() + parts.bit_length()
    anywhere = pl.BlockSpec(memory_space=pl.ANY)
    vmem = pl.BlockSpec(memory_space=pltpu.VMEM)
    shape = lambda *s: jax.ShapeDtypeStruct(*s)
    block = (3, frames, LANES)
    return pl.pallas_call(
        functools.partial(finish_kernel, pairs=pairs, parts=parts, utt=utt, rows_all=rows_all),
        in_specs=[anywhere] * (len(prev) + pairs + 5) + [vmem] * 2,
        out_specs=[vmem] * 3,
        out_shape=[
            shape((frames, depth), BF),
            shape(qkv_shape, BF),
            shape((2 * utt, depth), F32),
        ],
        scratch_shapes=[
            pltpu.VMEM((max(len(prev), 1),) + block, BF),
            pltpu.VMEM((pairs, parts) + block, BF),
            pltpu.VMEM(normed_all.shape, BF),
            pltpu.VMEM(weight.shape, BF),
            pltpu.VMEM((frames, depth), BF),
            pltpu.VMEM((frames, depth), F32),
            pltpu.VMEM((parts - 1,) + block, BF),
            pltpu.VMEM((frames, depth), F32),
            pltpu.VMEM(qkv_shape, BF),
            pltpu.VMEM(qkv_shape, BF),
            pltpu.SemaphoreType.DMA((4 + pairs + len(prev),)),
            pltpu.SemaphoreType.DMA((2 * copies,)),
        ],
        compiler_params=pltpu.CompilerParams(
            collective_id=1, has_side_effects=True, vmem_limit_bytes=56 * MIB
        ),
        cost_estimate=cost(60),
        name="finish",
    )(*prev, *own, normed_all, weight, base, base_in, grad_hidden, segment, scale)


def sums_kernel(
    inputs_hbm, inputs_in_hbm, skips_hbm, skips_in_hbm, grad_ref, sums_ref, skip_out_ref, sums_out_ref, grad_in_hbm,
    frames_in, away, held, first_in, half_in, sums_in, loads, sems, *, rows_all, parts,
):
    d, z, core, half = mesh_spot(parts)
    stays = z // half == core
    leaves = jnp.logical_not(stays)
    dp_bits, z_bits = bits_of(rows_all, parts)
    there = ((d - core) + z // half, core * half + z % half)
    depth = grad_ref.shape[1]
    half_rows, width = held.shape

    for at, (source, source_in) in enumerate(((inputs_hbm, inputs_in_hbm), (skips_hbm, skips_in_hbm))):
        slot = frames_in.at[1 - core if at == 0 else core]

        @pl.when(stays)
        def _():
            pltpu.make_async_copy(source, slot, loads.at[at]).start()

        @pl.when(leaves)
        def _():
            pltpu.make_async_copy(source_in, slot, loads.at[at]).start()

    sender = Sender(sems, PIECES)
    near = [("dp", 1)] + [("dp", bit) for bit in dp_bits] + [("tensor", bit) for bit in z_bits]
    barrier = pltpu.get_barrier_semaphore()
    for axis, bit in near:
        pl.semaphore_signal(
            barrier, inc=1, device_id=sender.device(axis, bit), device_id_type=pl.DeviceIdType.MESH
        )

    @pl.when(leaves)
    def _():
        pl.semaphore_signal(barrier, inc=1, device_id=there, device_id_type=pl.DeviceIdType.MESH)
        pl.semaphore_wait(barrier, len(near) + 1)

    @pl.when(stays)
    def _():
        pl.semaphore_wait(barrier, len(near))

    def start_move(k):
        @pl.when(leaves)
        def _():
            in_pieces(grad_ref, grad_in_hbm, sems, 0, there, [k])[0].start()

    def settle(starts, size):
        for side in range(2):
            skip_out_ref[rows_at(offset + starts[side], size), :] = held[rows_at(starts[side], size), :]
        yield

    offset = core * half_rows

    def skips():
        for slot in range(2):
            pltpu.make_async_copy(inputs_hbm, frames_in.at[slot], loads.at[slot]).wait()
        for slot, target in ((0, away), (1, held)):

            @pl.loop(0, depth // 256)
            def _(i):
                cut = frames_in[slot, :, pl.ds(pl.multiple_of(i * 256, 256), 256)]
                grad = lax.dot_general(cut, grad_ref[...], TN, preferred_element_type=F32).astype(BF)
                for k in range(depth // width):
                    target[rows_at(k * depth + i * 256, 256), :] = grad[:, k * width : (k + 1) * width]

            if slot == 0:
                copy = sender.send(away, first_in, "dp", 1)
                yield
        copy.wait()
        add_rows(held, 0, first_in, 0, half_rows)
        down = [
            [("dp", bit) for bit in dp_bits] + [("tensor", bit) for bit in z_bits],
            [("dp", bit) for bit in reversed(dp_bits)] + [("tensor", bit) for bit in z_bits],
        ]
        yield from sum_tree(sender, held, half_in, down, settle, down, skip_out_ref, offset)
        mine = skip_out_ref.at[rows_at(offset, half_rows), :]
        copy = sender.send(mine, mine, "dp", 1)
        yield
        copy.wait()

    running = [skips(), spread_sums(sender, sums_ref[...], sums_in, sums_out_ref, parts)]
    rounds = 0
    later = 1 + len(dp_bits) + 2 * len(z_bits) + 1
    while running:
        if rounds in (0, 1, later, later + 1):
            start_move(rounds if rounds < 2 else rounds - later + 2)
        rounds += 1
        run_all(running)

    @pl.when(leaves)
    def _():
        for copy in in_pieces(grad_ref, grad_in_hbm, sems, 0, there):
            copy.wait()


def sums(inputs, inputs_in, skips, skips_in, grad_base, utterance_sums, rows_all, parts):
    frames, depth = inputs.shape
    devices = rows_all * parts
    width = min(depth, depth * depth // (16 * devices))
    half_rows = depth * depth // width
    stages = rows_all.bit_length() + parts.bit_length() - 3
    copies = PIECES + 2 + 4 * stages + rows_all.bit_length() + parts.bit_length()
    vmem = pl.BlockSpec(memory_space=pltpu.VMEM)
    anywhere = pl.BlockSpec(memory_space=pl.ANY)
    shape = lambda *s: jax.ShapeDtypeStruct(*s)
    skip_sum, all_sums, grad_base_in = pl.pallas_call(
        functools.partial(sums_kernel, rows_all=rows_all, parts=parts),
        in_specs=[anywhere] * 4 + [vmem] * 2,
        out_specs=[vmem] * 2 + [anywhere],
        out_shape=[
            shape((2 * half_rows, width), BF),
            shape((rows_all,) + utterance_sums.shape, F32),
            shape((frames, depth), BF),
        ],
        scratch_shapes=[pltpu.VMEM((2, frames, depth), BF)]
        + [pltpu.VMEM((half_rows, width), BF)] * 4
        + [
            pltpu.VMEM((2 * parts.bit_length() - 1,) + utterance_sums.shape, F32),
            pltpu.SemaphoreType.DMA((2,)),
            pltpu.SemaphoreType.DMA((2 * copies,)),
        ],
        compiler_params=pltpu.CompilerParams(
            collective_id=0, has_side_effects=True, vmem_limit_bytes=56 * MIB
        ),
        cost_estimate=cost(100),
        name="sums",
    )(inputs, inputs_in, skips, skips_in, grad_base, utterance_sums)
    skip_sum = skip_sum.reshape(2, depth // width, depth, width)
    skip_sum = jnp.transpose(skip_sum, (0, 2, 1, 3)).reshape(2, depth, depth)
    return skip_sum, all_sums, grad_base_in


def front_kernel(
    ends_ref, inputs_ref, skips_ref, w_in_ref, w_res_ref, segment_ref, shift_ref, scale_ref, rate_ref, weight_hbm, w_out_ref,
    base_ref, out_ref, cos_ref, sin_ref, qmark_ref, kmark_ref, weight_in_hbm, w_out_all_ref, away, local, sems,
    *, parts, utt,
):
    d, z, core, half = mesh_spot(parts)
    stays = z // half == core
    leaves = jnp.logical_not(stays)
    there = ((d - core) + z // half, core * half + z % half)
    frames = base_ref.shape[0]
    rows = 256
    chunks = frames // rows

    barrier = pltpu.get_barrier_semaphore()
    near = [partner_of(d, z, b, half) for b in range(1, half + 1)] + [(d ^ bit, z) for bit in (2, 4, 6)]
    near += [(d, z ^ k) for k in range(half, parts)]
    for device in near:
        pl.semaphore_signal(barrier, inc=1, device_id=device, device_id_type=pl.DeviceIdType.MESH)

    @pl.when(leaves)
    def _():
        pl.semaphore_signal(barrier, inc=1, device_id=there, device_id_type=pl.DeviceIdType.MESH)
        pl.semaphore_wait(barrier, len(near) + 1)

    @pl.when(stays)
    def _():
        pl.semaphore_wait(barrier, len(near))

    def here(k):
        return pl.ds(pl.multiple_of(k * rows, rows), rows)

    def copy(kind, k, source, target, device):
        at = kind * chunks + k
        return pltpu.make_async_remote_copy(
            src_ref=source,
            dst_ref=target,
            send_sem=sems.at[2 * at],
            recv_sem=sems.at[2 * at + 1],
            device_id=device,
            device_id_type=pl.DeviceIdType.MESH,
        )

    def moving(k):
        return copy(0, k, away.at[here(k), :], out_ref.at[0, here(k), :], there)

    quarter = weight_hbm.shape[0] // 4
    column = d // 2 % 4

    def weight_part(k):
        cut = pl.ds(pl.multiple_of((column ^ k) * quarter, 16), quarter)
        if k == 0:
            return copy(parts, 0, weight_hbm.at[cut, :], weight_in_hbm.at[cut, :], there)
        own = pl.ds(pl.multiple_of(column * quarter, 16), quarter)
        return copy(parts, k, weight_in_hbm.at[own, :], weight_in_hbm.at[own, :], (d ^ (2 * k), z))

    @pl.when(leaves)
    def _():
        weight_part(0).start()

    @pl.when(stays)
    def _():
        pltpu.make_async_copy(weight_hbm, weight_in_hbm, local).start()

    eighth = d // 2 % 4 + 4 * core
    per = w_out_all_ref.shape[2]
    w_out_all_ref[eighth, z] = w_out_ref[pl.ds(pl.multiple_of(eighth * per, 16), per), :]

    def w_out_part(k):
        if k < parts:
            cut = w_out_all_ref.at[eighth, z]
            return copy(parts, 3 + k, cut, cut, (d, z ^ k))
        size = 1 << (k - parts)
        cut = w_out_all_ref.at[pl.ds(eighth // size * size, size)]
        return copy(parts, 3 + k, cut, cut, (d ^ (2, 4, 1)[k - parts], z))

    for k in range(1, parts):
        w_out_part(k).start()

    def across(b, k):
        return copy(b, k, out_ref.at[0, here(k), :], out_ref.at[b, here(k), :], partner_of(d, z, b, half))

    def beside(b, k):
        return copy(
            half + b, k, out_ref.at[b, here(k), :], out_ref.at[half + b, here(k), :], partner_of(d, z, half, half)
        )

    def spread_own(k):
        for b in range(1, half):
            across(b, k).start()
        beside(0, k).start()

    @pl.loop(0, chunks)
    def _(k):
        at = here(k)
        base = jnp.dot(inputs_ref[at, :], w_in_ref[...], preferred_element_type=F32)
        base = base + jnp.dot(skips_ref[at, :], w_res_ref[...], preferred_element_type=F32)
        base_ref[at, :] = base.astype(BF)
        unit, _ = unit_norm(base)
        segment = segment_ref[at, :]
        normed = (unit * (1.0 + spread(segment, scale_ref[...])) + spread(segment, shift_ref[...])).astype(BF)

        @pl.when(stays)
        def _():
            out_ref[0, at, :] = normed
            spread_own(k)

        @pl.when(leaves)
        def _():
            away[at, :] = normed
            moving(k).start()

    part = core * half + z % half

    @pl.loop(0, parts * chunks)
    def _(i):
        at = here(i)
        place = (part ^ (i // chunks)) * frames + (i % chunks) * rows
        place = place + lax.broadcasted_iota(jnp.int32, (rows, LANES), 0)
        lane = lax.broadcasted_iota(jnp.int32, (rows, LANES), 1)
        segment = jnp.zeros((rows, LANES), jnp.int32)
        start = jnp.zeros((rows, LANES), jnp.int32)
        for u in range(utt - 1):
            past = place >= ends_ref[u]
            segment = jnp.where(past, u + 1, segment)
            start = jnp.where(past, ends_ref[u], start)
        angle = (place - start).astype(F32) * rate_ref[0:1, :]
        cos_ref[at, :] = jnp.cos(angle)
        sin_ref[at, :] = jnp.sin(angle) * rate_ref[1:2, :]
        other = jnp.logical_and(lane < utt, lane != segment)
        qmark_ref[at, :] = jnp.where(other, MASKED, 0.0).astype(BF)
        shown = jnp.where(lane < utt + 3, 1.0, 0.0)
        kmark_ref[at, :] = jnp.where(other, 0.0, shown).astype(BF)

    for k in range(1, parts):
        w_out_part(k).wait()
    w_out_part(parts).start()

    @pl.when(leaves)
    def _():
        weight_part(0).wait()
        for k in range(1, 4):
            weight_part(k).start()

        @pl.loop(0, chunks)
        def _(k):
            moving(k).wait_recv()
            spread_own(k)

    w_out_part(parts).wait()
    w_out_part(parts + 1).start()

    @pl.loop(0, chunks)
    def _(k):
        for b in range(1, half):
            across(b, k).wait_recv()
            beside(b, k).start()

    w_out_part(parts + 1).wait()
    w_out_part(parts + 2).start()

    @pl.loop(0, chunks)
    def _(k):
        for b in range(half):
            beside(b, k).wait_recv()
            beside(b, k).wait_send()
        for b in range(1, half):
            across(b, k).wait_send()

    @pl.when(leaves)
    def _():
        @pl.loop(0, chunks)
        def _(k):
            moving(k).wait_send()

        for k in range(1, 4):
            weight_part(k).wait()

    @pl.when(stays)
    def _():
        pltpu.make_async_copy(weight_hbm, weight_in_hbm, local).wait()

    w_out_part(parts + 2).wait()


def front(ends, inputs, skips, w_in, w_res, segment, shift, scale, rate, weight, w_out, parts):
    frames, depth = inputs.shape
    utt = ends.shape[0]
    vmem = pl.BlockSpec(memory_space=pltpu.VMEM)
    return pl.pallas_call(
        functools.partial(front_kernel, parts=parts, utt=utt),
        in_specs=[pl.BlockSpec(memory_space=pltpu.SMEM)] + [vmem] * 8 + [pl.BlockSpec(memory_space=pl.ANY), vmem],
        out_specs=[vmem] * 6 + [pl.BlockSpec(memory_space=pl.ANY), vmem],
        out_shape=[
            jax.ShapeDtypeStruct((frames, depth), BF),
            jax.ShapeDtypeStruct((parts, frames, depth), BF),
            jax.ShapeDtypeStruct((parts * frames, LANES), F32),
            jax.ShapeDtypeStruct((parts * frames, LANES), F32),
            jax.ShapeDtypeStruct((parts * frames, LANES), BF),
            jax.ShapeDtypeStruct((parts * frames, LANES), BF),
            jax.ShapeDtypeStruct(weight.shape, BF),
            jax.ShapeDtypeStruct((8, parts, w_out.shape[0] // 8, depth), BF),
        ],
        scratch_shapes=[
            pltpu.VMEM((frames, depth), BF),
            pltpu.SemaphoreType.DMA,
            pltpu.SemaphoreType.DMA((2 * (parts * (frames // 256) + 6 + parts),)),
        ],
        compiler_params=pltpu.CompilerParams(
            collective_id=2, has_side_effects=True, vmem_limit_bytes=48 * MIB
        ),
        cost_estimate=cost(75),
        name="front",
    )(ends, inputs, skips, w_in, w_res, segment, shift, scale, rate, weight, w_out)


def dot(a, b, dims=(((1,), (0,)), ((), ()))):
    return lax.dot_general(a, b, dims, preferred_element_type=F32)


def after(value, token):
    return lax.optimization_barrier((value, token))[0]


def on_device(
    inputs, skip_input, lengths, time_steps, w_skip_in, w_skip_res, w_ada, w_qkv, w_out, w_up, w_down, cotangent
):
    parts = lax.axis_size("tensor")
    rows_all = lax.axis_size("dp")
    half = parts // 2
    columns = rows_all // 2
    d = lax.axis_index("dp")
    z = lax.axis_index("tensor")
    core, column = d % 2, d // 2
    stays = z // half == core
    part = core * half + z % half
    inputs, skip_input, cotangent = inputs[0], skip_input[0], cotangent[0]
    frames, depth = inputs.shape
    length = frames * parts
    ws = w_qkv.shape[2]
    pairs = ws // LANES
    utt = lengths.shape[1]
    both = ("dp", "tensor")

    def moved(value):
        pattern = [
            (i * parts + j, ((i // 2) * 2 + j // half) * parts + (i % 2) * half + j % half)
            for i in range(rows_all)
            for j in range(parts)
            if i % 2 != j // half
        ]
        return lax.ppermute(value, both, pattern)

    def partner(value, b):
        pattern = [
            (i * parts + j, (i ^ (b // half)) * parts + (j // half) * half + ((j % half) ^ (b % half)))
            for i in range(rows_all)
            for j in range(parts)
        ]
        return lax.ppermute(value, both, pattern)

    def exchange(blocks):
        return [blocks[0]] + [partner(blocks[b], b) for b in range(1, parts)]

    same_core = [[2 * i + k for i in range(columns)] for k in range(2)]

    other_lengths = partner(lengths, half)
    other_steps = partner(time_steps, half)
    lengths_work = jnp.where(stays, lengths, other_lengths)[0]
    steps_work = jnp.where(stays, time_steps, other_steps)[0]

    time_rate = jnp.exp(
        -math.log(10000.0) * (jnp.arange(w_ada.shape[0] // 2, dtype=F32) / (w_ada.shape[0] // 2))
    )

    def embed(steps):
        phases = steps.astype(F32)[:, None] * time_rate
        return jax.nn.silu(jnp.concatenate([jnp.sin(phases), jnp.cos(phases)], axis=-1)).astype(BF)

    def wide_segment(row_lengths, places):
        segment, _, _ = frame_marks(row_lengths, places, utt)
        return jnp.broadcast_to(segment[:, None], (places.shape[0], LANES))

    spot = jnp.arange(frames, dtype=jnp.int32)
    mods_home = dot(embed(time_steps[0]), w_ada[:, : 2 * depth])
    qkv_rows = jnp.transpose(w_qkv, (0, 2, 1)).reshape(3 * ws, depth)
    rotary_rate = jnp.exp(-math.log(10000.0) * (2.0 * jnp.arange(HEAD_DIM // 2, dtype=F32) / HEAD_DIM))
    sign = jnp.where(jnp.arange(LANES) % HEAD_DIM < HEAD_DIM // 2, -1.0, 1.0).astype(F32)
    base_home, normed_all, cosine, sine, qmark, kmark, w_mine, w_out_all = front(
        jnp.cumsum(lengths_work, dtype=jnp.int32),
        inputs,
        skip_input,
        w_skip_in,
        w_skip_res,
        wide_segment(lengths[0], z * frames + spot),
        mods_home[:, :depth],
        mods_home[:, depth:],
        jnp.stack([jnp.tile(rotary_rate, 4), sign]),
        qkv_rows,
        w_out,
        parts,
    )

    per_q, per_o = 3 * ws // rows_all, ws // rows_all
    units = w_down.shape[0]
    per_u = units // rows_all
    slice_feed = jnp.concatenate(
        [
            jnp.transpose(lax.dynamic_slice_in_dim(w_up, d * per_u, per_u, 1)),
            lax.dynamic_slice_in_dim(w_down, d * per_u, per_u, 0),
        ]
    )
    feed_rows = lax.all_gather(slice_feed, "tensor")
    feed_rows = lax.all_gather(after(feed_rows, base_home), "dp", axis_index_groups=same_core)
    feed_rows = feed_rows.reshape(columns * parts, 2, per_u, depth)

    cotangent = after(cotangent, base_home)
    cot = jnp.where(stays, cotangent, moved(cotangent))
    base_in = moved(after(base_home, cot))

    silu_work = embed(steps_work)
    mods = dot(silu_work, w_ada)
    shift_one, scale_one, shift_two, scale_two = [mods[:, k * depth : (k + 1) * depth] for k in range(4)]
    segment_here = wide_segment(lengths_work, part * frames + spot)

    qkv = project(normed_all.reshape(length, depth), w_mine, cosine, sine, pairs)

    def ranges(size, other):
        per = frames // size
        stored = jnp.arange(length // size, dtype=jnp.int32)
        natural = (part ^ (stored // per)) * per + stored % per
        return block_ranges(lengths_work, natural, size, other)

    own = jnp.stack([part.astype(jnp.int32), stays.astype(jnp.int32)])
    bq, bk = 512, 512
    low, high = ranges(bq, bk)
    low_back, high_back = ranges(bk, bq)
    ctx_pairs, lse_pairs, ctx_mine = [], [], []
    for pair in range(pairs):
        ctx, lse = attend(after(qkv, cot) if pair == pairs - 1 else qkv, pair, qmark, kmark, own, low, high, bq, bk, frames)
        ctx_pairs.append(ctx)
        lse_pairs.append(lse)
        ctx_mine += exchange([ctx[b] for b in range(parts)])
    hidden, ffn_in = join(
        own, ctx_mine, w_out_all, base_home, base_in, segment_here, shift_two, scale_two, pairs, parts
    )

    cot_other = partner(cot, half)
    spare = max(per_o, 16)
    heads = qkv_rows.reshape(3 * pairs, 8, LANES // 8, depth)
    out_own, out_send, gin_own, gin_send, grad_feed, inputs_in, w_heads = feed(
        ffn_in, cot, cot_other, feed_rows, inputs, heads, spare, parts
    )
    grad_hidden, low_grad, block_out, sums_two, *grad_context = turn(
        own, gin_own, partner(gin_send, half), out_own, partner(out_send, half), hidden, cot, skip_input, segment_here,
        scale_two,
        w_out_all, pairs, parts,
    )

    grad_feed = out_grad(low_grad, ctx_mine, grad_feed, 2 * per_u, pairs, parts, columns)
    grad_feed = grad_feed.reshape(columns, parts, 2 * per_u + spare, depth)
    feed_sum = lax.psum_scatter(grad_feed, "dp", scatter_dimension=0, axis_index_groups=same_core)
    grad_feed = lax.psum_scatter(feed_sum, "tensor", scatter_dimension=0)
    feed_shard = grad_feed
    grad_feed = lax.all_gather(grad_feed, "dp")
    grad_up = jnp.transpose(grad_feed[:, :per_u].reshape(units, depth)).astype(F32)
    grad_down = grad_feed[:, per_u : 2 * per_u].reshape(units, depth).astype(F32)
    grad_out = grad_feed[:, 2 * per_u : 2 * per_u + per_o].reshape(ws, depth).astype(F32)

    grad_mine = []
    for pair in range(pairs):
        grad = jnp.stack(exchange(grad_context[pair * parts : (pair + 1) * parts]))
        if pair == pairs - 1 and pairs > 1:
            grad = after(grad, feed_sum)
        grads = attend_back(
            qkv, pair, grad, ctx_pairs[pair], lse_pairs[pair], qmark, kmark, cosine, sine, own,
            low_back, high_back, bq, bk, utt, frames,
        )
        grad_mine.append(grads)

    returned = []
    for grads in grad_mine[:-1]:
        returned += exchange([grads[b] for b in range(parts)])
    block_out_in, skips_in = moved(block_out)
    grad_base, grad_qkv, sums_one = finish(
        returned, after(grad_mine, feed_shard), normed_all, w_heads, base_home, base_in, grad_hidden, segment_here, scale_one,
        pairs, parts, rows_all,
    )
    silu_rows = jnp.pad(silu_work.astype(F32) * (1.0 / parts), ((0, 0), (0, depth - silu_work.shape[1])))
    skip_sum, all_sums, grad_base_in = sums(
        inputs, inputs_in, skip_input, skips_in, grad_base, jnp.concatenate([sums_one, sums_two, silu_rows]),
        rows_all, parts,
    )
    grad_qkv = grad_qkv.reshape(-1, 3, ws, grad_qkv.shape[1])
    grad_qkv = jnp.transpose(grad_qkv, (1, 0, 3, 2)).reshape(3, depth, ws).astype(F32)
    grad_skip = skip_sum.astype(F32)
    grad_base_home = jnp.where(stays, grad_base, grad_base_in)
    grad_inputs = dot(grad_base_home, w_skip_in, NT)
    grad_skips = dot(grad_base_home, w_skip_res, NT)
    block_out = jnp.where(stays, block_out[0], block_out_in).astype(F32)

    all_sums = all_sums.reshape(rows_all, 5, utt, depth)
    silu_all = all_sums[:, 4, :, : w_ada.shape[0]].reshape(rows_all * utt, w_ada.shape[0])
    all_sums = jnp.concatenate([all_sums[:, k] for k in range(4)], axis=-1).reshape(rows_all * utt, 4 * depth)
    grad_ada = jnp.einsum("ut,um->tm", silu_all, all_sums, precision=lax.Precision.HIGHEST)

    return (
        block_out[None],
        grad_inputs[None],
        grad_skips[None],
        grad_skip[0],
        grad_skip[1],
        grad_ada,
        grad_qkv,
        grad_out,
        grad_up,
        grad_down,
    )


def solution(mesh):
    placed = (
        P("dp", "tensor", None),
        P("dp", "tensor", None),
        P("dp", None),
        P("dp", None),
        P(),
        P(),
        P(),
        P(None, None, "tensor"),
        P("tensor", None),
        P(None, "tensor"),
        P("tensor", None),
        P("dp", "tensor", None),
    )
    return jax.shard_map(
        on_device,
        mesh=mesh,
        in_specs=placed,
        out_specs=(
            P("dp", "tensor", None),
            P("dp", "tensor", None),
            P("dp", "tensor", None),
            P(),
            P(),
            P(),
            P(None, None, "tensor"),
            P("tensor", None),
            P(None, "tensor"),
            P("tensor", None),
        ),
        check_vma=False,
    )
```

```python
import functools
import math

import jax
import jax.numpy as jnp
from jax import lax
from jax.experimental import pallas as pl
from jax.experimental.pallas import tpu as pltpu
from jax.sharding import PartitionSpec as P

HEAD_DIM = 64
LANES = 128
MASKED = -1e30
LOG2E = math.log2(math.e)
MIB = 2**20
BF = jnp.bfloat16
F32 = jnp.float32
norm_epsilon = 1e-06
NT = (((1,), (1,)), ((), ()))
TN = (((0,), (0,)), ((), ()))


def cost(microseconds):
    return pl.CostEstimate(flops=int(microseconds * 1.1e9), bytes_accessed=0, transcendentals=0)


def stored_block(block, own, per_part):
    shift = per_part.bit_length() - 1
    part = lax.shift_right_logical(block, shift)
    return ((part ^ own) << shift) | (block & (per_part - 1))


def swap_halves(values):
    lane = lax.broadcasted_iota(jnp.int32, values.shape, 1)
    return jnp.where(lane % 64 < 32, pltpu.roll(values, 96, 1), pltpu.roll(values, 32, 1))


def mesh_spot(parts):
    d = lax.axis_index("dp")
    z = lax.axis_index("tensor")
    return d, z, d % 2, parts // 2


def partner_of(d, z, b, half):
    return d ^ (b // half), z ^ (b % half)


def remote_copy(source, target, sems, at, device):
    return pltpu.make_async_remote_copy(
        src_ref=source,
        dst_ref=target,
        send_sem=sems.at[2 * at],
        recv_sem=sems.at[2 * at + 1],
        device_id=device,
        device_id_type=pl.DeviceIdType.MESH,
    )


PIECES = 4


def in_pieces(source, target, sems, at, device, pieces=range(PIECES)):
    rows = source.shape[0] // PIECES
    return [
        remote_copy(
            source.at[k * rows : (k + 1) * rows, :], target.at[k * rows : (k + 1) * rows, :], sems, at + k, device
        )
        for k in pieces
    ]


def remote(source, target, sems, at, device):
    copy = remote_copy(source, target, sems, at, device)
    copy.start()
    return copy


def greet(devices):
    barrier = pltpu.get_barrier_semaphore()
    for device in devices:
        pl.semaphore_signal(barrier, inc=1, device_id=device, device_id_type=pl.DeviceIdType.MESH)
    pl.semaphore_wait(barrier, len(devices))


def project_kernel(normed_ref, weight_ref, cos_ref, sin_ref, out_ref, *, pairs):
    normed = normed_ref[...]
    cosine = cos_ref[...]
    sine = sin_ref[...]
    width = pairs * LANES
    for kind in range(3):
        weight = weight_ref[kind * width : (kind + 1) * width, :]
        part = lax.dot_general(normed, weight, NT, preferred_element_type=F32)
        for pair in range(pairs):
            cut = part[:, pair * LANES : (pair + 1) * LANES]
            if kind < 2:
                cut = cut * cosine + swap_halves(cut) * sine
            if kind == 0:
                cut = cut * (LOG2E * HEAD_DIM**-0.5)
            out_ref[pair * 3 + kind] = cut.astype(BF)


def project(normed_all, weight, cosine, sine, pairs):
    length, depth = normed_all.shape
    rows = 512
    return pl.pallas_call(
        functools.partial(project_kernel, pairs=pairs),
        grid=(length // rows,),
        in_specs=[
            pl.BlockSpec((rows, depth), lambda i: (i, 0)),
            pl.BlockSpec(weight.shape, lambda i: (0, 0)),
            pl.BlockSpec((rows, LANES), lambda i: (i, 0)),
            pl.BlockSpec((rows, LANES), lambda i: (i, 0)),
        ],
        out_specs=pl.BlockSpec((3 * pairs, rows, LANES), lambda i: (0, i, 0)),
        out_shape=jax.ShapeDtypeStruct((3 * pairs, length, LANES), BF),
        compiler_params=pltpu.CompilerParams(vmem_limit_bytes=40 * MIB),
        cost_estimate=cost(11),
        name="project",
    )(normed_all, weight, cosine, sine)


def attend_kernel(
    own_ref, low_ref, high_ref, q_ref, k_ref, v_ref, qmark_ref, kmark_ref, ctx_ref, lse_ref, keys, vals,
    *, bq, bk, per_part,
):
    step = pl.program_id(0)
    length = kmark_ref.shape[0]
    own = own_ref[0]

    @pl.when(step == 0)
    def _():
        lane = lax.broadcasted_iota(jnp.int32, (512, LANES), 1)

        @pl.loop(0, length // 512)
        def _(i):
            rows = pl.ds(pl.multiple_of(i * 512, 512), 512)
            keys[rows, :LANES] = k_ref[0, rows, :]
            keys[rows, LANES:] = kmark_ref[rows, :]
            v = v_ref[0, rows, :]
            one = jnp.ones_like(v)
            vals[0, rows, :] = jnp.where(lane < 64, v, one)
            vals[1, rows, :] = jnp.where(lane < 64, one, v)

    first = lax.broadcasted_iota(jnp.int32, (bq, LANES), 1) < 64
    q = q_ref[0]
    mark = qmark_ref[...]
    zero = jnp.zeros_like(q)
    queries = (
        jnp.concatenate([jnp.where(first, q, zero), mark], axis=1),
        jnp.concatenate([jnp.where(first, zero, q), mark], axis=1),
    )

    def body(j, carry):
        rows = pl.ds(pl.multiple_of(stored_block(j, own, per_part // bk) * bk, bk), bk)
        block = keys[rows, :]
        new = []
        for head in range(2):
            peak, total = carry[head]
            scores = lax.dot_general(queries[head], block, NT, preferred_element_type=F32)
            cuts = [scores[:, k * LANES : (k + 1) * LANES] for k in range(bk // LANES)]
            tallest = functools.reduce(jnp.maximum, cuts)
            higher = jnp.maximum(peak, jnp.max(tallest, axis=1, keepdims=True))
            weights = jnp.concatenate([jnp.exp2(cut - higher).astype(BF) for cut in cuts], axis=1)
            total = total * jnp.exp2(peak - higher) + jnp.dot(
                weights, vals[head, rows, :], preferred_element_type=F32
            )
            new.append((higher, total))
        return tuple(new)

    init = (jnp.full((bq, LANES), -3e38, F32), jnp.zeros((bq, LANES), F32))
    (peak_a, sum_a), (peak_b, sum_b) = lax.fori_loop(low_ref[step], high_ref[step], body, (init, init))
    weight_sum = pltpu.roll(jnp.where(first, sum_b, sum_a), 64, 1)
    ctx_ref[0] = (jnp.where(first, sum_a, sum_b) / weight_sum).astype(BF)
    lse_ref[...] = jnp.where(first, peak_a, peak_b) + jnp.log2(weight_sum)


def attend(qkv, pair, qmark, kmark, own, low, high, bq, bk, per_part):
    length = qmark.shape[0]
    row = lambda i, *_: (i, 0)
    whole = lambda i, *_: (0, 0)
    return pl.pallas_call(
        functools.partial(attend_kernel, bq=bq, bk=bk, per_part=per_part),
        grid_spec=pltpu.PrefetchScalarGridSpec(
            num_scalar_prefetch=3,
            grid=(length // bq,),
            in_specs=[
                pl.BlockSpec((1, bq, LANES), lambda i, *_: (3 * pair, i, 0)),
                pl.BlockSpec((1, length, LANES), lambda i, *_: (3 * pair + 1, 0, 0)),
                pl.BlockSpec((1, length, LANES), lambda i, *_: (3 * pair + 2, 0, 0)),
                pl.BlockSpec((bq, LANES), row),
                pl.BlockSpec((length, LANES), whole),
            ],
            out_specs=[
                pl.BlockSpec((1, bq, LANES), lambda i, *_: (i // (per_part // bq), i % (per_part // bq), 0)),
                pl.BlockSpec((bq, LANES), row),
            ],
            scratch_shapes=[pltpu.VMEM((length, 2 * LANES), BF), pltpu.VMEM((2, length, LANES), BF)],
        ),
        out_shape=[
            jax.ShapeDtypeStruct((length // per_part, per_part, LANES), BF),
            jax.ShapeDtypeStruct((length, LANES), F32),
        ],
        compiler_params=pltpu.CompilerParams(
            dimension_semantics=("arbitrary",), vmem_limit_bytes=48 * MIB
        ),
        cost_estimate=cost(35),
        name="attend",
    )(own, low, high, qkv, qkv, qkv, qmark, kmark)


def three_parts(value):
    high = value.astype(BF).astype(F32)
    rest = value - high
    middle = rest.astype(BF).astype(F32)
    return high, middle, (rest - middle).astype(BF).astype(F32)


def attend_back_kernel(
    own_ref, low_ref, high_ref, q_ref, k_ref, v_ref, do_ref, ctx_ref, lse_ref, qmark_ref, kmark_ref, cos_ref,
    sin_ref, out_ref, keys, vals, key_heads, query_heads, grad_heads, dq_sum,
    *, bq, bk, utt, per_part,
):
    length = kmark_ref.shape[0]
    own = own_ref[0]
    pb = 512
    lane = lax.broadcasted_iota(jnp.int32, (pb, LANES), 1)
    first = lane < 64

    @pl.loop(0, length // pb)
    def _(i):
        rows = pl.ds(pl.multiple_of(i * pb, pb), pb)
        at, within = i // (per_part // pb), pl.ds(pl.multiple_of(i % (per_part // pb) * pb, pb), pb)
        k = k_ref[0, rows, :]
        zero = jnp.zeros_like(k)
        mark = kmark_ref[rows, :]
        keys[rows, :LANES] = k
        keys[rows, LANES:] = mark
        vals[rows, :LANES] = v_ref[0, rows, :]
        vals[rows, LANES:] = mark
        q = q_ref[0, rows, :]
        grad = do_ref[at, within, :]
        qmark = qmark_ref[rows, :].astype(F32)
        lse = lse_ref[rows, :]
        product = grad.astype(F32) * ctx_ref[at, within, :].astype(F32)
        for head in range(2):
            mine = first if head == 0 else jnp.logical_not(first)
            key_heads[head, rows, :] = jnp.where(mine, k, zero)
            query_heads[head, rows, :LANES] = jnp.where(mine, q, zero)
            grad_heads[head, rows, :LANES] = jnp.where(mine, grad, zero)
            high, middle, low = three_parts(-lse[:, 64 * head : 64 * head + 1])
            query_heads[head, rows, LANES:] = jnp.where(
                lane == utt, high, jnp.where(lane == utt + 1, middle, jnp.where(lane == utt + 2, low, qmark))
            ).astype(BF)
            delta = jnp.sum(jnp.where(mine, product, 0.0), axis=1, keepdims=True)
            high, middle, low = three_parts(-delta)
            grad_heads[head, rows, LANES:] = jnp.where(
                lane == utt, high, jnp.where(lane == utt + 1, middle, jnp.where(lane == utt + 2, low, 0.0))
            ).astype(BF)
        dq_sum[rows, :] = jnp.zeros((pb, LANES), F32)

    @pl.loop(0, length // bk)
    def _(j):
        key_rows = pl.ds(pl.multiple_of(j * bk, bk), bk)
        key_block = keys[key_rows, :]
        value_block = vals[key_rows, :]

        def body(i, carry):
            dk, dv = carry
            rows = pl.ds(pl.multiple_of(stored_block(i, own, per_part // bq) * bq, bq), bq)
            dq = dq_sum[rows, :]
            for head in range(2):
                query = query_heads[head, rows, :]
                grad = grad_heads[head, rows, :]
                probs = jnp.exp2(lax.dot_general(key_block, query, NT, preferred_element_type=F32))
                pulled = lax.dot_general(value_block, grad, NT, preferred_element_type=F32)
                grad_scores = (probs * pulled).astype(BF)
                dv = dv + jnp.dot(probs.astype(BF), grad[:, :LANES], preferred_element_type=F32)
                dk = dk + jnp.dot(grad_scores, query[:, :LANES], preferred_element_type=F32)
                dq = dq + lax.dot_general(
                    grad_scores, key_heads[head, key_rows, :], TN, preferred_element_type=F32
                )
            dq_sum[rows, :] = dq
            return dk, dv

        zero = jnp.zeros((bk, LANES), F32)
        dk, dv = lax.fori_loop(low_ref[j], high_ref[j], body, (zero, zero))
        at, within = j // (per_part // bk), pl.ds(pl.multiple_of(j % (per_part // bk) * bk, bk), bk)
        out_ref[at, 2, within, :] = dv.astype(BF)
        dk = dk * (1.0 / LOG2E)
        out_ref[at, 1, within, :] = (dk * cos_ref[key_rows, :] - swap_halves(dk) * sin_ref[key_rows, :]).astype(BF)

    @pl.loop(0, length // pb)
    def _(i):
        rows = pl.ds(pl.multiple_of(i * pb, pb), pb)
        at, within = i // (per_part // pb), pl.ds(pl.multiple_of(i % (per_part // pb) * pb, pb), pb)
        dq = dq_sum[rows, :] * HEAD_DIM**-0.5
        out_ref[at, 0, within, :] = (dq * cos_ref[rows, :] - swap_halves(dq) * sin_ref[rows, :]).astype(BF)


def attend_back(
    qkv, pair, grad, ctx, lse, qmark, kmark, cosine, sine, own, low, high, bq, bk, utt, per_part
):
    length = qmark.shape[0]
    in_smem = pl.BlockSpec(memory_space=pltpu.SMEM)
    whole = pl.BlockSpec((length, LANES), lambda i: (0, 0))
    parts = length // per_part
    by_part = pl.BlockSpec((parts, per_part, LANES), lambda i: (0, 0, 0))
    cut = lambda kind: pl.BlockSpec((1, length, LANES), lambda i: (3 * pair + kind, 0, 0))
    wide = pltpu.VMEM((length, 2 * LANES), BF)
    return pl.pallas_call(
        functools.partial(attend_back_kernel, bq=bq, bk=bk, utt=utt, per_part=per_part),
        grid=(1,),
        in_specs=[in_smem] * 3 + [cut(0), cut(1), cut(2)] + [by_part] * 2 + [whole] * 5,
        out_specs=pl.BlockSpec((parts, 3, per_part, LANES), lambda i: (0, 0, 0, 0)),
        out_shape=jax.ShapeDtypeStruct((parts, 3, per_part, LANES), BF),
        scratch_shapes=[
            wide,
            wide,
            pltpu.VMEM((2, length, LANES), BF),
            pltpu.VMEM((2, length, 2 * LANES), BF),
            pltpu.VMEM((2, length, 2 * LANES), BF),
            pltpu.VMEM((length, LANES), F32),
        ],
        compiler_params=pltpu.CompilerParams(vmem_limit_bytes=56 * MIB),
        cost_estimate=cost(66),
        name="attend_back",
    )(own, low, high, qkv, qkv, qkv, grad, ctx, lse, qmark, kmark, cosine, sine)


def frame_marks(lengths, places, utt):
    ends = jnp.cumsum(lengths)
    starts = ends - lengths
    segment = jnp.sum((places[:, None] >= ends[None, :]).astype(jnp.int32), axis=1, dtype=jnp.int32)
    member = segment[:, None] == jnp.arange(utt, dtype=jnp.int32)[None, :]
    offsets = jnp.sum(jnp.where(member, starts[None, :], 0), axis=1, dtype=jnp.int32)
    return segment, member, offsets


def block_ranges(lengths, blocks, size, other):
    ends = jnp.cumsum(lengths)
    starts = ends - lengths
    at_first = blocks * size
    at_last = at_first + (size - 1)
    index = jnp.arange(lengths.shape[0], dtype=jnp.int32)
    seg_first = jnp.sum((at_first[:, None] >= ends[None]).astype(jnp.int32), axis=1)
    seg_last = jnp.sum((at_last[:, None] >= ends[None]).astype(jnp.int32), axis=1)
    low = jnp.sum(jnp.where(index[None] == seg_first[:, None], starts[None], 0), axis=1)
    high = jnp.sum(jnp.where(index[None] == seg_last[:, None], ends[None], 0), axis=1)
    return (low // other).astype(jnp.int32), ((high + other - 1) // other).astype(jnp.int32)


def feed_kernel(
    x_own_ref, cot_own_ref, cot_other_ref, weights_ref, heads_hbm,
    out_own_ref, out_other_ref, gin_own_ref, gin_other_ref, grads_ref, heads_out_hbm,
    x_other_ref, out_sum, gin_sum, local, sems, *, parts,
):
    step = pl.program_id(0)
    last = pl.num_programs(0) - 1
    d, z, core, half = mesh_spot(parts)
    beside = partner_of(d, z, half, half)

    eighth = d // 2 % 4 + 4 * core

    def heads_part(k):
        if k < parts:
            cut = heads_out_hbm.at[eighth, z]
            return remote_copy(cut, cut, sems, PIECES + k, (d, z ^ k))
        size = 1 << (k - parts)
        cut = heads_out_hbm.at[pl.ds(eighth // size * size, size)]
        return remote_copy(cut, cut, sems, PIECES + k, (d ^ (2, 4)[k - parts], z))

    @pl.when(step == 0)
    def _():
        greet([(d ^ bit, z) for bit in (1, 2, 4)] + [(d, z ^ k) for k in range(1, parts)])
        remote_copy(x_own_ref, x_other_ref, sems, 0, beside).start()
        copy = pltpu.make_async_copy(heads_hbm.at[:, eighth], heads_out_hbm.at[eighth, z], local)
        copy.start()
        copy.wait()
        for k in range(1, parts):
            heads_part(k).start()

    @pl.when(step == 2)
    def _():
        for k in range(1, parts):
            heads_part(k).wait()
        heads_part(parts).start()

    @pl.when(step == 4)
    def _():
        heads_part(parts).wait()
        heads_part(parts + 1).start()

    chunk, depth = weights_ref.shape[0] * weights_ref.shape[2], weights_ref.shape[3]
    up = weights_ref[:, 0].reshape(chunk, depth)
    down = weights_ref[:, 1].reshape(chunk, depth)
    root = math.sqrt(2.0 / math.pi)
    gup = gdown = None
    for side, (x_ref, cot_ref) in enumerate(((x_own_ref, cot_own_ref), (x_other_ref, cot_other_ref))):
        if side == 1:

            @pl.when(step == 0)
            def _():
                remote_copy(x_own_ref, x_other_ref, sems, 0, beside).wait()

        x = x_ref[...]
        cot = cot_ref[...]
        before = lax.dot_general(x, up, NT, preferred_element_type=F32)
        grad_act = lax.dot_general(cot, down, NT, preferred_element_type=F32)
        square = before * before
        bend = jnp.tanh(root * before * (1.0 + 0.044715 * square))
        half = 0.5 * (1.0 + bend)
        activated = (before * half).astype(BF)
        slope = half + 0.5 * before * (1.0 - bend * bend) * (root + (3.0 * 0.044715 * root) * square)
        grad_before = (grad_act * slope).astype(BF)
        out = jnp.dot(activated, down, preferred_element_type=F32)
        gin = jnp.dot(grad_before, up, preferred_element_type=F32)
        gd = lax.dot_general(activated, cot, TN, preferred_element_type=F32)
        gu = lax.dot_general(grad_before, x, TN, preferred_element_type=F32)
        gup = gu if side == 0 else gup + gu
        gdown = gd if side == 0 else gdown + gd

        @pl.when(step == 0)
        def _():
            out_sum[side] = out
            gin_sum[side] = gin

        @pl.when(step > 0)
        def _():
            out_sum[side] += out
            gin_sum[side] += gin

    per = weights_ref.shape[2]
    grads_ref[:, :per] = gup.astype(BF).reshape(-1, per, depth)
    grads_ref[:, per : 2 * per] = gdown.astype(BF).reshape(-1, per, depth)
    grads_ref[:, 2 * per :] = jnp.zeros(grads_ref[:, 2 * per :].shape, BF)

    @pl.when(step == last)
    def _():
        out_own_ref[...] = out_sum[0]
        out_other_ref[...] = out_sum[1].astype(BF)
        gin_own_ref[...] = gin_sum[0]
        gin_other_ref[...] = gin_sum[1].astype(BF)

        heads_part(parts + 1).wait()


def feed(x_own, cot_own, cot_other, weights, heads, spare, parts):
    frames, depth = x_own.shape
    groups, _, per, _ = weights.shape
    chunk = 256
    whole = pl.BlockSpec((frames, depth), lambda j: (0, 0))
    cut = pl.BlockSpec((chunk // per, 2, per, depth), lambda j: (j, 0, 0, 0))
    grads = pl.BlockSpec((chunk // per, 2 * per + spare, depth), lambda j: (j, 0, 0))
    shape = lambda *s: jax.ShapeDtypeStruct(*s)
    anywhere = pl.BlockSpec(memory_space=pl.ANY)
    return pl.pallas_call(
        functools.partial(feed_kernel, parts=parts),
        grid=(groups * per // chunk,),
        in_specs=[whole] * 3 + [cut, anywhere],
        out_specs=[whole] * 4 + [grads, anywhere],
        out_shape=[
            shape((frames, depth), F32),
            shape((frames, depth), BF),
            shape((frames, depth), F32),
            shape((frames, depth), BF),
            shape((groups, 2 * per + spare, depth), BF),
            shape((8, parts) + heads.shape[:1] + heads.shape[2:], BF),
        ],
        scratch_shapes=[
            pltpu.VMEM((frames, depth), BF),
            pltpu.VMEM((2, frames, depth), F32),
            pltpu.VMEM((2, frames, depth), F32),
            pltpu.SemaphoreType.DMA,
            pltpu.SemaphoreType.DMA((2 * (PIECES + parts + 3),)),
        ],
        compiler_params=pltpu.CompilerParams(
            dimension_semantics=("arbitrary",), vmem_limit_bytes=60 * MIB, collective_id=3, has_side_effects=True
        ),
        cost_estimate=cost(84),
        name="feed",
    )(x_own, cot_own, cot_other, weights, heads)


def spread(segment, table):
    masks = [segment == u for u in range(1, table.shape[0])]
    columns = []
    for k in range(table.shape[1] // LANES):
        cut = table[:, k * LANES : (k + 1) * LANES]
        out = jnp.broadcast_to(cut[0:1], segment.shape)
        for u, mask in enumerate(masks):
            out = jnp.where(mask, cut[u + 1 : u + 2], out)
        columns.append(out)
    return jnp.concatenate(columns, axis=1)


def collect(segment, values, utt):
    rows = []
    for u in range(utt):
        mask = segment == u
        rows.append(
            jnp.concatenate(
                [
                    jnp.sum(jnp.where(mask, values[:, k * LANES : (k + 1) * LANES], 0.0), axis=0, keepdims=True)
                    for k in range(values.shape[1] // LANES)
                ],
                axis=1,
            )
        )
    return jnp.concatenate(rows, axis=0)


def unit_norm(hidden):
    center = hidden - jnp.mean(hidden, axis=-1, keepdims=True)
    inverse = lax.rsqrt(jnp.mean(center * center, axis=-1, keepdims=True) + norm_epsilon)
    return center * inverse, inverse


def pull_norm(unit, inverse, grad, gain):
    pulled = grad * gain
    return (
        pulled
        - jnp.mean(pulled, axis=-1, keepdims=True)
        - unit * jnp.mean(pulled * unit, axis=-1, keepdims=True)
    ) * inverse


def join_kernel(*refs, pairs, parts):
    ctx_refs, refs = refs[: (pairs - 1) * parts], refs[(pairs - 1) * parts :]
    (
        last_hbm, w_out_ref, base_ref, base_in_ref, segment_ref, shift_ref, scale_ref,
        hidden_ref, normed_ref, last_out_hbm, last, local, sems,
    ) = refs
    step = pl.program_id(0)
    steps = pl.num_programs(0)
    d, z, core, half = mesh_spot(parts)
    part = core * half + z % half
    stays = z // half == core
    rows = hidden_ref.shape[0]

    def chunk(b, k):
        here = pl.ds(pl.multiple_of(k * rows, rows), rows)
        return remote_copy(
            last_hbm.at[b, here, :], last.at[b, here, :], sems, k * parts + b, partner_of(d, z, b, half)
        )

    own = pltpu.make_async_copy(last_hbm.at[0], last.at[0], local)

    @pl.when(step == 0)
    def _():
        own.start()
        greet([partner_of(d, z, b, half) for b in range(1, parts)])

        @pl.loop(0, steps)
        def _(k):
            for b in range(1, parts):
                chunk(b, k).start()

    hidden = jnp.where(stays, base_ref[...], base_in_ref[...]).astype(F32)
    for b in range(parts):
        for pair in range(pairs - 1):
            weights = w_out_ref[:, part ^ b].reshape(pairs * LANES, -1)[pair * LANES : (pair + 1) * LANES]
            hidden = hidden + jnp.dot(ctx_refs[pair * parts + b][...], weights, preferred_element_type=F32)

    @pl.when(step == 0)
    def _():
        own.wait()

    for b in range(1, parts):
        chunk(b, step).wait()
    here = pl.ds(pl.multiple_of(step * rows, rows), rows)
    for b in range(parts):
        weights = w_out_ref[:, part ^ b].reshape(pairs * LANES, -1)[(pairs - 1) * LANES :]
        hidden = hidden + jnp.dot(last[b, here, :], weights, preferred_element_type=F32)
    hidden_ref[...] = hidden
    unit, _ = unit_norm(hidden)
    segment = segment_ref[...]
    normed_ref[...] = (unit * (1.0 + spread(segment, scale_ref[...])) + spread(segment, shift_ref[...])).astype(BF)

    @pl.when(step == steps - 1)
    def _():
        copy = pltpu.make_async_copy(last, last_out_hbm, local)
        copy.start()
        copy.wait()


def join(ctx_blocks, last, w_out, base, base_in, segment, shift, scale, pairs, parts):
    frames, depth = base.shape
    rows = 256
    row = lambda i: (i, 0)
    wide = pl.BlockSpec((rows, depth), row)
    thin = pl.BlockSpec((rows, LANES), row)
    table = pl.BlockSpec(shift.shape, lambda i: (0, 0))
    anywhere = pl.BlockSpec(memory_space=pl.ANY)
    return pl.pallas_call(
        functools.partial(join_kernel, pairs=pairs, parts=parts),
        grid=(frames // rows,),
        in_specs=[thin] * len(ctx_blocks)
        + [anywhere, pl.BlockSpec(w_out.shape, lambda i: (0, 0, 0, 0)), wide, wide, thin]
        + [table] * 2,
        out_specs=[wide, wide, anywhere],
        out_shape=[
            jax.ShapeDtypeStruct((frames, depth), F32),
            jax.ShapeDtypeStruct((frames, depth), BF),
            jax.ShapeDtypeStruct(last.shape, BF),
        ],
        scratch_shapes=[
            pltpu.VMEM(last.shape, BF),
            pltpu.SemaphoreType.DMA,
            pltpu.SemaphoreType.DMA((2 * parts * (frames // rows),)),
        ],
        compiler_params=pltpu.CompilerParams(
            dimension_semantics=("arbitrary",), vmem_limit_bytes=40 * MIB, collective_id=5, has_side_effects=True
        ),
        cost_estimate=cost(18),
        name="join",
    )(*ctx_blocks, last, w_out, base, base_in, segment, shift, scale)


def turn_kernel(
    own_ref, gin_own_ref, gin_in_ref, out_own_ref, out_in_ref, hidden_ref, cot_ref, skips_ref, segment_ref, scale_ref,
    w_out_ref, grad_hidden_ref, low_ref, block_out_ref, sums_ref, *grad_context_refs, pairs, parts, utt,
):
    own = own_ref[0]
    hidden = hidden_ref[...]
    unit, inverse = unit_norm(hidden)
    segment = segment_ref[...]
    block_out_ref[0] = (hidden + out_own_ref[...] + out_in_ref[...].astype(F32)).astype(BF)
    block_out_ref[1] = skips_ref[...]
    grad = gin_own_ref[...] + gin_in_ref[...].astype(F32)
    grad_hidden = cot_ref[...].astype(F32) + pull_norm(unit, inverse, grad, 1.0 + spread(segment, scale_ref[...]))
    grad_hidden_ref[...] = grad_hidden
    low = grad_hidden.astype(BF)
    low_ref[...] = low
    for b in range(parts):
        part = lax.dot_general(low, w_out_ref[:, own ^ b].reshape(pairs * LANES, -1), NT, preferred_element_type=F32).astype(BF)
        for pair in range(pairs):
            grad_context_refs[pair * parts + b][...] = part[:, pair * LANES : (pair + 1) * LANES]
    sums = jnp.concatenate([collect(segment, grad, utt), collect(segment, grad * unit, utt)], axis=0)

    @pl.when(pl.program_id(0) == 0)
    def _():
        sums_ref[...] = sums

    @pl.when(pl.program_id(0) > 0)
    def _():
        sums_ref[...] += sums


def turn(own, gin_own, gin_in, out_own, out_in, hidden, cot, skips, segment, scale, w_out, pairs, parts):
    frames, depth = hidden.shape
    utt = scale.shape[0]
    rows = 256
    row = lambda i, *_: (i, 0)
    wide = pl.BlockSpec((rows, depth), row)
    thin = pl.BlockSpec((rows, LANES), row)
    shape = lambda *s: jax.ShapeDtypeStruct(*s)
    return pl.pallas_call(
        functools.partial(turn_kernel, pairs=pairs, parts=parts, utt=utt),
        grid_spec=pltpu.PrefetchScalarGridSpec(
            num_scalar_prefetch=1,
            grid=(frames // rows,),
            in_specs=[wide] * 7
            + [thin, pl.BlockSpec(scale.shape, lambda i, *_: (0, 0)), pl.BlockSpec(w_out.shape, lambda i, *_: (0, 0, 0, 0))],
            out_specs=[wide] * 2
            + [pl.BlockSpec((2, rows, depth), lambda i, *_: (0, i, 0)), pl.BlockSpec((2 * utt, depth), lambda i, *_: (0, 0))]
            + [thin] * (pairs * parts),
        ),
        out_shape=[
            shape((frames, depth), F32),
            shape((frames, depth), BF),
            shape((2, frames, depth), BF),
            shape((2 * utt, depth), F32),
        ]
        + [shape((frames, LANES), BF)] * (pairs * parts),
        compiler_params=pltpu.CompilerParams(
            dimension_semantics=("arbitrary",), vmem_limit_bytes=48 * MIB
        ),
        cost_estimate=cost(15),
        name="turn",
    )(own, gin_own, gin_in, out_own, out_in, hidden, cot, skips, segment, scale, w_out)


def out_grad_kernel(*refs, pairs, parts, columns, at_row):
    low_ref, ctx_refs, (last_ref, _, out_hbm, held, landing, local, sems) = refs[0], refs[1:-7], refs[-7:]
    d, z, core, half = mesh_spot(parts)
    part = core * half + z % half
    beside = partner_of(d, z, half, half)
    per = pairs * LANES // (2 * columns)
    greet([beside])
    if per < held.shape[3]:
        held[...] = jnp.zeros_like(held)
    low = low_ref[...]
    for b in range(parts):
        for pair in range(pairs):
            ctx = last_ref[b] if pair == pairs - 1 else ctx_refs[pair * parts + b][...]
            grad = lax.dot_general(ctx, low, TN, preferred_element_type=F32)
            for k in range(LANES // per):
                spot = pair * (LANES // per) + k
                held[spot % 2, spot // 2, part ^ b, :per, :] = grad[k * per : (k + 1) * per].astype(BF)
    remote(held.at[1 - core], landing, sems, 0, beside).wait()

    @pl.loop(0, columns)
    def _(i):
        held[core, i] = (held[core, i].astype(F32) + landing[i].astype(F32)).astype(BF)

    copies = []
    for i in range(columns):
        copy = pltpu.make_async_copy(
            held.at[core, i], out_hbm.at[i * parts : (i + 1) * parts, at_row:, :], local.at[i]
        )
        copy.start()
        copies.append(copy)
    for copy in copies:
        copy.wait()


def out_grad(low, ctx_blocks, last, grad_feed, at_row, pairs, parts, columns):
    depth = low.shape[1]
    spare = grad_feed.shape[1] - at_row
    vmem = pl.BlockSpec(memory_space=pltpu.VMEM)
    anywhere = pl.BlockSpec(memory_space=pl.ANY)
    return pl.pallas_call(
        functools.partial(out_grad_kernel, pairs=pairs, parts=parts, columns=columns, at_row=at_row),
        in_specs=[vmem] * (2 + len(ctx_blocks)) + [anywhere],
        out_specs=anywhere,
        out_shape=jax.ShapeDtypeStruct(grad_feed.shape, BF),
        scratch_shapes=[
            pltpu.VMEM((2, columns, parts, spare, depth), BF),
            pltpu.VMEM((columns, parts, spare, depth), BF),
            pltpu.SemaphoreType.DMA((columns,)),
            pltpu.SemaphoreType.DMA((2,)),
        ],
        input_output_aliases={2 + len(ctx_blocks): 0},
        compiler_params=pltpu.CompilerParams(
            collective_id=4, has_side_effects=True, vmem_limit_bytes=32 * MIB
        ),
        cost_estimate=cost(9),
        name="out_grad",
    )(low, *ctx_blocks, last, grad_feed)


class Sender:
    def __init__(self, sems, used=0):
        self.sems, self.used = sems, used
        self.d, self.z = lax.axis_index("dp"), lax.axis_index("tensor")

    def device(self, axis, bit):
        return (self.d ^ bit, self.z) if axis == "dp" else (self.d, self.z ^ bit)

    def side(self, axis, bit):
        return ((self.d if axis == "dp" else self.z) // bit) % 2

    def take(self, count):
        self.used += count
        return self.used - count

    def send(self, source, target, axis, bit):
        return remote(source, target, self.sems, self.take(1), self.device(axis, bit))


def rows_at(start, size):
    return pl.ds(pl.multiple_of(start, 16), size)


def few_rows(size):
    while size > 128:
        size //= 2
    return size


def add_rows(target, start, landing, landing_at, size):
    step = few_rows(size)

    @pl.loop(0, size // step)
    def _(i):
        here = rows_at(start + i * step, step)
        there = landing[rows_at(landing_at + i * step, step), :].astype(F32)
        target[here, :] = (target[here, :].astype(F32) + there).astype(target.dtype)


def sum_tree(sender, buffer, landing, down, turn_round, up, out, offset):
    size = buffer.shape[0] // 2
    starts, begin, kept = [0, size], [0, size], []
    for step in range(len(down[0])):
        kept.append(list(starts))
        size //= 2
        copies = []
        for side in range(2):
            axis, bit = down[side][step]
            upper = sender.side(axis, bit)
            lose = starts[side] + (1 - upper) * size
            copies.append(
                sender.send(buffer.at[rows_at(lose, size), :], landing.at[rows_at(begin[side], size), :], axis, bit)
            )
            starts[side] = starts[side] + upper * size
        yield
        for side in range(2):
            copies[side].wait()
            add_rows(buffer, starts[side], landing, begin[side], size)
            begin[side] += size
    yield from turn_round(starts, size)
    for step in reversed(range(len(down[0]))):
        copies = []
        for side in range(2):
            mine = out.at[rows_at(offset + starts[side], size), :]
            copies.append(sender.send(mine, mine, *up[side][step]))
        yield
        for side in range(2):
            copies[side].wait()
        starts = kept[step]
        size *= 2


def spread_sums(sender, own, held, out, parts):
    half = parts // 2
    slot = (sender.d // 2) * 2 + sender.z // half
    held[0] = own
    group = [("dp", 1)] + [("tensor", 1 << k) for k in range(parts.bit_length() - 2)]
    for at, (axis, bit) in enumerate(group):
        copy = sender.send(held.at[2 * at], held.at[2 * at + 1], axis, bit)
        yield
        copy.wait()
        held[2 * at + 2] = held[2 * at] + held[2 * at + 1]
    out[pl.ds(slot, 1)] = held[pl.ds(2 * len(group), 1)]
    size = 1
    rows_all = out.shape[0]
    for axis, bit in [("tensor", half)] + [("dp", 1 << k) for k in range(1, rows_all.bit_length() - 1)]:
        mine = out.at[pl.ds(slot // size * size, size)]
        copy = sender.send(mine, mine, axis, bit)
        yield
        copy.wait()
        size *= 2


def run_all(running):
    for work in list(running):
        try:
            next(work)
        except StopIteration:
            running.remove(work)


def bits_of(rows_all, parts):
    dp_bits = [1 << k for k in range(1, rows_all.bit_length() - 1)]
    return dp_bits, [1 << k for k in reversed(range(parts.bit_length() - 1))]


def finish_kernel(*refs, pairs, parts, utt, rows_all):
    cut = (pairs - 1) * parts
    prev_hbm, refs = refs[:cut], refs[cut:]
    own_hbm, refs = refs[:pairs], refs[pairs:]
    (
        normed_hbm, weight_hbm, base_hbm, base_in_hbm, grad_hbm, inputs_hbm, segment_ref, scale_ref,
        grad_base_ref, qkv_ref, sums_ref, inputs_in_hbm,
        prev, own, normed, weight, base, grad_hidden, arrived, total, qkv_held, qkv_in, loads, sems,
    ) = refs
    d, z, core, half = mesh_spot(parts)
    part = core * half + z % half
    stays = z // half == core
    frames = normed.shape[1]
    width = pairs * LANES

    there = ((d - core) + z // half, core * half + z % half)
    dp_bits, _ = bits_of(rows_all, parts)
    near = [partner_of(d, z, b, half) for b in range(1, parts)] + [(d, z ^ half)] + [(d ^ bit, z) for bit in dp_bits]
    barrier = pltpu.get_barrier_semaphore()
    for device in near:
        pl.semaphore_signal(barrier, inc=1, device_id=device, device_id_type=pl.DeviceIdType.MESH)

    @pl.when(jnp.logical_not(stays))
    def _():
        pl.semaphore_signal(barrier, inc=1, device_id=there, device_id_type=pl.DeviceIdType.MESH)
        pl.semaphore_wait(barrier, len(near) + 1)

    @pl.when(stays)
    def _():
        pl.semaphore_wait(barrier, len(near))

    sends = []
    order = [b for b in range(1, parts) if b % half] + [b for b in range(1, parts) if b % half == 0]
    for b in order:
        sends.append(
            (b, remote(own_hbm[-1].at[b], arrived.at[b - 1], sems, b - 1, partner_of(d, z, b, half)))
        )

    @pl.when(jnp.logical_not(stays))
    def _():
        for copy in in_pieces(inputs_hbm, inputs_in_hbm, sems, parts, there):
            copy.start()

    def load(at, source, target):
        copy = pltpu.make_async_copy(source, target, loads.at[at])
        copy.start()
        return copy

    first = [load(0, normed_hbm, normed)]
    for pair in range(pairs):
        first.append(load(1 + pair, own_hbm[pair], own.at[pair]))
    at = 1 + pairs
    four = pl.ds(core * 4, 4)
    second = [
        load(at, weight_hbm.at[four], weight.at[four]),
        remote(weight_hbm.at[four], weight.at[four], sems, parts - 1, (d ^ 1, z)),
    ]
    for k in range(cut):
        second.append(load(at + 1 + k, prev_hbm[k], prev.at[k]))
    at += 1 + cut
    third = [load(at, grad_hbm, grad_hidden)]

    @pl.when(stays)
    def _():
        pltpu.make_async_copy(base_hbm, base, loads.at[at + 1]).start()

    @pl.when(jnp.logical_not(stays))
    def _():
        pltpu.make_async_copy(base_in_hbm, base, loads.at[at + 1]).start()

    for copy in first:
        copy.wait()
    for kind in range(3):
        for pair in range(pairs):

            def gather(b, carry):
                return carry + lax.dot_general(own[pair, b, kind], normed[b], TN, preferred_element_type=F32)

            grad = lax.fori_loop(0, parts, gather, jnp.zeros((LANES, normed.shape[2]), F32)).astype(BF)
            wide = qkv_held.shape[1]
            for k in range(normed.shape[2] // wide):
                at_row = k * 3 * width + kind * width + pair * LANES
                qkv_held[at_row : at_row + LANES, :] = grad[:, k * wide : (k + 1) * wide]

    sender = Sender(sems, parts + PIECES)
    down = [
        [("dp", bit) for bit in dp_bits] + [("tensor", half)],
        [("dp", bit) for bit in reversed(dp_bits)] + [("tensor", half)],
    ]

    def go_home(starts, size):
        at_sem = sender.take(2)

        def copies():
            return [
                remote_copy(
                    qkv_held.at[rows_at(starts[side], size), :],
                    qkv_ref.at[rows_at(starts[side], size), :],
                    sems,
                    at_sem + side,
                    there,
                )
                for side in range(2)
            ]

        @pl.when(stays)
        def _():
            for side in range(2):
                here = rows_at(starts[side], size)
                qkv_ref[here, :] = qkv_held[here, :]

        @pl.when(jnp.logical_not(stays))
        def _():
            for copy in copies():
                copy.start()

        yield

        @pl.when(jnp.logical_not(stays))
        def _():
            for copy in copies():
                copy.wait()

        for side in range(2):
            starts[side] = starts[side] + (core - z // half) * size

    up = [line[:-1] + [("dp", 1)] for line in down]
    running = [sum_tree(sender, qkv_held, qkv_in, down, go_home, up, qkv_ref, 0)]
    run_all(running)

    for copy in second:
        copy.wait()
    rows = 256

    def add_block(source, b, pair, fresh):
        weights = jnp.concatenate(
            [weight[:, part ^ b, kind * pairs + pair].reshape(LANES, -1) for kind in range(3)],
            axis=0,
        )

        @pl.loop(0, frames // rows)
        def _(i):
            here = pl.ds(pl.multiple_of(i * rows, rows), rows)
            block = jnp.concatenate([source[kind, here, :] for kind in range(3)], axis=1)
            term = jnp.dot(block, weights, preferred_element_type=F32)
            if fresh:
                total[here, :] = term
            else:
                total[here, :] += term

    add_block(own.at[pairs - 1, 0], 0, pairs - 1, True)
    run_all(running)
    for pair in range(pairs - 1):
        for b in range(parts):
            add_block(prev.at[pair * parts + b], b, pair, False)
            if b % 2:
                run_all(running)
    for b, copy in sorted(sends, key=lambda item: (item[0] % half, item[0])):
        copy.wait()
        add_block(arrived.at[b - 1], b, pairs - 1, False)
        run_all(running)

    for copy in third:
        copy.wait()
    pltpu.make_async_copy(base_hbm, base, loads.at[at + 1]).wait()
    sums_ref[...] = jnp.zeros_like(sums_ref)

    @pl.loop(0, frames // rows)
    def _(i):
        here = pl.ds(pl.multiple_of(i * rows, rows), rows)
        unit, inverse = unit_norm(base[here, :].astype(F32))
        grad = total[here, :]
        segment = segment_ref[here, :]
        pulled = pull_norm(unit, inverse, grad, 1.0 + spread(segment, scale_ref[...]))
        grad_base_ref[here, :] = (grad_hidden[here, :] + pulled).astype(BF)
        sums_ref[...] += jnp.concatenate([collect(segment, grad, utt), collect(segment, grad * unit, utt)], axis=0)

    while running:
        run_all(running)

    @pl.when(jnp.logical_not(stays))
    def _():
        for copy in in_pieces(inputs_hbm, inputs_in_hbm, sems, parts, there):
            copy.wait()


def finish(
    prev, own, normed_all, weight, base, base_in, grad_hidden, inputs, segment, scale, pairs, parts, rows_all
):
    frames, depth = base.shape
    utt = scale.shape[0]
    units = 3 * pairs * LANES
    wide = depth
    while units * depth // wide % (16 * rows_all * 2):
        wide //= 2
    qkv_shape = (units * depth // wide, wide)
    copies = parts + 2 + PIECES + 5 * rows_all.bit_length() + parts.bit_length()
    anywhere = pl.BlockSpec(memory_space=pl.ANY)
    vmem = pl.BlockSpec(memory_space=pltpu.VMEM)
    shape = lambda *s: jax.ShapeDtypeStruct(*s)
    block = (3, frames, LANES)
    return pl.pallas_call(
        functools.partial(finish_kernel, pairs=pairs, parts=parts, utt=utt, rows_all=rows_all),
        in_specs=[anywhere] * (len(prev) + pairs + 6) + [vmem] * 2,
        out_specs=[vmem] * 3 + [anywhere],
        out_shape=[
            shape((frames, depth), BF),
            shape(qkv_shape, BF),
            shape((2 * utt, depth), F32),
            shape((frames, depth), BF),
        ],
        scratch_shapes=[
            pltpu.VMEM((max(len(prev), 1),) + block, BF),
            pltpu.VMEM((pairs, parts) + block, BF),
            pltpu.VMEM(normed_all.shape, BF),
            pltpu.VMEM(weight.shape, BF),
            pltpu.VMEM((frames, depth), BF),
            pltpu.VMEM((frames, depth), F32),
            pltpu.VMEM((parts - 1,) + block, BF),
            pltpu.VMEM((frames, depth), F32),
            pltpu.VMEM(qkv_shape, BF),
            pltpu.VMEM(qkv_shape, BF),
            pltpu.SemaphoreType.DMA((4 + pairs + len(prev),)),
            pltpu.SemaphoreType.DMA((2 * copies,)),
        ],
        compiler_params=pltpu.CompilerParams(
            collective_id=1, has_side_effects=True, vmem_limit_bytes=56 * MIB
        ),
        cost_estimate=cost(60),
        name="finish",
    )(*prev, *own, normed_all, weight, base, base_in, grad_hidden, inputs, segment, scale)


def sums_kernel(
    inputs_hbm, inputs_in_hbm, skips_hbm, skips_in_hbm, grad_ref, sums_ref, skip_out_ref, sums_out_ref, grad_in_hbm,
    frames_in, away, held, first_in, half_in, sums_in, loads, sems, *, rows_all, parts,
):
    d, z, core, half = mesh_spot(parts)
    stays = z // half == core
    leaves = jnp.logical_not(stays)
    dp_bits, z_bits = bits_of(rows_all, parts)
    there = ((d - core) + z // half, core * half + z % half)
    depth = grad_ref.shape[1]
    half_rows, width = held.shape

    for at, (source, source_in) in enumerate(((inputs_hbm, inputs_in_hbm), (skips_hbm, skips_in_hbm))):
        slot = frames_in.at[1 - core if at == 0 else core]

        @pl.when(stays)
        def _():
            pltpu.make_async_copy(source, slot, loads.at[at]).start()

        @pl.when(leaves)
        def _():
            pltpu.make_async_copy(source_in, slot, loads.at[at]).start()

    sender = Sender(sems, PIECES)
    near = [("dp", 1)] + [("dp", bit) for bit in dp_bits] + [("tensor", bit) for bit in z_bits]
    barrier = pltpu.get_barrier_semaphore()
    for axis, bit in near:
        pl.semaphore_signal(
            barrier, inc=1, device_id=sender.device(axis, bit), device_id_type=pl.DeviceIdType.MESH
        )

    @pl.when(leaves)
    def _():
        pl.semaphore_signal(barrier, inc=1, device_id=there, device_id_type=pl.DeviceIdType.MESH)
        pl.semaphore_wait(barrier, len(near) + 1)

    @pl.when(stays)
    def _():
        pl.semaphore_wait(barrier, len(near))

    def start_move(k):
        @pl.when(leaves)
        def _():
            in_pieces(grad_ref, grad_in_hbm, sems, 0, there, [k])[0].start()

    def settle(starts, size):
        for side in range(2):
            skip_out_ref[rows_at(offset + starts[side], size), :] = held[rows_at(starts[side], size), :]
        yield

    offset = core * half_rows

    def skips():
        for slot in range(2):
            pltpu.make_async_copy(inputs_hbm, frames_in.at[slot], loads.at[slot]).wait()
        for slot, target in ((0, away), (1, held)):

            @pl.loop(0, depth // 256)
            def _(i):
                cut = frames_in[slot, :, pl.ds(pl.multiple_of(i * 256, 256), 256)]
                grad = lax.dot_general(cut, grad_ref[...], TN, preferred_element_type=F32).astype(BF)
                for k in range(depth // width):
                    target[rows_at(k * depth + i * 256, 256), :] = grad[:, k * width : (k + 1) * width]

            if slot == 0:
                copy = sender.send(away, first_in, "dp", 1)
                yield
        copy.wait()
        add_rows(held, 0, first_in, 0, half_rows)
        down = [
            [("dp", bit) for bit in dp_bits] + [("tensor", bit) for bit in z_bits],
            [("dp", bit) for bit in reversed(dp_bits)] + [("tensor", bit) for bit in z_bits],
        ]
        yield from sum_tree(sender, held, half_in, down, settle, down, skip_out_ref, offset)
        mine = skip_out_ref.at[rows_at(offset, half_rows), :]
        copy = sender.send(mine, mine, "dp", 1)
        yield
        copy.wait()

    running = [skips(), spread_sums(sender, sums_ref[...], sums_in, sums_out_ref, parts)]
    rounds = 0
    later = 1 + len(dp_bits) + 2 * len(z_bits) + 1
    while running:
        if rounds in (0, 1, later, later + 1):
            start_move(rounds if rounds < 2 else rounds - later + 2)
        rounds += 1
        run_all(running)

    @pl.when(leaves)
    def _():
        for copy in in_pieces(grad_ref, grad_in_hbm, sems, 0, there):
            copy.wait()


def sums(inputs, inputs_in, skips, skips_in, grad_base, utterance_sums, rows_all, parts):
    frames, depth = inputs.shape
    devices = rows_all * parts
    width = min(depth, depth * depth // (16 * devices))
    half_rows = depth * depth // width
    stages = rows_all.bit_length() + parts.bit_length() - 3
    copies = PIECES + 2 + 4 * stages + rows_all.bit_length() + parts.bit_length()
    vmem = pl.BlockSpec(memory_space=pltpu.VMEM)
    anywhere = pl.BlockSpec(memory_space=pl.ANY)
    shape = lambda *s: jax.ShapeDtypeStruct(*s)
    skip_sum, all_sums, grad_base_in = pl.pallas_call(
        functools.partial(sums_kernel, rows_all=rows_all, parts=parts),
        in_specs=[anywhere] * 4 + [vmem] * 2,
        out_specs=[vmem] * 2 + [anywhere],
        out_shape=[
            shape((2 * half_rows, width), BF),
            shape((rows_all,) + utterance_sums.shape, F32),
            shape((frames, depth), BF),
        ],
        scratch_shapes=[pltpu.VMEM((2, frames, depth), BF)]
        + [pltpu.VMEM((half_rows, width), BF)] * 4
        + [
            pltpu.VMEM((2 * parts.bit_length() - 1,) + utterance_sums.shape, F32),
            pltpu.SemaphoreType.DMA((2,)),
            pltpu.SemaphoreType.DMA((2 * copies,)),
        ],
        compiler_params=pltpu.CompilerParams(
            collective_id=0, has_side_effects=True, vmem_limit_bytes=56 * MIB
        ),
        cost_estimate=cost(100),
        name="sums",
    )(inputs, inputs_in, skips, skips_in, grad_base, utterance_sums)
    skip_sum = skip_sum.reshape(2, depth // width, depth, width)
    skip_sum = jnp.transpose(skip_sum, (0, 2, 1, 3)).reshape(2, depth, depth)
    return skip_sum, all_sums, grad_base_in


def front_kernel(
    ends_ref, inputs_ref, skips_ref, w_in_ref, w_res_ref, segment_ref, shift_ref, scale_ref, rate_ref, weight_hbm, w_out_ref,
    base_ref, out_ref, cos_ref, sin_ref, qmark_ref, kmark_ref, weight_in_hbm, w_out_all_ref, away, local, sems,
    *, parts, utt,
):
    d, z, core, half = mesh_spot(parts)
    stays = z // half == core
    leaves = jnp.logical_not(stays)
    there = ((d - core) + z // half, core * half + z % half)
    frames = base_ref.shape[0]
    rows = 256
    chunks = frames // rows

    barrier = pltpu.get_barrier_semaphore()
    near = [partner_of(d, z, b, half) for b in range(1, half + 1)] + [(d ^ bit, z) for bit in (2, 4, 6)]
    near += [(d, z ^ k) for k in range(half, parts)]
    for device in near:
        pl.semaphore_signal(barrier, inc=1, device_id=device, device_id_type=pl.DeviceIdType.MESH)

    @pl.when(leaves)
    def _():
        pl.semaphore_signal(barrier, inc=1, device_id=there, device_id_type=pl.DeviceIdType.MESH)
        pl.semaphore_wait(barrier, len(near) + 1)

    @pl.when(stays)
    def _():
        pl.semaphore_wait(barrier, len(near))

    def here(k):
        return pl.ds(pl.multiple_of(k * rows, rows), rows)

    def copy(kind, k, source, target, device):
        at = kind * chunks + k
        return pltpu.make_async_remote_copy(
            src_ref=source,
            dst_ref=target,
            send_sem=sems.at[2 * at],
            recv_sem=sems.at[2 * at + 1],
            device_id=device,
            device_id_type=pl.DeviceIdType.MESH,
        )

    def moving(k):
        return copy(0, k, away.at[here(k), :], out_ref.at[0, here(k), :], there)

    quarter = weight_hbm.shape[0] // 4
    column = d // 2 % 4

    def weight_part(k):
        cut = pl.ds(pl.multiple_of((column ^ k) * quarter, 16), quarter)
        if k == 0:
            return copy(parts, 0, weight_hbm.at[cut, :], weight_in_hbm.at[cut, :], there)
        own = pl.ds(pl.multiple_of(column * quarter, 16), quarter)
        return copy(parts, k, weight_in_hbm.at[own, :], weight_in_hbm.at[own, :], (d ^ (2 * k), z))

    @pl.when(leaves)
    def _():
        weight_part(0).start()

    @pl.when(stays)
    def _():
        pltpu.make_async_copy(weight_hbm, weight_in_hbm, local).start()

    eighth = d // 2 % 4 + 4 * core
    per = w_out_all_ref.shape[2]
    w_out_all_ref[eighth, z] = w_out_ref[pl.ds(pl.multiple_of(eighth * per, 16), per), :]

    def w_out_part(k):
        if k < parts:
            cut = w_out_all_ref.at[eighth, z]
            return copy(parts, 3 + k, cut, cut, (d, z ^ k))
        size = 1 << (k - parts)
        cut = w_out_all_ref.at[pl.ds(eighth // size * size, size)]
        return copy(parts, 3 + k, cut, cut, (d ^ (2, 4, 1)[k - parts], z))

    for k in range(1, parts):
        w_out_part(k).start()

    def across(b, k):
        return copy(b, k, out_ref.at[0, here(k), :], out_ref.at[b, here(k), :], partner_of(d, z, b, half))

    def beside(b, k):
        return copy(
            half + b, k, out_ref.at[b, here(k), :], out_ref.at[half + b, here(k), :], partner_of(d, z, half, half)
        )

    def spread_own(k):
        for b in range(1, half):
            across(b, k).start()
        beside(0, k).start()

    @pl.loop(0, chunks)
    def _(k):
        at = here(k)
        base = jnp.dot(inputs_ref[at, :], w_in_ref[...], preferred_element_type=F32)
        base = base + jnp.dot(skips_ref[at, :], w_res_ref[...], preferred_element_type=F32)
        base_ref[at, :] = base.astype(BF)
        unit, _ = unit_norm(base)
        segment = segment_ref[at, :]
        normed = (unit * (1.0 + spread(segment, scale_ref[...])) + spread(segment, shift_ref[...])).astype(BF)

        @pl.when(stays)
        def _():
            out_ref[0, at, :] = normed
            spread_own(k)

        @pl.when(leaves)
        def _():
            away[at, :] = normed
            moving(k).start()

    part = core * half + z % half

    @pl.loop(0, parts * chunks)
    def _(i):
        at = here(i)
        place = (part ^ (i // chunks)) * frames + (i % chunks) * rows
        place = place + lax.broadcasted_iota(jnp.int32, (rows, LANES), 0)
        lane = lax.broadcasted_iota(jnp.int32, (rows, LANES), 1)
        segment = jnp.zeros((rows, LANES), jnp.int32)
        start = jnp.zeros((rows, LANES), jnp.int32)
        for u in range(utt - 1):
            past = place >= ends_ref[u]
            segment = jnp.where(past, u + 1, segment)
            start = jnp.where(past, ends_ref[u], start)
        angle = (place - start).astype(F32) * rate_ref[0:1, :]
        cos_ref[at, :] = jnp.cos(angle)
        sin_ref[at, :] = jnp.sin(angle) * rate_ref[1:2, :]
        other = jnp.logical_and(lane < utt, lane != segment)
        qmark_ref[at, :] = jnp.where(other, MASKED, 0.0).astype(BF)
        shown = jnp.where(lane < utt + 3, 1.0, 0.0)
        kmark_ref[at, :] = jnp.where(other, 0.0, shown).astype(BF)

    for k in range(1, parts):
        w_out_part(k).wait()
    w_out_part(parts).start()

    @pl.when(leaves)
    def _():
        weight_part(0).wait()
        for k in range(1, 4):
            weight_part(k).start()

        @pl.loop(0, chunks)
        def _(k):
            moving(k).wait_recv()
            spread_own(k)

    w_out_part(parts).wait()
    w_out_part(parts + 1).start()

    @pl.loop(0, chunks)
    def _(k):
        for b in range(1, half):
            across(b, k).wait_recv()
            beside(b, k).start()

    w_out_part(parts + 1).wait()
    w_out_part(parts + 2).start()

    @pl.loop(0, chunks)
    def _(k):
        for b in range(half):
            beside(b, k).wait_recv()
            beside(b, k).wait_send()
        for b in range(1, half):
            across(b, k).wait_send()

    @pl.when(leaves)
    def _():
        @pl.loop(0, chunks)
        def _(k):
            moving(k).wait_send()

        for k in range(1, 4):
            weight_part(k).wait()

    @pl.when(stays)
    def _():
        pltpu.make_async_copy(weight_hbm, weight_in_hbm, local).wait()

    w_out_part(parts + 2).wait()


def front(ends, inputs, skips, w_in, w_res, segment, shift, scale, rate, weight, w_out, parts):
    frames, depth = inputs.shape
    utt = ends.shape[0]
    vmem = pl.BlockSpec(memory_space=pltpu.VMEM)
    return pl.pallas_call(
        functools.partial(front_kernel, parts=parts, utt=utt),
        in_specs=[pl.BlockSpec(memory_space=pltpu.SMEM)] + [vmem] * 8 + [pl.BlockSpec(memory_space=pl.ANY), vmem],
        out_specs=[vmem] * 6 + [pl.BlockSpec(memory_space=pl.ANY), vmem],
        out_shape=[
            jax.ShapeDtypeStruct((frames, depth), BF),
            jax.ShapeDtypeStruct((parts, frames, depth), BF),
            jax.ShapeDtypeStruct((parts * frames, LANES), F32),
            jax.ShapeDtypeStruct((parts * frames, LANES), F32),
            jax.ShapeDtypeStruct((parts * frames, LANES), BF),
            jax.ShapeDtypeStruct((parts * frames, LANES), BF),
            jax.ShapeDtypeStruct(weight.shape, BF),
            jax.ShapeDtypeStruct((8, parts, w_out.shape[0] // 8, depth), BF),
        ],
        scratch_shapes=[
            pltpu.VMEM((frames, depth), BF),
            pltpu.SemaphoreType.DMA,
            pltpu.SemaphoreType.DMA((2 * (parts * (frames // 256) + 6 + parts),)),
        ],
        compiler_params=pltpu.CompilerParams(
            collective_id=2, has_side_effects=True, vmem_limit_bytes=48 * MIB
        ),
        cost_estimate=cost(75),
        name="front",
    )(ends, inputs, skips, w_in, w_res, segment, shift, scale, rate, weight, w_out)


def dot(a, b, dims=(((1,), (0,)), ((), ()))):
    return lax.dot_general(a, b, dims, preferred_element_type=F32)


def after(value, token):
    return lax.optimization_barrier((value, token))[0]


def on_device(
    inputs, skip_input, lengths, time_steps, w_skip_in, w_skip_res, w_ada, w_qkv, w_out, w_up, w_down, cotangent
):
    parts = lax.axis_size("tensor")
    rows_all = lax.axis_size("dp")
    half = parts // 2
    columns = rows_all // 2
    d = lax.axis_index("dp")
    z = lax.axis_index("tensor")
    core, column = d % 2, d // 2
    stays = z // half == core
    part = core * half + z % half
    inputs, skip_input, cotangent = inputs[0], skip_input[0], cotangent[0]
    frames, depth = inputs.shape
    length = frames * parts
    ws = w_qkv.shape[2]
    pairs = ws // LANES
    utt = lengths.shape[1]
    both = ("dp", "tensor")

    def moved(value):
        pattern = [
            (i * parts + j, ((i // 2) * 2 + j // half) * parts + (i % 2) * half + j % half)
            for i in range(rows_all)
            for j in range(parts)
            if i % 2 != j // half
        ]
        return lax.ppermute(value, both, pattern)

    def partner(value, b):
        pattern = [
            (i * parts + j, (i ^ (b // half)) * parts + (j // half) * half + ((j % half) ^ (b % half)))
            for i in range(rows_all)
            for j in range(parts)
        ]
        return lax.ppermute(value, both, pattern)

    def exchange(blocks):
        return [blocks[0]] + [partner(blocks[b], b) for b in range(1, parts)]

    same_core = [[2 * i + k for i in range(columns)] for k in range(2)]

    other_lengths = partner(lengths, half)
    other_steps = partner(time_steps, half)
    lengths_work = jnp.where(stays, lengths, other_lengths)[0]
    steps_work = jnp.where(stays, time_steps, other_steps)[0]

    time_rate = jnp.exp(
        -math.log(10000.0) * (jnp.arange(w_ada.shape[0] // 2, dtype=F32) / (w_ada.shape[0] // 2))
    )

    def embed(steps):
        phases = steps.astype(F32)[:, None] * time_rate
        return jax.nn.silu(jnp.concatenate([jnp.sin(phases), jnp.cos(phases)], axis=-1)).astype(BF)

    def wide_segment(row_lengths, places):
        segment, _, _ = frame_marks(row_lengths, places, utt)
        return jnp.broadcast_to(segment[:, None], (places.shape[0], LANES))

    spot = jnp.arange(frames, dtype=jnp.int32)
    mods_home = dot(embed(time_steps[0]), w_ada[:, : 2 * depth])
    qkv_rows = jnp.transpose(w_qkv, (0, 2, 1)).reshape(3 * ws, depth)
    rotary_rate = jnp.exp(-math.log(10000.0) * (2.0 * jnp.arange(HEAD_DIM // 2, dtype=F32) / HEAD_DIM))
    sign = jnp.where(jnp.arange(LANES) % HEAD_DIM < HEAD_DIM // 2, -1.0, 1.0).astype(F32)
    base_home, normed_all, cosine, sine, qmark, kmark, w_mine, w_out_all = front(
        jnp.cumsum(lengths_work, dtype=jnp.int32),
        inputs,
        skip_input,
        w_skip_in,
        w_skip_res,
        wide_segment(lengths[0], z * frames + spot),
        mods_home[:, :depth],
        mods_home[:, depth:],
        jnp.stack([jnp.tile(rotary_rate, 4), sign]),
        qkv_rows,
        w_out,
        parts,
    )

    per_q, per_o = 3 * ws // rows_all, ws // rows_all
    units = w_down.shape[0]
    per_u = units // rows_all
    slice_feed = jnp.concatenate(
        [
            jnp.transpose(lax.dynamic_slice_in_dim(w_up, d * per_u, per_u, 1)),
            lax.dynamic_slice_in_dim(w_down, d * per_u, per_u, 0),
        ]
    )
    feed_rows = lax.all_gather(slice_feed, "tensor")
    feed_rows = lax.all_gather(after(feed_rows, base_home), "dp", axis_index_groups=same_core)
    feed_rows = feed_rows.reshape(columns * parts, 2, per_u, depth)

    cotangent = after(cotangent, base_home)
    cot = jnp.where(stays, cotangent, moved(cotangent))
    base_in = moved(after(base_home, cot))

    silu_work = embed(steps_work)
    mods = dot(silu_work, w_ada)
    shift_one, scale_one, shift_two, scale_two = [mods[:, k * depth : (k + 1) * depth] for k in range(4)]
    segment_here = wide_segment(lengths_work, part * frames + spot)

    qkv = project(normed_all.reshape(length, depth), w_mine, cosine, sine, pairs)

    def ranges(size, other):
        per = frames // size
        stored = jnp.arange(length // size, dtype=jnp.int32)
        natural = (part ^ (stored // per)) * per + stored % per
        return block_ranges(lengths_work, natural, size, other)

    own = jnp.stack([part.astype(jnp.int32), stays.astype(jnp.int32)])
    wide = min(frames, 1024)
    low, high = ranges(wide, wide)
    bq, bk = 512, 512
    low_back, high_back = ranges(bk, bq)
    ctx_pairs, lse_pairs, ctx_mine = [], [], []
    for pair in range(pairs):
        ctx, lse = attend(
            after(qkv, cot) if pair == pairs - 1 else qkv, pair, qmark, kmark, own, low, high, wide, wide, frames
        )
        ctx_pairs.append(ctx)
        lse_pairs.append(lse)
        if pair < pairs - 1:
            ctx_mine += exchange([ctx[b] for b in range(parts)])
    hidden, ffn_in, ctx_last = join(
        ctx_mine, ctx_pairs[-1], w_out_all, base_home, base_in, segment_here, shift_two, scale_two, pairs, parts
    )

    cot_other = partner(cot, half)
    spare = max(per_o, 16)
    heads = qkv_rows.reshape(3 * pairs, 8, LANES // 8, depth)
    out_own, out_send, gin_own, gin_send, grad_feed, w_heads = feed(
        ffn_in, cot, cot_other, feed_rows, heads, spare, parts
    )
    grad_hidden, low_grad, block_out, sums_two, *grad_context = turn(
        own, gin_own, partner(gin_send, half), out_own, partner(out_send, half), hidden, cot, skip_input, segment_here,
        scale_two,
        w_out_all, pairs, parts,
    )

    grad_feed = out_grad(low_grad, ctx_mine, ctx_last, grad_feed, 2 * per_u, pairs, parts, columns)
    grad_feed = grad_feed.reshape(columns, parts, 2 * per_u + spare, depth)
    feed_sum = lax.psum_scatter(grad_feed, "dp", scatter_dimension=0, axis_index_groups=same_core)
    grad_feed = lax.psum_scatter(feed_sum, "tensor", scatter_dimension=0)
    feed_shard = grad_feed
    grad_feed = lax.all_gather(grad_feed, "dp")
    grad_up = jnp.transpose(grad_feed[:, :per_u].reshape(units, depth)).astype(F32)
    grad_down = grad_feed[:, per_u : 2 * per_u].reshape(units, depth).astype(F32)
    grad_out = grad_feed[:, 2 * per_u : 2 * per_u + per_o].reshape(ws, depth).astype(F32)

    grad_mine = []
    for pair in range(pairs):
        grad = jnp.stack(exchange(grad_context[pair * parts : (pair + 1) * parts]))
        if pair == pairs - 1 and pairs > 1:
            grad = after(grad, feed_sum)
        grads = attend_back(
            qkv, pair, grad, ctx_pairs[pair], lse_pairs[pair], qmark, kmark, cosine, sine, own,
            low_back, high_back, bq, bk, utt, frames,
        )
        grad_mine.append(grads)

    returned = []
    for grads in grad_mine[:-1]:
        returned += exchange([grads[b] for b in range(parts)])
    block_out_in, skips_in = moved(block_out)
    grad_base, grad_qkv, sums_one, inputs_in = finish(
        returned, after(grad_mine, feed_shard), normed_all, w_heads, base_home, base_in, grad_hidden, inputs, segment_here, scale_one,
        pairs, parts, rows_all,
    )
    silu_rows = jnp.pad(silu_work.astype(F32) * (1.0 / parts), ((0, 0), (0, depth - silu_work.shape[1])))
    skip_sum, all_sums, grad_base_in = sums(
        inputs, inputs_in, skip_input, skips_in, grad_base, jnp.concatenate([sums_one, sums_two, silu_rows]),
        rows_all, parts,
    )
    grad_qkv = grad_qkv.reshape(-1, 3, ws, grad_qkv.shape[1])
    grad_qkv = jnp.transpose(grad_qkv, (1, 0, 3, 2)).reshape(3, depth, ws).astype(F32)
    grad_skip = skip_sum.astype(F32)
    grad_base_home = jnp.where(stays, grad_base, grad_base_in)
    grad_inputs = dot(grad_base_home, w_skip_in, NT)
    grad_skips = dot(grad_base_home, w_skip_res, NT)
    block_out = jnp.where(stays, block_out[0], block_out_in).astype(F32)

    all_sums = all_sums.reshape(rows_all, 5, utt, depth)
    silu_all = all_sums[:, 4, :, : w_ada.shape[0]].reshape(rows_all * utt, w_ada.shape[0])
    all_sums = jnp.concatenate([all_sums[:, k] for k in range(4)], axis=-1).reshape(rows_all * utt, 4 * depth)
    grad_ada = jnp.einsum("ut,um->tm", silu_all, all_sums, precision=lax.Precision.HIGHEST)

    return (
        block_out[None],
        grad_inputs[None],
        grad_skips[None],
        grad_skip[0],
        grad_skip[1],
        grad_ada,
        grad_qkv,
        grad_out,
        grad_up,
        grad_down,
    )


def solution(mesh):
    placed = (
        P("dp", "tensor", None),
        P("dp", "tensor", None),
        P("dp", None),
        P("dp", None),
        P(),
        P(),
        P(),
        P(None, None, "tensor"),
        P("tensor", None),
        P(None, "tensor"),
        P("tensor", None),
        P("dp", "tensor", None),
    )
    return jax.shard_map(
        on_device,
        mesh=mesh,
        in_specs=placed,
        out_specs=(
            P("dp", "tensor", None),
            P("dp", "tensor", None),
            P("dp", "tensor", None),
            P(),
            P(),
            P(),
            P(None, None, "tensor"),
            P("tensor", None),
            P(None, "tensor"),
            P("tensor", None),
        ),
        check_vma=False,
    )
```

```python
import functools
import math

import jax
import jax.numpy as jnp
from jax import lax
from jax.experimental import pallas as pl
from jax.experimental.pallas import tpu as pltpu
from jax.sharding import PartitionSpec as P

HEAD_DIM = 64
LANES = 128
MASKED = -1e30
LOG2E = math.log2(math.e)
MIB = 2**20
BF = jnp.bfloat16
F32 = jnp.float32
norm_epsilon = 1e-06
NT = (((1,), (1,)), ((), ()))
TN = (((0,), (0,)), ((), ()))


def cost(microseconds):
    return pl.CostEstimate(flops=int(microseconds * 1.1e9), bytes_accessed=0, transcendentals=0)


def stored_block(block, own, per_part):
    shift = per_part.bit_length() - 1
    part = lax.shift_right_logical(block, shift)
    return ((part ^ own) << shift) | (block & (per_part - 1))


def swap_halves(values):
    lane = lax.broadcasted_iota(jnp.int32, values.shape, 1)
    return jnp.where(lane % 64 < 32, pltpu.roll(values, 96, 1), pltpu.roll(values, 32, 1))


def mesh_spot(parts):
    d = lax.axis_index("dp")
    z = lax.axis_index("tensor")
    return d, z, d % 2, parts // 2


def partner_of(d, z, b, half):
    return d ^ (b // half), z ^ (b % half)


def remote_copy(source, target, sems, at, device):
    return pltpu.make_async_remote_copy(
        src_ref=source,
        dst_ref=target,
        send_sem=sems.at[2 * at],
        recv_sem=sems.at[2 * at + 1],
        device_id=device,
        device_id_type=pl.DeviceIdType.MESH,
    )


PIECES = 4


def in_pieces(source, target, sems, at, device, pieces=range(PIECES)):
    rows = source.shape[0] // PIECES
    return [
        remote_copy(
            source.at[k * rows : (k + 1) * rows, :], target.at[k * rows : (k + 1) * rows, :], sems, at + k, device
        )
        for k in pieces
    ]


def remote(source, target, sems, at, device):
    copy = remote_copy(source, target, sems, at, device)
    copy.start()
    return copy


def greet(devices):
    barrier = pltpu.get_barrier_semaphore()
    for device in devices:
        pl.semaphore_signal(barrier, inc=1, device_id=device, device_id_type=pl.DeviceIdType.MESH)
    pl.semaphore_wait(barrier, len(devices))


def project_kernel(normed_ref, weight_ref, cos_ref, sin_ref, out_ref, *, pairs):
    normed = normed_ref[...]
    cosine = cos_ref[...]
    sine = sin_ref[...]
    width = pairs * LANES
    for kind in range(3):
        weight = weight_ref[kind * width : (kind + 1) * width, :]
        part = lax.dot_general(normed, weight, NT, preferred_element_type=F32)
        for pair in range(pairs):
            cut = part[:, pair * LANES : (pair + 1) * LANES]
            if kind < 2:
                cut = cut * cosine + swap_halves(cut) * sine
            if kind == 0:
                cut = cut * (LOG2E * HEAD_DIM**-0.5)
            out_ref[pair * 3 + kind] = cut.astype(BF)


def project(normed_all, weight, cosine, sine, pairs):
    length, depth = normed_all.shape
    rows = 512
    return pl.pallas_call(
        functools.partial(project_kernel, pairs=pairs),
        grid=(length // rows,),
        in_specs=[
            pl.BlockSpec((rows, depth), lambda i: (i, 0)),
            pl.BlockSpec(weight.shape, lambda i: (0, 0)),
            pl.BlockSpec((rows, LANES), lambda i: (i, 0)),
            pl.BlockSpec((rows, LANES), lambda i: (i, 0)),
        ],
        out_specs=pl.BlockSpec((3 * pairs, rows, LANES), lambda i: (0, i, 0)),
        out_shape=jax.ShapeDtypeStruct((3 * pairs, length, LANES), BF),
        compiler_params=pltpu.CompilerParams(vmem_limit_bytes=40 * MIB),
        cost_estimate=cost(11),
        name="project",
    )(normed_all, weight, cosine, sine)


def attend_kernel(
    own_ref, low_ref, high_ref, q_ref, k_ref, v_ref, qmark_ref, kmark_ref, ctx_ref, lse_ref, keys, vals,
    *, bq, bk, per_part,
):
    step = pl.program_id(0)
    length = kmark_ref.shape[0]
    own = own_ref[0]

    @pl.when(step == 0)
    def _():
        lane = lax.broadcasted_iota(jnp.int32, (512, LANES), 1)

        @pl.loop(0, length // 512)
        def _(i):
            rows = pl.ds(pl.multiple_of(i * 512, 512), 512)
            keys[rows, :LANES] = k_ref[0, rows, :]
            keys[rows, LANES:] = kmark_ref[rows, :]
            v = v_ref[0, rows, :]
            one = jnp.ones_like(v)
            vals[0, rows, :] = jnp.where(lane < 64, v, one)
            vals[1, rows, :] = jnp.where(lane < 64, one, v)

    first = lax.broadcasted_iota(jnp.int32, (bq, LANES), 1) < 64
    q = q_ref[0]
    mark = qmark_ref[...]
    zero = jnp.zeros_like(q)
    queries = (
        jnp.concatenate([jnp.where(first, q, zero), mark], axis=1),
        jnp.concatenate([jnp.where(first, zero, q), mark], axis=1),
    )

    def body(j, carry):
        rows = pl.ds(pl.multiple_of(stored_block(j, own, per_part // bk) * bk, bk), bk)
        block = keys[rows, :]
        new = []
        for head in range(2):
            peak, total = carry[head]
            scores = lax.dot_general(queries[head], block, NT, preferred_element_type=F32)
            cuts = [scores[:, k * LANES : (k + 1) * LANES] for k in range(bk // LANES)]
            tallest = functools.reduce(jnp.maximum, cuts)
            higher = jnp.maximum(peak, jnp.max(tallest, axis=1, keepdims=True))
            weights = jnp.concatenate([jnp.exp2(cut - higher).astype(BF) for cut in cuts], axis=1)
            total = total * jnp.exp2(peak - higher) + jnp.dot(
                weights, vals[head, rows, :], preferred_element_type=F32
            )
            new.append((higher, total))
        return tuple(new)

    init = (jnp.full((bq, LANES), -3e38, F32), jnp.zeros((bq, LANES), F32))
    (peak_a, sum_a), (peak_b, sum_b) = lax.fori_loop(low_ref[step], high_ref[step], body, (init, init))
    weight_sum = pltpu.roll(jnp.where(first, sum_b, sum_a), 64, 1)
    ctx_ref[0] = (jnp.where(first, sum_a, sum_b) / weight_sum).astype(BF)
    lse_ref[...] = jnp.where(first, peak_a, peak_b) + jnp.log2(weight_sum)


def attend(qkv, pair, qmark, kmark, own, low, high, bq, bk, per_part):
    length = qmark.shape[0]
    row = lambda i, *_: (i, 0)
    whole = lambda i, *_: (0, 0)
    return pl.pallas_call(
        functools.partial(attend_kernel, bq=bq, bk=bk, per_part=per_part),
        grid_spec=pltpu.PrefetchScalarGridSpec(
            num_scalar_prefetch=3,
            grid=(length // bq,),
            in_specs=[
                pl.BlockSpec((1, bq, LANES), lambda i, *_: (3 * pair, i, 0)),
                pl.BlockSpec((1, length, LANES), lambda i, *_: (3 * pair + 1, 0, 0)),
                pl.BlockSpec((1, length, LANES), lambda i, *_: (3 * pair + 2, 0, 0)),
                pl.BlockSpec((bq, LANES), row),
                pl.BlockSpec((length, LANES), whole),
            ],
            out_specs=[
                pl.BlockSpec((1, bq, LANES), lambda i, *_: (i // (per_part // bq), i % (per_part // bq), 0)),
                pl.BlockSpec((bq, LANES), row),
            ],
            scratch_shapes=[pltpu.VMEM((length, 2 * LANES), BF), pltpu.VMEM((2, length, LANES), BF)],
        ),
        out_shape=[
            jax.ShapeDtypeStruct((length // per_part, per_part, LANES), BF),
            jax.ShapeDtypeStruct((length, LANES), F32),
        ],
        compiler_params=pltpu.CompilerParams(
            dimension_semantics=("arbitrary",), vmem_limit_bytes=48 * MIB
        ),
        cost_estimate=cost(35),
        name="attend",
    )(own, low, high, qkv, qkv, qkv, qmark, kmark)


def three_parts(value):
    high = value.astype(BF).astype(F32)
    rest = value - high
    middle = rest.astype(BF).astype(F32)
    return high, middle, (rest - middle).astype(BF).astype(F32)


def attend_back_kernel(
    own_ref, low_ref, high_ref, q_ref, k_ref, v_ref, do_ref, ctx_ref, lse_ref, qmark_ref, kmark_ref, cos_ref,
    sin_ref, out_ref, keys, vals, key_heads, query_heads, grad_heads, dq_sum,
    *, bq, bk, utt, per_part,
):
    length = kmark_ref.shape[0]
    own = own_ref[0]
    pb = 512
    lane = lax.broadcasted_iota(jnp.int32, (pb, LANES), 1)
    first = lane < 64

    @pl.loop(0, length // pb)
    def _(i):
        rows = pl.ds(pl.multiple_of(i * pb, pb), pb)
        at, within = i // (per_part // pb), pl.ds(pl.multiple_of(i % (per_part // pb) * pb, pb), pb)
        k = k_ref[0, rows, :]
        zero = jnp.zeros_like(k)
        mark = kmark_ref[rows, :]
        keys[rows, :LANES] = k
        keys[rows, LANES:] = mark
        vals[rows, :LANES] = v_ref[0, rows, :]
        vals[rows, LANES:] = mark
        q = q_ref[0, rows, :]
        grad = do_ref[at, within, :]
        qmark = qmark_ref[rows, :].astype(F32)
        lse = lse_ref[rows, :]
        product = grad.astype(F32) * ctx_ref[at, within, :].astype(F32)
        for head in range(2):
            mine = first if head == 0 else jnp.logical_not(first)
            key_heads[head, rows, :] = jnp.where(mine, k, zero)
            query_heads[head, rows, :LANES] = jnp.where(mine, q, zero)
            grad_heads[head, rows, :LANES] = jnp.where(mine, grad, zero)
            high, middle, low = three_parts(-lse[:, 64 * head : 64 * head + 1])
            query_heads[head, rows, LANES:] = jnp.where(
                lane == utt, high, jnp.where(lane == utt + 1, middle, jnp.where(lane == utt + 2, low, qmark))
            ).astype(BF)
            delta = jnp.sum(jnp.where(mine, product, 0.0), axis=1, keepdims=True)
            high, middle, low = three_parts(-delta)
            grad_heads[head, rows, LANES:] = jnp.where(
                lane == utt, high, jnp.where(lane == utt + 1, middle, jnp.where(lane == utt + 2, low, 0.0))
            ).astype(BF)
        dq_sum[rows, :] = jnp.zeros((pb, LANES), F32)

    @pl.loop(0, length // bk)
    def _(j):
        key_rows = pl.ds(pl.multiple_of(j * bk, bk), bk)
        key_block = keys[key_rows, :]
        value_block = vals[key_rows, :]

        def body(i, carry):
            dk, dv = carry
            rows = pl.ds(pl.multiple_of(stored_block(i, own, per_part // bq) * bq, bq), bq)
            dq = dq_sum[rows, :]
            for head in range(2):
                query = query_heads[head, rows, :]
                grad = grad_heads[head, rows, :]
                probs = jnp.exp2(lax.dot_general(key_block, query, NT, preferred_element_type=F32))
                pulled = lax.dot_general(value_block, grad, NT, preferred_element_type=F32)
                grad_scores = (probs * pulled).astype(BF)
                dv = dv + jnp.dot(probs.astype(BF), grad[:, :LANES], preferred_element_type=F32)
                dk = dk + jnp.dot(grad_scores, query[:, :LANES], preferred_element_type=F32)
                dq = dq + lax.dot_general(
                    grad_scores, key_heads[head, key_rows, :], TN, preferred_element_type=F32
                )
            dq_sum[rows, :] = dq
            return dk, dv

        zero = jnp.zeros((bk, LANES), F32)
        dk, dv = lax.fori_loop(low_ref[j], high_ref[j], body, (zero, zero))
        at, within = j // (per_part // bk), pl.ds(pl.multiple_of(j % (per_part // bk) * bk, bk), bk)
        out_ref[at, 2, within, :] = dv.astype(BF)
        dk = dk * (1.0 / LOG2E)
        out_ref[at, 1, within, :] = (dk * cos_ref[key_rows, :] - swap_halves(dk) * sin_ref[key_rows, :]).astype(BF)

    @pl.loop(0, length // pb)
    def _(i):
        rows = pl.ds(pl.multiple_of(i * pb, pb), pb)
        at, within = i // (per_part // pb), pl.ds(pl.multiple_of(i % (per_part // pb) * pb, pb), pb)
        dq = dq_sum[rows, :] * HEAD_DIM**-0.5
        out_ref[at, 0, within, :] = (dq * cos_ref[rows, :] - swap_halves(dq) * sin_ref[rows, :]).astype(BF)


def attend_back(
    qkv, pair, grad, ctx, lse, qmark, kmark, cosine, sine, own, low, high, bq, bk, utt, per_part
):
    length = qmark.shape[0]
    in_smem = pl.BlockSpec(memory_space=pltpu.SMEM)
    whole = pl.BlockSpec((length, LANES), lambda i: (0, 0))
    parts = length // per_part
    by_part = pl.BlockSpec((parts, per_part, LANES), lambda i: (0, 0, 0))
    cut = lambda kind: pl.BlockSpec((1, length, LANES), lambda i: (3 * pair + kind, 0, 0))
    wide = pltpu.VMEM((length, 2 * LANES), BF)
    return pl.pallas_call(
        functools.partial(attend_back_kernel, bq=bq, bk=bk, utt=utt, per_part=per_part),
        grid=(1,),
        in_specs=[in_smem] * 3 + [cut(0), cut(1), cut(2)] + [by_part] * 2 + [whole] * 5,
        out_specs=pl.BlockSpec((parts, 3, per_part, LANES), lambda i: (0, 0, 0, 0)),
        out_shape=jax.ShapeDtypeStruct((parts, 3, per_part, LANES), BF),
        scratch_shapes=[
            wide,
            wide,
            pltpu.VMEM((2, length, LANES), BF),
            pltpu.VMEM((2, length, 2 * LANES), BF),
            pltpu.VMEM((2, length, 2 * LANES), BF),
            pltpu.VMEM((length, LANES), F32),
        ],
        compiler_params=pltpu.CompilerParams(vmem_limit_bytes=56 * MIB),
        cost_estimate=cost(66),
        name="attend_back",
    )(own, low, high, qkv, qkv, qkv, grad, ctx, lse, qmark, kmark, cosine, sine)


def frame_marks(lengths, places, utt):
    ends = jnp.cumsum(lengths)
    starts = ends - lengths
    segment = jnp.sum((places[:, None] >= ends[None, :]).astype(jnp.int32), axis=1, dtype=jnp.int32)
    member = segment[:, None] == jnp.arange(utt, dtype=jnp.int32)[None, :]
    offsets = jnp.sum(jnp.where(member, starts[None, :], 0), axis=1, dtype=jnp.int32)
    return segment, member, offsets


def block_ranges(lengths, blocks, size, other):
    ends = jnp.cumsum(lengths)
    starts = ends - lengths
    at_first = blocks * size
    at_last = at_first + (size - 1)
    index = jnp.arange(lengths.shape[0], dtype=jnp.int32)
    seg_first = jnp.sum((at_first[:, None] >= ends[None]).astype(jnp.int32), axis=1)
    seg_last = jnp.sum((at_last[:, None] >= ends[None]).astype(jnp.int32), axis=1)
    low = jnp.sum(jnp.where(index[None] == seg_first[:, None], starts[None], 0), axis=1)
    high = jnp.sum(jnp.where(index[None] == seg_last[:, None], ends[None], 0), axis=1)
    return (low // other).astype(jnp.int32), ((high + other - 1) // other).astype(jnp.int32)


def feed_kernel(
    x_own_ref, cot_own_ref, cot_other_ref, weights_ref, heads_hbm,
    out_own_ref, out_other_ref, gin_own_ref, gin_other_ref, grads_ref, heads_out_hbm,
    x_other_ref, out_sum, gin_sum, local, sems, *, parts,
):
    step = pl.program_id(0)
    last = pl.num_programs(0) - 1
    d, z, core, half = mesh_spot(parts)
    beside = partner_of(d, z, half, half)

    eighth = d // 2 % 4 + 4 * core

    def heads_part(k):
        if k < parts:
            cut = heads_out_hbm.at[eighth, z]
            return remote_copy(cut, cut, sems, PIECES + k, (d, z ^ k))
        size = 1 << (k - parts)
        cut = heads_out_hbm.at[pl.ds(eighth // size * size, size)]
        return remote_copy(cut, cut, sems, PIECES + k, (d ^ (2, 4)[k - parts], z))

    @pl.when(step == 0)
    def _():
        greet([(d ^ bit, z) for bit in (1, 2, 4)] + [(d, z ^ k) for k in range(1, parts)])
        remote_copy(x_own_ref, x_other_ref, sems, 0, beside).start()
        copy = pltpu.make_async_copy(heads_hbm.at[:, eighth], heads_out_hbm.at[eighth, z], local)
        copy.start()
        copy.wait()
        for k in range(1, parts):
            heads_part(k).start()

    @pl.when(step == 1)
    def _():
        for k in range(1, parts):
            heads_part(k).wait()
        heads_part(parts).start()

    @pl.when(step == 2)
    def _():
        heads_part(parts).wait()
        heads_part(parts + 1).start()

    chunk, depth = weights_ref.shape[0] * weights_ref.shape[2], weights_ref.shape[3]
    up = weights_ref[:, 0].reshape(chunk, depth)
    down = weights_ref[:, 1].reshape(chunk, depth)
    root = math.sqrt(2.0 / math.pi)
    gup = gdown = None
    for side, (x_ref, cot_ref) in enumerate(((x_own_ref, cot_own_ref), (x_other_ref, cot_other_ref))):
        if side == 1:

            @pl.when(step == 0)
            def _():
                remote_copy(x_own_ref, x_other_ref, sems, 0, beside).wait()

        x = x_ref[...]
        cot = cot_ref[...]
        before = lax.dot_general(x, up, NT, preferred_element_type=F32)
        grad_act = lax.dot_general(cot, down, NT, preferred_element_type=F32)
        square = before * before
        bend = jnp.tanh(root * before * (1.0 + 0.044715 * square))
        half = 0.5 * (1.0 + bend)
        activated = (before * half).astype(BF)
        slope = half + 0.5 * before * (1.0 - bend * bend) * (root + (3.0 * 0.044715 * root) * square)
        grad_before = (grad_act * slope).astype(BF)
        out = jnp.dot(activated, down, preferred_element_type=F32)
        gin = jnp.dot(grad_before, up, preferred_element_type=F32)
        gd = lax.dot_general(activated, cot, TN, preferred_element_type=F32)
        gu = lax.dot_general(grad_before, x, TN, preferred_element_type=F32)
        gup = gu if side == 0 else gup + gu
        gdown = gd if side == 0 else gdown + gd

        out_to, gin_to = (out_own_ref, gin_own_ref) if side == 0 else (out_sum, gin_sum)

        @pl.when(step == 0)
        def _():
            out_to[...] = out
            gin_to[...] = gin

        @pl.when(step > 0)
        def _():
            out_to[...] += out
            gin_to[...] += gin

    per = weights_ref.shape[2]
    grads_ref[:, :per] = gup.astype(BF).reshape(-1, per, depth)
    grads_ref[:, per : 2 * per] = gdown.astype(BF).reshape(-1, per, depth)
    grads_ref[:, 2 * per :] = jnp.zeros(grads_ref[:, 2 * per :].shape, BF)

    @pl.when(step == last)
    def _():
        out_other_ref[...] = out_sum[...].astype(BF)
        gin_other_ref[...] = gin_sum[...].astype(BF)

        heads_part(parts + 1).wait()


def feed(x_own, cot_own, cot_other, weights, heads, spare, parts):
    frames, depth = x_own.shape
    groups, _, per, _ = weights.shape
    chunk = 512
    whole = pl.BlockSpec((frames, depth), lambda j: (0, 0), pipeline_mode=pl.Buffered(1))
    cut = pl.BlockSpec((chunk // per, 2, per, depth), lambda j: (j, 0, 0, 0))
    grads = pl.BlockSpec((chunk // per, 2 * per + spare, depth), lambda j: (j, 0, 0))
    shape = lambda *s: jax.ShapeDtypeStruct(*s)
    anywhere = pl.BlockSpec(memory_space=pl.ANY)
    return pl.pallas_call(
        functools.partial(feed_kernel, parts=parts),
        grid=(groups * per // chunk,),
        in_specs=[whole] * 3 + [cut, anywhere],
        out_specs=[whole] * 4 + [grads, anywhere],
        out_shape=[
            shape((frames, depth), F32),
            shape((frames, depth), BF),
            shape((frames, depth), F32),
            shape((frames, depth), BF),
            shape((groups, 2 * per + spare, depth), BF),
            shape((8, parts) + heads.shape[:1] + heads.shape[2:], BF),
        ],
        scratch_shapes=[
            pltpu.VMEM((frames, depth), BF),
            pltpu.VMEM((frames, depth), F32),
            pltpu.VMEM((frames, depth), F32),
            pltpu.SemaphoreType.DMA,
            pltpu.SemaphoreType.DMA((2 * (PIECES + parts + 3),)),
        ],
        compiler_params=pltpu.CompilerParams(
            dimension_semantics=("arbitrary",), vmem_limit_bytes=60 * MIB, collective_id=3, has_side_effects=True
        ),
        cost_estimate=cost(84),
        name="feed",
    )(x_own, cot_own, cot_other, weights, heads)


def spread(segment, table):
    masks = [segment == u for u in range(1, table.shape[0])]
    columns = []
    for k in range(table.shape[1] // LANES):
        cut = table[:, k * LANES : (k + 1) * LANES]
        out = jnp.broadcast_to(cut[0:1], segment.shape)
        for u, mask in enumerate(masks):
            out = jnp.where(mask, cut[u + 1 : u + 2], out)
        columns.append(out)
    return jnp.concatenate(columns, axis=1)


def collect(segment, values, utt):
    rows = []
    for u in range(utt):
        mask = segment == u
        rows.append(
            jnp.concatenate(
                [
                    jnp.sum(jnp.where(mask, values[:, k * LANES : (k + 1) * LANES], 0.0), axis=0, keepdims=True)
                    for k in range(values.shape[1] // LANES)
                ],
                axis=1,
            )
        )
    return jnp.concatenate(rows, axis=0)


def unit_norm(hidden):
    center = hidden - jnp.mean(hidden, axis=-1, keepdims=True)
    inverse = lax.rsqrt(jnp.mean(center * center, axis=-1, keepdims=True) + norm_epsilon)
    return center * inverse, inverse


def pull_norm(unit, inverse, grad, gain):
    pulled = grad * gain
    return (
        pulled
        - jnp.mean(pulled, axis=-1, keepdims=True)
        - unit * jnp.mean(pulled * unit, axis=-1, keepdims=True)
    ) * inverse


def join_kernel(*refs, pairs, parts):
    ctx_refs, refs = refs[: (pairs - 1) * parts], refs[(pairs - 1) * parts :]
    (
        last_hbm, w_out_ref, base_ref, base_in_ref, segment_ref, shift_ref, scale_ref,
        hidden_ref, normed_ref, last_out_hbm, last, local, sems,
    ) = refs
    step = pl.program_id(0)
    steps = pl.num_programs(0)
    d, z, core, half = mesh_spot(parts)
    part = core * half + z % half
    stays = z // half == core
    rows = hidden_ref.shape[0]

    def chunk(b, k):
        here = pl.ds(pl.multiple_of(k * rows, rows), rows)
        return remote_copy(
            last_hbm.at[b, here, :], last.at[b, here, :], sems, k * parts + b, partner_of(d, z, b, half)
        )

    own = pltpu.make_async_copy(last_hbm.at[0], last.at[0], local)

    @pl.when(step == 0)
    def _():
        own.start()
        greet([partner_of(d, z, b, half) for b in range(1, parts)])

        @pl.loop(0, steps)
        def _(k):
            for b in range(1, parts):
                chunk(b, k).start()

    hidden = jnp.where(stays, base_ref[...], base_in_ref[...]).astype(F32)
    for b in range(parts):
        for pair in range(pairs - 1):
            weights = w_out_ref[:, part ^ b].reshape(pairs * LANES, -1)[pair * LANES : (pair + 1) * LANES]
            hidden = hidden + jnp.dot(ctx_refs[pair * parts + b][...], weights, preferred_element_type=F32)

    @pl.when(step == 0)
    def _():
        own.wait()

    for b in range(1, parts):
        chunk(b, step).wait()
    here = pl.ds(pl.multiple_of(step * rows, rows), rows)
    for b in range(parts):
        weights = w_out_ref[:, part ^ b].reshape(pairs * LANES, -1)[(pairs - 1) * LANES :]
        hidden = hidden + jnp.dot(last[b, here, :], weights, preferred_element_type=F32)
    hidden_ref[...] = hidden
    unit, _ = unit_norm(hidden)
    segment = segment_ref[...]
    normed_ref[...] = (unit * (1.0 + spread(segment, scale_ref[...])) + spread(segment, shift_ref[...])).astype(BF)

    @pl.when(step == steps - 1)
    def _():
        copy = pltpu.make_async_copy(last, last_out_hbm, local)
        copy.start()
        copy.wait()


def join(ctx_blocks, last, w_out, base, base_in, segment, shift, scale, pairs, parts):
    frames, depth = base.shape
    rows = 256
    row = lambda i: (i, 0)
    wide = pl.BlockSpec((rows, depth), row)
    thin = pl.BlockSpec((rows, LANES), row)
    table = pl.BlockSpec(shift.shape, lambda i: (0, 0))
    anywhere = pl.BlockSpec(memory_space=pl.ANY)
    return pl.pallas_call(
        functools.partial(join_kernel, pairs=pairs, parts=parts),
        grid=(frames // rows,),
        in_specs=[thin] * len(ctx_blocks)
        + [anywhere, pl.BlockSpec(w_out.shape, lambda i: (0, 0, 0, 0)), wide, wide, thin]
        + [table] * 2,
        out_specs=[wide, wide, anywhere],
        out_shape=[
            jax.ShapeDtypeStruct((frames, depth), F32),
            jax.ShapeDtypeStruct((frames, depth), BF),
            jax.ShapeDtypeStruct(last.shape, BF),
        ],
        scratch_shapes=[
            pltpu.VMEM(last.shape, BF),
            pltpu.SemaphoreType.DMA,
            pltpu.SemaphoreType.DMA((2 * parts * (frames // rows),)),
        ],
        compiler_params=pltpu.CompilerParams(
            dimension_semantics=("arbitrary",), vmem_limit_bytes=40 * MIB, collective_id=5, has_side_effects=True
        ),
        cost_estimate=cost(18),
        name="join",
    )(*ctx_blocks, last, w_out, base, base_in, segment, shift, scale)


def turn_kernel(
    own_ref, gin_own_ref, gin_in_ref, out_own_ref, out_in_ref, hidden_ref, cot_ref, skips_ref, segment_ref, scale_ref,
    w_out_ref, grad_hidden_ref, low_ref, block_out_ref, sums_ref, *grad_context_refs, pairs, parts, utt,
):
    own = own_ref[0]
    hidden = hidden_ref[...]
    unit, inverse = unit_norm(hidden)
    segment = segment_ref[...]
    block_out_ref[0] = (hidden + out_own_ref[...] + out_in_ref[...].astype(F32)).astype(BF)
    block_out_ref[1] = skips_ref[...]
    grad = gin_own_ref[...] + gin_in_ref[...].astype(F32)
    grad_hidden = cot_ref[...].astype(F32) + pull_norm(unit, inverse, grad, 1.0 + spread(segment, scale_ref[...]))
    grad_hidden_ref[...] = grad_hidden
    low = grad_hidden.astype(BF)
    low_ref[...] = low
    for b in range(parts):
        part = lax.dot_general(low, w_out_ref[:, own ^ b].reshape(pairs * LANES, -1), NT, preferred_element_type=F32).astype(BF)
        for pair in range(pairs):
            grad_context_refs[pair * parts + b][...] = part[:, pair * LANES : (pair + 1) * LANES]
    sums = jnp.concatenate([collect(segment, grad, utt), collect(segment, grad * unit, utt)], axis=0)

    @pl.when(pl.program_id(0) == 0)
    def _():
        sums_ref[...] = sums

    @pl.when(pl.program_id(0) > 0)
    def _():
        sums_ref[...] += sums


def turn(own, gin_own, gin_in, out_own, out_in, hidden, cot, skips, segment, scale, w_out, pairs, parts):
    frames, depth = hidden.shape
    utt = scale.shape[0]
    rows = 256
    row = lambda i, *_: (i, 0)
    wide = pl.BlockSpec((rows, depth), row)
    thin = pl.BlockSpec((rows, LANES), row)
    shape = lambda *s: jax.ShapeDtypeStruct(*s)
    return pl.pallas_call(
        functools.partial(turn_kernel, pairs=pairs, parts=parts, utt=utt),
        grid_spec=pltpu.PrefetchScalarGridSpec(
            num_scalar_prefetch=1,
            grid=(frames // rows,),
            in_specs=[wide] * 7
            + [thin, pl.BlockSpec(scale.shape, lambda i, *_: (0, 0)), pl.BlockSpec(w_out.shape, lambda i, *_: (0, 0, 0, 0))],
            out_specs=[wide] * 2
            + [pl.BlockSpec((2, rows, depth), lambda i, *_: (0, i, 0)), pl.BlockSpec((2 * utt, depth), lambda i, *_: (0, 0))]
            + [thin] * (pairs * parts),
        ),
        out_shape=[
            shape((frames, depth), F32),
            shape((frames, depth), BF),
            shape((2, frames, depth), BF),
            shape((2 * utt, depth), F32),
        ]
        + [shape((frames, LANES), BF)] * (pairs * parts),
        compiler_params=pltpu.CompilerParams(
            dimension_semantics=("arbitrary",), vmem_limit_bytes=48 * MIB
        ),
        cost_estimate=cost(15),
        name="turn",
    )(own, gin_own, gin_in, out_own, out_in, hidden, cot, skips, segment, scale, w_out)


def out_grad_kernel(*refs, pairs, parts, columns, at_row):
    low_ref, ctx_refs, (last_ref, _, out_hbm, held, landing, local, sems) = refs[0], refs[1:-7], refs[-7:]
    d, z, core, half = mesh_spot(parts)
    part = core * half + z % half
    beside = partner_of(d, z, half, half)
    per = pairs * LANES // (2 * columns)
    greet([beside])
    if per < held.shape[3]:
        held[...] = jnp.zeros_like(held)
    low = low_ref[...]
    for b in range(parts):
        for pair in range(pairs):
            ctx = last_ref[b] if pair == pairs - 1 else ctx_refs[pair * parts + b][...]
            grad = lax.dot_general(ctx, low, TN, preferred_element_type=F32)
            for k in range(LANES // per):
                spot = pair * (LANES // per) + k
                held[spot % 2, spot // 2, part ^ b, :per, :] = grad[k * per : (k + 1) * per].astype(BF)
    remote(held.at[1 - core], landing, sems, 0, beside).wait()

    @pl.loop(0, columns)
    def _(i):
        held[core, i] = (held[core, i].astype(F32) + landing[i].astype(F32)).astype(BF)

    copies = []
    for i in range(columns):
        copy = pltpu.make_async_copy(
            held.at[core, i], out_hbm.at[i * parts : (i + 1) * parts, at_row:, :], local.at[i]
        )
        copy.start()
        copies.append(copy)
    for copy in copies:
        copy.wait()


def out_grad(low, ctx_blocks, last, grad_feed, at_row, pairs, parts, columns):
    depth = low.shape[1]
    spare = grad_feed.shape[1] - at_row
    vmem = pl.BlockSpec(memory_space=pltpu.VMEM)
    anywhere = pl.BlockSpec(memory_space=pl.ANY)
    return pl.pallas_call(
        functools.partial(out_grad_kernel, pairs=pairs, parts=parts, columns=columns, at_row=at_row),
        in_specs=[vmem] * (2 + len(ctx_blocks)) + [anywhere],
        out_specs=anywhere,
        out_shape=jax.ShapeDtypeStruct(grad_feed.shape, BF),
        scratch_shapes=[
            pltpu.VMEM((2, columns, parts, spare, depth), BF),
            pltpu.VMEM((columns, parts, spare, depth), BF),
            pltpu.SemaphoreType.DMA((columns,)),
            pltpu.SemaphoreType.DMA((2,)),
        ],
        input_output_aliases={2 + len(ctx_blocks): 0},
        compiler_params=pltpu.CompilerParams(
            collective_id=4, has_side_effects=True, vmem_limit_bytes=32 * MIB
        ),
        cost_estimate=cost(9),
        name="out_grad",
    )(low, *ctx_blocks, last, grad_feed)


class Sender:
    def __init__(self, sems, used=0):
        self.sems, self.used = sems, used
        self.d, self.z = lax.axis_index("dp"), lax.axis_index("tensor")

    def device(self, axis, bit):
        return (self.d ^ bit, self.z) if axis == "dp" else (self.d, self.z ^ bit)

    def side(self, axis, bit):
        return ((self.d if axis == "dp" else self.z) // bit) % 2

    def take(self, count):
        self.used += count
        return self.used - count

    def send(self, source, target, axis, bit):
        return remote(source, target, self.sems, self.take(1), self.device(axis, bit))


def rows_at(start, size):
    return pl.ds(pl.multiple_of(start, 16), size)


def few_rows(size):
    while size > 128:
        size //= 2
    return size


def add_rows(target, start, landing, landing_at, size):
    step = few_rows(size)

    @pl.loop(0, size // step)
    def _(i):
        here = rows_at(start + i * step, step)
        there = landing[rows_at(landing_at + i * step, step), :].astype(F32)
        target[here, :] = (target[here, :].astype(F32) + there).astype(target.dtype)


def sum_tree(sender, buffer, landing, down, turn_round, up, out, offset):
    size = buffer.shape[0] // 2
    starts, begin, kept = [0, size], [0, size], []
    for step in range(len(down[0])):
        kept.append(list(starts))
        size //= 2
        copies = []
        for side in range(2):
            axis, bit = down[side][step]
            upper = sender.side(axis, bit)
            lose = starts[side] + (1 - upper) * size
            copies.append(
                sender.send(buffer.at[rows_at(lose, size), :], landing.at[rows_at(begin[side], size), :], axis, bit)
            )
            starts[side] = starts[side] + upper * size
        yield
        for side in range(2):
            copies[side].wait()
            add_rows(buffer, starts[side], landing, begin[side], size)
            begin[side] += size
    yield from turn_round(starts, size)
    for step in reversed(range(len(down[0]))):
        copies = []
        for side in range(2):
            mine = out.at[rows_at(offset + starts[side], size), :]
            copies.append(sender.send(mine, mine, *up[side][step]))
        yield
        for side in range(2):
            copies[side].wait()
        starts = kept[step]
        size *= 2


def gather_rows(sender, own_hbm, out, semaphore):
    columns = out.shape[0] // 2
    slot = sender.d // 2 + columns * (sender.d % 2)
    copy = pltpu.make_async_copy(own_hbm, out.at[slot], semaphore)
    copy.start()
    yield
    copy.wait()
    size = 1
    while size < 2 * columns:
        cut = out.at[pl.ds(slot // size * size, size)]
        copy = sender.send(cut, cut, "dp", 2 * size if size < columns else 1)
        yield
        copy.wait()
        size *= 2


def spread_sums(sender, own, held, out, parts):
    half = parts // 2
    slot = (sender.d // 2) * 2 + sender.z // half
    held[0] = own
    group = [("dp", 1)] + [("tensor", 1 << k) for k in range(parts.bit_length() - 2)]
    for at, (axis, bit) in enumerate(group):
        copy = sender.send(held.at[2 * at], held.at[2 * at + 1], axis, bit)
        yield
        copy.wait()
        held[2 * at + 2] = held[2 * at] + held[2 * at + 1]
    out[pl.ds(slot, 1)] = held[pl.ds(2 * len(group), 1)]
    size = 1
    rows_all = out.shape[0]
    for axis, bit in [("tensor", half)] + [("dp", 1 << k) for k in range(1, rows_all.bit_length() - 1)]:
        mine = out.at[pl.ds(slot // size * size, size)]
        copy = sender.send(mine, mine, axis, bit)
        yield
        copy.wait()
        size *= 2


def run_all(running):
    for work in list(running):
        try:
            next(work)
        except StopIteration:
            running.remove(work)


def bits_of(rows_all, parts):
    dp_bits = [1 << k for k in range(1, rows_all.bit_length() - 1)]
    return dp_bits, [1 << k for k in reversed(range(parts.bit_length() - 1))]


def finish_kernel(*refs, pairs, parts, utt, rows_all):
    cut = (pairs - 1) * parts
    prev_hbm, refs = refs[:cut], refs[cut:]
    own_hbm, refs = refs[:pairs], refs[pairs:]
    (
        normed_hbm, weight_hbm, base_hbm, base_in_hbm, grad_hbm, inputs_hbm, shard_hbm, segment_ref, scale_ref,
        grad_base_ref, qkv_ref, sums_ref, shards_ref, inputs_in_hbm,
        prev, own, normed, weight, base, grad_hidden, arrived, total, qkv_held, qkv_in, loads, sems,
    ) = refs
    d, z, core, half = mesh_spot(parts)
    part = core * half + z % half
    stays = z // half == core
    frames = normed.shape[1]
    width = pairs * LANES

    there = ((d - core) + z // half, core * half + z % half)
    dp_bits, _ = bits_of(rows_all, parts)
    near = [partner_of(d, z, b, half) for b in range(1, parts)] + [(d, z ^ half)] + [(d ^ bit, z) for bit in dp_bits]
    barrier = pltpu.get_barrier_semaphore()
    for device in near:
        pl.semaphore_signal(barrier, inc=1, device_id=device, device_id_type=pl.DeviceIdType.MESH)

    @pl.when(jnp.logical_not(stays))
    def _():
        pl.semaphore_signal(barrier, inc=1, device_id=there, device_id_type=pl.DeviceIdType.MESH)
        pl.semaphore_wait(barrier, len(near) + 1)

    @pl.when(stays)
    def _():
        pl.semaphore_wait(barrier, len(near))

    sends = []
    order = [b for b in range(1, parts) if b % half] + [b for b in range(1, parts) if b % half == 0]
    for b in order:
        sends.append(
            (b, remote(own_hbm[-1].at[b], arrived.at[b - 1], sems, b - 1, partner_of(d, z, b, half)))
        )

    @pl.when(jnp.logical_not(stays))
    def _():
        for copy in in_pieces(inputs_hbm, inputs_in_hbm, sems, parts, there):
            copy.start()

    def load(at, source, target):
        copy = pltpu.make_async_copy(source, target, loads.at[at])
        copy.start()
        return copy

    first = [load(0, normed_hbm, normed)]
    for pair in range(pairs):
        first.append(load(1 + pair, own_hbm[pair], own.at[pair]))
    at = 1 + pairs
    four = pl.ds(core * 4, 4)
    second = [
        load(at, weight_hbm.at[four], weight.at[four]),
        remote(weight_hbm.at[four], weight.at[four], sems, parts - 1, (d ^ 1, z)),
    ]
    for k in range(cut):
        second.append(load(at + 1 + k, prev_hbm[k], prev.at[k]))
    at += 1 + cut
    third = [load(at, grad_hbm, grad_hidden)]

    @pl.when(stays)
    def _():
        pltpu.make_async_copy(base_hbm, base, loads.at[at + 1]).start()

    @pl.when(jnp.logical_not(stays))
    def _():
        pltpu.make_async_copy(base_in_hbm, base, loads.at[at + 1]).start()

    sender = Sender(sems, parts + PIECES)
    running = [gather_rows(sender, shard_hbm, shards_ref, loads.at[len(own_hbm) + cut + 4])]
    run_all(running)
    for copy in first:
        copy.wait()
    run_all(running)
    for kind in range(3):
        for pair in range(pairs):

            def gather(b, carry):
                return carry + lax.dot_general(own[pair, b, kind], normed[b], TN, preferred_element_type=F32)

            grad = lax.fori_loop(0, parts, gather, jnp.zeros((LANES, normed.shape[2]), F32)).astype(BF)
            wide = qkv_held.shape[1]
            for k in range(normed.shape[2] // wide):
                at_row = k * 3 * width + kind * width + pair * LANES
                qkv_held[at_row : at_row + LANES, :] = grad[:, k * wide : (k + 1) * wide]

    down = [
        [("dp", bit) for bit in dp_bits] + [("tensor", half)],
        [("dp", bit) for bit in reversed(dp_bits)] + [("tensor", half)],
    ]

    def go_home(starts, size):
        at_sem = sender.take(2)

        def copies():
            return [
                remote_copy(
                    qkv_held.at[rows_at(starts[side], size), :],
                    qkv_ref.at[rows_at(starts[side], size), :],
                    sems,
                    at_sem + side,
                    there,
                )
                for side in range(2)
            ]

        @pl.when(stays)
        def _():
            for side in range(2):
                here = rows_at(starts[side], size)
                qkv_ref[here, :] = qkv_held[here, :]

        @pl.when(jnp.logical_not(stays))
        def _():
            for copy in copies():
                copy.start()

        yield

        @pl.when(jnp.logical_not(stays))
        def _():
            for copy in copies():
                copy.wait()

        for side in range(2):
            starts[side] = starts[side] + (core - z // half) * size

    up = [line[:-1] + [("dp", 1)] for line in down]
    running.append(sum_tree(sender, qkv_held, qkv_in, down, go_home, up, qkv_ref, 0))
    run_all(running)

    for copy in second:
        copy.wait()
    rows = 256

    def add_block(source, b, pair, fresh):
        weights = jnp.concatenate(
            [weight[:, part ^ b, kind * pairs + pair].reshape(LANES, -1) for kind in range(3)],
            axis=0,
        )

        @pl.loop(0, frames // rows)
        def _(i):
            here = pl.ds(pl.multiple_of(i * rows, rows), rows)
            block = jnp.concatenate([source[kind, here, :] for kind in range(3)], axis=1)
            term = jnp.dot(block, weights, preferred_element_type=F32)
            if fresh:
                total[here, :] = term
            else:
                total[here, :] += term

    add_block(own.at[pairs - 1, 0], 0, pairs - 1, True)
    run_all(running)
    for pair in range(pairs - 1):
        for b in range(parts):
            add_block(prev.at[pair * parts + b], b, pair, False)
            if b % 2:
                run_all(running)
    for b, copy in sorted(sends, key=lambda item: (item[0] % half, item[0])):
        copy.wait()
        add_block(arrived.at[b - 1], b, pairs - 1, False)
        run_all(running)

    for copy in third:
        copy.wait()
    pltpu.make_async_copy(base_hbm, base, loads.at[at + 1]).wait()
    sums_ref[...] = jnp.zeros_like(sums_ref)

    @pl.loop(0, frames // rows)
    def _(i):
        here = pl.ds(pl.multiple_of(i * rows, rows), rows)
        unit, inverse = unit_norm(base[here, :].astype(F32))
        grad = total[here, :]
        segment = segment_ref[here, :]
        pulled = pull_norm(unit, inverse, grad, 1.0 + spread(segment, scale_ref[...]))
        grad_base_ref[here, :] = (grad_hidden[here, :] + pulled).astype(BF)
        sums_ref[...] += jnp.concatenate([collect(segment, grad, utt), collect(segment, grad * unit, utt)], axis=0)

    while running:
        run_all(running)

    @pl.when(jnp.logical_not(stays))
    def _():
        for copy in in_pieces(inputs_hbm, inputs_in_hbm, sems, parts, there):
            copy.wait()


def finish(
    prev, own, normed_all, weight, base, base_in, grad_hidden, inputs, shard, segment, scale, pairs, parts, rows_all
):
    frames, depth = base.shape
    utt = scale.shape[0]
    units = 3 * pairs * LANES
    wide = depth
    while units * depth // wide % (16 * rows_all * 2):
        wide //= 2
    qkv_shape = (units * depth // wide, wide)
    copies = parts + 2 + PIECES + 6 * rows_all.bit_length() + parts.bit_length()
    anywhere = pl.BlockSpec(memory_space=pl.ANY)
    vmem = pl.BlockSpec(memory_space=pltpu.VMEM)
    shape = lambda *s: jax.ShapeDtypeStruct(*s)
    block = (3, frames, LANES)
    return pl.pallas_call(
        functools.partial(finish_kernel, pairs=pairs, parts=parts, utt=utt, rows_all=rows_all),
        in_specs=[anywhere] * (len(prev) + pairs + 7) + [vmem] * 2,
        out_specs=[vmem] * 4 + [anywhere],
        out_shape=[
            shape((frames, depth), BF),
            shape(qkv_shape, BF),
            shape((2 * utt, depth), F32),
            shape((rows_all,) + shard.shape, BF),
            shape((frames, depth), BF),
        ],
        scratch_shapes=[
            pltpu.VMEM((max(len(prev), 1),) + block, BF),
            pltpu.VMEM((pairs, parts) + block, BF),
            pltpu.VMEM(normed_all.shape, BF),
            pltpu.VMEM(weight.shape, BF),
            pltpu.VMEM((frames, depth), BF),
            pltpu.VMEM((frames, depth), F32),
            pltpu.VMEM((parts - 1,) + block, BF),
            pltpu.VMEM((frames, depth), F32),
            pltpu.VMEM(qkv_shape, BF),
            pltpu.VMEM(qkv_shape, BF),
            pltpu.SemaphoreType.DMA((5 + pairs + len(prev),)),
            pltpu.SemaphoreType.DMA((2 * copies,)),
        ],
        compiler_params=pltpu.CompilerParams(
            collective_id=1, has_side_effects=True, vmem_limit_bytes=56 * MIB
        ),
        cost_estimate=cost(60),
        name="finish",
    )(*prev, *own, normed_all, weight, base, base_in, grad_hidden, inputs, shard, segment, scale)


def sums_kernel(
    inputs_hbm, inputs_in_hbm, skips_hbm, skips_in_hbm, grad_ref, sums_ref, skip_out_ref, sums_out_ref, grad_in_hbm,
    frames_in, away, held, first_in, half_in, sums_in, loads, sems, *, rows_all, parts,
):
    d, z, core, half = mesh_spot(parts)
    stays = z // half == core
    leaves = jnp.logical_not(stays)
    dp_bits, z_bits = bits_of(rows_all, parts)
    there = ((d - core) + z // half, core * half + z % half)
    depth = grad_ref.shape[1]
    half_rows, width = held.shape

    for at, (source, source_in) in enumerate(((inputs_hbm, inputs_in_hbm), (skips_hbm, skips_in_hbm))):
        slot = frames_in.at[1 - core if at == 0 else core]

        @pl.when(stays)
        def _():
            pltpu.make_async_copy(source, slot, loads.at[at]).start()

        @pl.when(leaves)
        def _():
            pltpu.make_async_copy(source_in, slot, loads.at[at]).start()

    sender = Sender(sems, PIECES)
    near = [("dp", 1)] + [("dp", bit) for bit in dp_bits] + [("tensor", bit) for bit in z_bits]
    barrier = pltpu.get_barrier_semaphore()
    for axis, bit in near:
        pl.semaphore_signal(
            barrier, inc=1, device_id=sender.device(axis, bit), device_id_type=pl.DeviceIdType.MESH
        )

    @pl.when(leaves)
    def _():
        pl.semaphore_signal(barrier, inc=1, device_id=there, device_id_type=pl.DeviceIdType.MESH)
        pl.semaphore_wait(barrier, len(near) + 1)

    @pl.when(stays)
    def _():
        pl.semaphore_wait(barrier, len(near))

    def start_move(k):
        @pl.when(leaves)
        def _():
            in_pieces(grad_ref, grad_in_hbm, sems, 0, there, [k])[0].start()

    def settle(starts, size):
        for side in range(2):
            skip_out_ref[rows_at(offset + starts[side], size), :] = held[rows_at(starts[side], size), :]
        yield

    offset = core * half_rows

    def skips():
        for slot in range(2):
            pltpu.make_async_copy(inputs_hbm, frames_in.at[slot], loads.at[slot]).wait()
        for slot, target in ((0, away), (1, held)):

            @pl.loop(0, depth // 256)
            def _(i):
                cut = frames_in[slot, :, pl.ds(pl.multiple_of(i * 256, 256), 256)]
                grad = lax.dot_general(cut, grad_ref[...], TN, preferred_element_type=F32).astype(BF)
                for k in range(depth // width):
                    target[rows_at(k * depth + i * 256, 256), :] = grad[:, k * width : (k + 1) * width]

            if slot == 0:
                copy = sender.send(away, first_in, "dp", 1)
                yield
        copy.wait()
        add_rows(held, 0, first_in, 0, half_rows)
        down = [
            [("dp", bit) for bit in dp_bits] + [("tensor", bit) for bit in z_bits],
            [("dp", bit) for bit in reversed(dp_bits)] + [("tensor", bit) for bit in z_bits],
        ]
        yield from sum_tree(sender, held, half_in, down, settle, down, skip_out_ref, offset)
        mine = skip_out_ref.at[rows_at(offset, half_rows), :]
        copy = sender.send(mine, mine, "dp", 1)
        yield
        copy.wait()

    running = [skips(), spread_sums(sender, sums_ref[...], sums_in, sums_out_ref, parts)]
    rounds = 0
    later = 1 + len(dp_bits) + 2 * len(z_bits) + 1
    while running:
        if rounds in (0, 1, later, later + 1):
            start_move(rounds if rounds < 2 else rounds - later + 2)
        rounds += 1
        run_all(running)

    @pl.when(leaves)
    def _():
        for copy in in_pieces(grad_ref, grad_in_hbm, sems, 0, there):
            copy.wait()


def sums(inputs, inputs_in, skips, skips_in, grad_base, utterance_sums, rows_all, parts):
    frames, depth = inputs.shape
    devices = rows_all * parts
    width = min(depth, depth * depth // (16 * devices))
    half_rows = depth * depth // width
    stages = rows_all.bit_length() + parts.bit_length() - 3
    copies = PIECES + 2 + 4 * stages + rows_all.bit_length() + parts.bit_length()
    vmem = pl.BlockSpec(memory_space=pltpu.VMEM)
    anywhere = pl.BlockSpec(memory_space=pl.ANY)
    shape = lambda *s: jax.ShapeDtypeStruct(*s)
    skip_sum, all_sums, grad_base_in = pl.pallas_call(
        functools.partial(sums_kernel, rows_all=rows_all, parts=parts),
        in_specs=[anywhere] * 4 + [vmem] * 2,
        out_specs=[vmem] * 2 + [anywhere],
        out_shape=[
            shape((2 * half_rows, width), BF),
            shape((rows_all,) + utterance_sums.shape, F32),
            shape((frames, depth), BF),
        ],
        scratch_shapes=[pltpu.VMEM((2, frames, depth), BF)]
        + [pltpu.VMEM((half_rows, width), BF)] * 4
        + [
            pltpu.VMEM((2 * parts.bit_length() - 1,) + utterance_sums.shape, F32),
            pltpu.SemaphoreType.DMA((2,)),
            pltpu.SemaphoreType.DMA((2 * copies,)),
        ],
        compiler_params=pltpu.CompilerParams(
            collective_id=0, has_side_effects=True, vmem_limit_bytes=56 * MIB
        ),
        cost_estimate=cost(100),
        name="sums",
    )(inputs, inputs_in, skips, skips_in, grad_base, utterance_sums)
    skip_sum = skip_sum.reshape(2, depth // width, depth, width)
    skip_sum = jnp.transpose(skip_sum, (0, 2, 1, 3)).reshape(2, depth, depth)
    return skip_sum, all_sums, grad_base_in


def spread_out_kernel(shard_ref, up_ref, down_ref):
    per = down_ref.shape[0]
    rows = shard_ref[0].astype(F32)
    up_ref[...] = rows[:per].T
    down_ref[...] = rows[per : 2 * per]


def spread_out(shards, per):
    count, _, depth = shards.shape
    units = count * per
    if per % LANES:
        up = jnp.transpose(shards[:, :per].reshape(units, depth)).astype(F32)
        return up, shards[:, per : 2 * per].reshape(units, depth).astype(F32)
    return pl.pallas_call(
        spread_out_kernel,
        grid=(count,),
        in_specs=[pl.BlockSpec((1,) + shards.shape[1:], lambda i: (i, 0, 0))],
        out_specs=[pl.BlockSpec((depth, per), lambda i: (0, i)), pl.BlockSpec((per, depth), lambda i: (i, 0))],
        out_shape=[jax.ShapeDtypeStruct((depth, units), F32), jax.ShapeDtypeStruct((units, depth), F32)],
        compiler_params=pltpu.CompilerParams(vmem_limit_bytes=24 * MIB),
        cost_estimate=cost(4),
        name="spread_out",
    )(shards)


def front_kernel(
    ends_ref, inputs_ref, skips_ref, w_in_ref, w_res_ref, segment_ref, shift_ref, scale_ref, rate_ref, weight_hbm, w_out_ref,
    base_ref, out_ref, cos_ref, sin_ref, qmark_ref, kmark_ref, weight_in_hbm, w_out_all_ref, away, local, sems,
    *, parts, utt,
):
    d, z, core, half = mesh_spot(parts)
    stays = z // half == core
    leaves = jnp.logical_not(stays)
    there = ((d - core) + z // half, core * half + z % half)
    frames = base_ref.shape[0]
    rows = 256
    chunks = frames // rows

    barrier = pltpu.get_barrier_semaphore()
    near = [partner_of(d, z, b, half) for b in range(1, half + 1)] + [(d ^ bit, z) for bit in (2, 4, 6)]
    near += [(d, z ^ k) for k in range(half, parts)]
    for device in near:
        pl.semaphore_signal(barrier, inc=1, device_id=device, device_id_type=pl.DeviceIdType.MESH)

    @pl.when(leaves)
    def _():
        pl.semaphore_signal(barrier, inc=1, device_id=there, device_id_type=pl.DeviceIdType.MESH)
        pl.semaphore_wait(barrier, len(near) + 1)

    @pl.when(stays)
    def _():
        pl.semaphore_wait(barrier, len(near))

    def here(k):
        return pl.ds(pl.multiple_of(k * rows, rows), rows)

    def copy(kind, k, source, target, device):
        at = kind * chunks + k
        return pltpu.make_async_remote_copy(
            src_ref=source,
            dst_ref=target,
            send_sem=sems.at[2 * at],
            recv_sem=sems.at[2 * at + 1],
            device_id=device,
            device_id_type=pl.DeviceIdType.MESH,
        )

    def moving(k):
        return copy(0, k, away.at[here(k), :], out_ref.at[0, here(k), :], there)

    quarter = weight_hbm.shape[0] // 4
    column = d // 2 % 4

    def weight_part(k):
        cut = pl.ds(pl.multiple_of((column ^ k) * quarter, 16), quarter)
        if k == 0:
            return copy(parts, 0, weight_hbm.at[cut, :], weight_in_hbm.at[cut, :], there)
        own = pl.ds(pl.multiple_of(column * quarter, 16), quarter)
        return copy(parts, k, weight_in_hbm.at[own, :], weight_in_hbm.at[own, :], (d ^ (2 * k), z))

    @pl.when(leaves)
    def _():
        weight_part(0).start()

    @pl.when(stays)
    def _():
        pltpu.make_async_copy(weight_hbm, weight_in_hbm, local).start()

    eighth = d // 2 % 4 + 4 * core
    per = w_out_all_ref.shape[2]
    w_out_all_ref[eighth, z] = w_out_ref[pl.ds(pl.multiple_of(eighth * per, 16), per), :]

    def w_out_part(k):
        if k < parts:
            cut = w_out_all_ref.at[eighth, z]
            return copy(parts, 3 + k, cut, cut, (d, z ^ k))
        size = 1 << (k - parts)
        cut = w_out_all_ref.at[pl.ds(eighth // size * size, size)]
        return copy(parts, 3 + k, cut, cut, (d ^ (2, 4, 1)[k - parts], z))

    for k in range(1, parts):
        w_out_part(k).start()

    def across(b, k):
        return copy(b, k, out_ref.at[0, here(k), :], out_ref.at[b, here(k), :], partner_of(d, z, b, half))

    def beside(b, k):
        return copy(
            half + b, k, out_ref.at[b, here(k), :], out_ref.at[half + b, here(k), :], partner_of(d, z, half, half)
        )

    def spread_own(k):
        for b in range(1, half):
            across(b, k).start()
        beside(0, k).start()

    @pl.loop(0, chunks)
    def _(k):
        at = here(k)
        base = jnp.dot(inputs_ref[at, :], w_in_ref[...], preferred_element_type=F32)
        base = base + jnp.dot(skips_ref[at, :], w_res_ref[...], preferred_element_type=F32)
        base_ref[at, :] = base.astype(BF)
        unit, _ = unit_norm(base)
        segment = segment_ref[at, :]
        normed = (unit * (1.0 + spread(segment, scale_ref[...])) + spread(segment, shift_ref[...])).astype(BF)

        @pl.when(stays)
        def _():
            out_ref[0, at, :] = normed
            spread_own(k)

        @pl.when(leaves)
        def _():
            away[at, :] = normed
            moving(k).start()

    part = core * half + z % half

    @pl.loop(0, parts * chunks)
    def _(i):
        at = here(i)
        place = (part ^ (i // chunks)) * frames + (i % chunks) * rows
        place = place + lax.broadcasted_iota(jnp.int32, (rows, LANES), 0)
        lane = lax.broadcasted_iota(jnp.int32, (rows, LANES), 1)
        segment = jnp.zeros((rows, LANES), jnp.int32)
        start = jnp.zeros((rows, LANES), jnp.int32)
        for u in range(utt - 1):
            past = place >= ends_ref[u]
            segment = jnp.where(past, u + 1, segment)
            start = jnp.where(past, ends_ref[u], start)
        angle = (place - start).astype(F32) * rate_ref[0:1, :]
        cos_ref[at, :] = jnp.cos(angle)
        sin_ref[at, :] = jnp.sin(angle) * rate_ref[1:2, :]
        other = jnp.logical_and(lane < utt, lane != segment)
        qmark_ref[at, :] = jnp.where(other, MASKED, 0.0).astype(BF)
        shown = jnp.where(lane < utt + 3, 1.0, 0.0)
        kmark_ref[at, :] = jnp.where(other, 0.0, shown).astype(BF)

    for k in range(1, parts):
        w_out_part(k).wait()
    w_out_part(parts).start()

    @pl.when(leaves)
    def _():
        weight_part(0).wait()
        for k in range(1, 4):
            weight_part(k).start()

        @pl.loop(0, chunks)
        def _(k):
            moving(k).wait_recv()
            spread_own(k)

    w_out_part(parts).wait()
    w_out_part(parts + 1).start()

    @pl.loop(0, chunks)
    def _(k):
        for b in range(1, half):
            across(b, k).wait_recv()
            beside(b, k).start()

    w_out_part(parts + 1).wait()
    w_out_part(parts + 2).start()

    @pl.loop(0, chunks)
    def _(k):
        for b in range(half):
            beside(b, k).wait_recv()
            beside(b, k).wait_send()
        for b in range(1, half):
            across(b, k).wait_send()

    @pl.when(leaves)
    def _():
        @pl.loop(0, chunks)
        def _(k):
            moving(k).wait_send()

        for k in range(1, 4):
            weight_part(k).wait()

    @pl.when(stays)
    def _():
        pltpu.make_async_copy(weight_hbm, weight_in_hbm, local).wait()

    w_out_part(parts + 2).wait()


def front(ends, inputs, skips, w_in, w_res, segment, shift, scale, rate, weight, w_out, parts):
    frames, depth = inputs.shape
    utt = ends.shape[0]
    vmem = pl.BlockSpec(memory_space=pltpu.VMEM)
    return pl.pallas_call(
        functools.partial(front_kernel, parts=parts, utt=utt),
        in_specs=[pl.BlockSpec(memory_space=pltpu.SMEM)] + [vmem] * 8 + [pl.BlockSpec(memory_space=pl.ANY), vmem],
        out_specs=[vmem] * 6 + [pl.BlockSpec(memory_space=pl.ANY), vmem],
        out_shape=[
            jax.ShapeDtypeStruct((frames, depth), BF),
            jax.ShapeDtypeStruct((parts, frames, depth), BF),
            jax.ShapeDtypeStruct((parts * frames, LANES), F32),
            jax.ShapeDtypeStruct((parts * frames, LANES), F32),
            jax.ShapeDtypeStruct((parts * frames, LANES), BF),
            jax.ShapeDtypeStruct((parts * frames, LANES), BF),
            jax.ShapeDtypeStruct(weight.shape, BF),
            jax.ShapeDtypeStruct((8, parts, w_out.shape[0] // 8, depth), BF),
        ],
        scratch_shapes=[
            pltpu.VMEM((frames, depth), BF),
            pltpu.SemaphoreType.DMA,
            pltpu.SemaphoreType.DMA((2 * (parts * (frames // 256) + 6 + parts),)),
        ],
        compiler_params=pltpu.CompilerParams(
            collective_id=2, has_side_effects=True, vmem_limit_bytes=48 * MIB
        ),
        cost_estimate=cost(75),
        name="front",
    )(ends, inputs, skips, w_in, w_res, segment, shift, scale, rate, weight, w_out)


def dot(a, b, dims=(((1,), (0,)), ((), ()))):
    return lax.dot_general(a, b, dims, preferred_element_type=F32)


def after(value, token):
    return lax.optimization_barrier((value, token))[0]


def on_device(
    inputs, skip_input, lengths, time_steps, w_skip_in, w_skip_res, w_ada, w_qkv, w_out, w_up, w_down, cotangent
):
    parts = lax.axis_size("tensor")
    rows_all = lax.axis_size("dp")
    half = parts // 2
    columns = rows_all // 2
    d = lax.axis_index("dp")
    z = lax.axis_index("tensor")
    core, column = d % 2, d // 2
    stays = z // half == core
    part = core * half + z % half
    inputs, skip_input, cotangent = inputs[0], skip_input[0], cotangent[0]
    frames, depth = inputs.shape
    length = frames * parts
    ws = w_qkv.shape[2]
    pairs = ws // LANES
    utt = lengths.shape[1]
    both = ("dp", "tensor")

    def moved(value):
        pattern = [
            (i * parts + j, ((i // 2) * 2 + j // half) * parts + (i % 2) * half + j % half)
            for i in range(rows_all)
            for j in range(parts)
            if i % 2 != j // half
        ]
        return lax.ppermute(value, both, pattern)

    def partner(value, b):
        pattern = [
            (i * parts + j, (i ^ (b // half)) * parts + (j // half) * half + ((j % half) ^ (b % half)))
            for i in range(rows_all)
            for j in range(parts)
        ]
        return lax.ppermute(value, both, pattern)

    def exchange(blocks):
        return [blocks[0]] + [partner(blocks[b], b) for b in range(1, parts)]

    same_core = [[2 * i + k for i in range(columns)] for k in range(2)]

    other_lengths = partner(lengths, half)
    other_steps = partner(time_steps, half)
    lengths_work = jnp.where(stays, lengths, other_lengths)[0]
    steps_work = jnp.where(stays, time_steps, other_steps)[0]

    time_rate = jnp.exp(
        -math.log(10000.0) * (jnp.arange(w_ada.shape[0] // 2, dtype=F32) / (w_ada.shape[0] // 2))
    )

    def embed(steps):
        phases = steps.astype(F32)[:, None] * time_rate
        return jax.nn.silu(jnp.concatenate([jnp.sin(phases), jnp.cos(phases)], axis=-1)).astype(BF)

    def wide_segment(row_lengths, places):
        segment, _, _ = frame_marks(row_lengths, places, utt)
        return jnp.broadcast_to(segment[:, None], (places.shape[0], LANES))

    spot = jnp.arange(frames, dtype=jnp.int32)
    mods_home = dot(embed(time_steps[0]), w_ada[:, : 2 * depth])
    qkv_rows = jnp.transpose(w_qkv, (0, 2, 1)).reshape(3 * ws, depth)
    rotary_rate = jnp.exp(-math.log(10000.0) * (2.0 * jnp.arange(HEAD_DIM // 2, dtype=F32) / HEAD_DIM))
    sign = jnp.where(jnp.arange(LANES) % HEAD_DIM < HEAD_DIM // 2, -1.0, 1.0).astype(F32)
    base_home, normed_all, cosine, sine, qmark, kmark, w_mine, w_out_all = front(
        jnp.cumsum(lengths_work, dtype=jnp.int32),
        inputs,
        skip_input,
        w_skip_in,
        w_skip_res,
        wide_segment(lengths[0], z * frames + spot),
        mods_home[:, :depth],
        mods_home[:, depth:],
        jnp.stack([jnp.tile(rotary_rate, 4), sign]),
        qkv_rows,
        w_out,
        parts,
    )

    per_q, per_o = 3 * ws // rows_all, ws // rows_all
    units = w_down.shape[0]
    per_u = units // rows_all
    slice_feed = jnp.concatenate(
        [
            jnp.transpose(lax.dynamic_slice_in_dim(w_up, d * per_u, per_u, 1)),
            lax.dynamic_slice_in_dim(w_down, d * per_u, per_u, 0),
        ]
    )
    feed_rows = lax.all_gather(slice_feed, "tensor")
    feed_rows = lax.all_gather(after(feed_rows, base_home), "dp", axis_index_groups=same_core)
    feed_rows = feed_rows.reshape(columns * parts, 2, per_u, depth)

    cotangent = after(cotangent, base_home)
    cot = jnp.where(stays, cotangent, moved(cotangent))
    base_in = moved(after(base_home, cot))

    silu_work = embed(steps_work)
    mods = dot(silu_work, w_ada)
    shift_one, scale_one, shift_two, scale_two = [mods[:, k * depth : (k + 1) * depth] for k in range(4)]
    segment_here = wide_segment(lengths_work, part * frames + spot)

    qkv = project(normed_all.reshape(length, depth), w_mine, cosine, sine, pairs)

    def ranges(size, other):
        per = frames // size
        stored = jnp.arange(length // size, dtype=jnp.int32)
        natural = (part ^ (stored // per)) * per + stored % per
        return block_ranges(lengths_work, natural, size, other)

    own = jnp.stack([part.astype(jnp.int32), stays.astype(jnp.int32)])
    wide = min(frames, 1024)
    low, high = ranges(wide, wide)
    bq, bk = 512, 512
    low_back, high_back = ranges(bk, bq)
    ctx_pairs, lse_pairs, ctx_mine = [], [], []
    for pair in range(pairs):
        ctx, lse = attend(
            after(qkv, cot) if pair == pairs - 1 else qkv, pair, qmark, kmark, own, low, high, wide, wide, frames
        )
        ctx_pairs.append(ctx)
        lse_pairs.append(lse)
        if pair < pairs - 1:
            ctx_mine += exchange([ctx[b] for b in range(parts)])
    hidden, ffn_in, ctx_last = join(
        ctx_mine, ctx_pairs[-1], w_out_all, base_home, base_in, segment_here, shift_two, scale_two, pairs, parts
    )

    cot_other = partner(cot, half)
    spare = max(per_o, 16)
    heads = qkv_rows.reshape(3 * pairs, 8, LANES // 8, depth)
    out_own, out_send, gin_own, gin_send, grad_feed, w_heads = feed(
        ffn_in, cot, cot_other, feed_rows, heads, spare, parts
    )
    grad_hidden, low_grad, block_out, sums_two, *grad_context = turn(
        own, gin_own, partner(gin_send, half), out_own, partner(out_send, half), hidden, cot, skip_input, segment_here,
        scale_two,
        w_out_all, pairs, parts,
    )

    grad_feed = out_grad(low_grad, ctx_mine, ctx_last, grad_feed, 2 * per_u, pairs, parts, columns)
    grad_feed = grad_feed.reshape(columns, parts, 2 * per_u + spare, depth)
    feed_sum = lax.psum_scatter(grad_feed, "dp", scatter_dimension=0, axis_index_groups=same_core)
    feed_shard = lax.psum_scatter(feed_sum, "tensor", scatter_dimension=0)

    grad_mine = []
    for pair in range(pairs):
        grad = jnp.stack(exchange(grad_context[pair * parts : (pair + 1) * parts]))
        if pair == pairs - 1 and pairs > 1:
            grad = after(grad, feed_sum)
        grads = attend_back(
            qkv, pair, grad, ctx_pairs[pair], lse_pairs[pair], qmark, kmark, cosine, sine, own,
            low_back, high_back, bq, bk, utt, frames,
        )
        grad_mine.append(grads)

    returned = []
    for grads in grad_mine[:-1]:
        returned += exchange([grads[b] for b in range(parts)])
    block_out_in, skips_in = moved(block_out)
    grad_base, grad_qkv, sums_one, shards, inputs_in = finish(
        returned, grad_mine, normed_all, w_heads, base_home, base_in, grad_hidden, inputs, feed_shard.reshape(-1, depth), segment_here,
        scale_one, pairs, parts, rows_all,
    )
    shards = jnp.transpose(shards.reshape((2, columns) + shards.shape[1:]), (1, 0, 2, 3))
    grad_up, grad_down = spread_out(shards.reshape((rows_all,) + shards.shape[2:]), per_u)
    grad_out = shards[:, :, 2 * per_u : 2 * per_u + per_o].reshape(ws, depth).astype(F32)
    silu_rows = jnp.pad(silu_work.astype(F32) * (1.0 / parts), ((0, 0), (0, depth - silu_work.shape[1])))
    skip_sum, all_sums, grad_base_in = sums(
        inputs, inputs_in, skip_input, skips_in, grad_base, jnp.concatenate([sums_one, sums_two, silu_rows]),
        rows_all, parts,
    )
    grad_qkv = grad_qkv.reshape(-1, 3, ws, grad_qkv.shape[1])
    grad_qkv = jnp.transpose(grad_qkv, (1, 0, 3, 2)).reshape(3, depth, ws).astype(F32)
    grad_skip = skip_sum.astype(F32)
    grad_base_home = jnp.where(stays, grad_base, grad_base_in)
    grad_inputs = dot(grad_base_home, w_skip_in, NT)
    grad_skips = dot(grad_base_home, w_skip_res, NT)
    block_out = jnp.where(stays, block_out[0], block_out_in).astype(F32)

    all_sums = all_sums.reshape(rows_all, 5, utt, depth)
    silu_all = all_sums[:, 4, :, : w_ada.shape[0]].reshape(rows_all * utt, w_ada.shape[0])
    all_sums = jnp.concatenate([all_sums[:, k] for k in range(4)], axis=-1).reshape(rows_all * utt, 4 * depth)
    grad_ada = jnp.einsum("ut,um->tm", silu_all, all_sums, precision=lax.Precision.HIGHEST)

    return (
        block_out[None],
        grad_inputs[None],
        grad_skips[None],
        grad_skip[0],
        grad_skip[1],
        grad_ada,
        grad_qkv,
        grad_out,
        grad_up,
        grad_down,
    )


def solution(mesh):
    placed = (
        P("dp", "tensor", None),
        P("dp", "tensor", None),
        P("dp", None),
        P("dp", None),
        P(),
        P(),
        P(),
        P(None, None, "tensor"),
        P("tensor", None),
        P(None, "tensor"),
        P("tensor", None),
        P("dp", "tensor", None),
    )
    return jax.shard_map(
        on_device,
        mesh=mesh,
        in_specs=placed,
        out_specs=(
            P("dp", "tensor", None),
            P("dp", "tensor", None),
            P("dp", "tensor", None),
            P(),
            P(),
            P(),
            P(None, None, "tensor"),
            P("tensor", None),
            P(None, "tensor"),
            P("tensor", None),
        ),
        check_vma=False,
    )
```

```python
import functools
import math

import jax
import jax.numpy as jnp
from jax import lax
from jax.experimental import pallas as pl
from jax.experimental.pallas import tpu as pltpu
from jax.sharding import PartitionSpec as P

HEAD_DIM = 64
LANES = 128
MASKED = -1e30
LOG2E = math.log2(math.e)
MIB = 2**20
BF = jnp.bfloat16
F32 = jnp.float32
norm_epsilon = 1e-06
NT = (((1,), (1,)), ((), ()))
TN = (((0,), (0,)), ((), ()))


def cost(microseconds):
    return pl.CostEstimate(flops=int(microseconds * 1.1e9), bytes_accessed=0, transcendentals=0)


def stored_block(block, own, per_part):
    shift = per_part.bit_length() - 1
    part = lax.shift_right_logical(block, shift)
    return ((part ^ own) << shift) | (block & (per_part - 1))


def swap_halves(values):
    lane = lax.broadcasted_iota(jnp.int32, values.shape, 1)
    return jnp.where(lane % 64 < 32, pltpu.roll(values, 96, 1), pltpu.roll(values, 32, 1))


def mesh_spot(parts):
    d = lax.axis_index("dp")
    z = lax.axis_index("tensor")
    return d, z, d % 2, parts // 2


def partner_of(d, z, b, half):
    return d ^ (b // half), z ^ (b % half)


def remote_copy(source, target, sems, at, device):
    return pltpu.make_async_remote_copy(
        src_ref=source,
        dst_ref=target,
        send_sem=sems.at[2 * at],
        recv_sem=sems.at[2 * at + 1],
        device_id=device,
        device_id_type=pl.DeviceIdType.MESH,
    )


PIECES = 4


def in_pieces(source, target, sems, at, device, pieces=range(PIECES)):
    rows = source.shape[0] // PIECES
    return [
        remote_copy(
            source.at[k * rows : (k + 1) * rows, :], target.at[k * rows : (k + 1) * rows, :], sems, at + k, device
        )
        for k in pieces
    ]


def remote(source, target, sems, at, device):
    copy = remote_copy(source, target, sems, at, device)
    copy.start()
    return copy


def greet(devices):
    barrier = pltpu.get_barrier_semaphore()
    for device in devices:
        pl.semaphore_signal(barrier, inc=1, device_id=device, device_id_type=pl.DeviceIdType.MESH)
    pl.semaphore_wait(barrier, len(devices))


def project_kernel(normed_ref, weight_ref, cos_ref, sin_ref, out_ref, *, pairs):
    normed = normed_ref[...]
    cosine = cos_ref[...]
    sine = sin_ref[...]
    width = pairs * LANES
    for kind in range(3):
        weight = weight_ref[kind * width : (kind + 1) * width, :]
        part = lax.dot_general(normed, weight, NT, preferred_element_type=F32)
        for pair in range(pairs):
            cut = part[:, pair * LANES : (pair + 1) * LANES]
            if kind < 2:
                cut = cut * cosine + swap_halves(cut) * sine
            if kind == 0:
                cut = cut * (LOG2E * HEAD_DIM**-0.5)
            out_ref[pair * 3 + kind] = cut.astype(BF)


def project(normed_all, weight, cosine, sine, pairs):
    length, depth = normed_all.shape
    rows = 512
    return pl.pallas_call(
        functools.partial(project_kernel, pairs=pairs),
        grid=(length // rows,),
        in_specs=[
            pl.BlockSpec((rows, depth), lambda i: (i, 0)),
            pl.BlockSpec(weight.shape, lambda i: (0, 0)),
            pl.BlockSpec((rows, LANES), lambda i: (i, 0)),
            pl.BlockSpec((rows, LANES), lambda i: (i, 0)),
        ],
        out_specs=pl.BlockSpec((3 * pairs, rows, LANES), lambda i: (0, i, 0)),
        out_shape=jax.ShapeDtypeStruct((3 * pairs, length, LANES), BF),
        compiler_params=pltpu.CompilerParams(vmem_limit_bytes=40 * MIB),
        cost_estimate=cost(11),
        name="project",
    )(normed_all, weight, cosine, sine)


def attend_kernel(
    own_ref, low_ref, high_ref, q_ref, k_ref, v_ref, qmark_ref, kmark_ref, ctx_ref, lse_ref, keys, vals,
    *, bq, bk, per_part,
):
    step = pl.program_id(0)
    length = kmark_ref.shape[0]
    own = own_ref[0]

    @pl.when(step == 0)
    def _():
        lane = lax.broadcasted_iota(jnp.int32, (512, LANES), 1)

        @pl.loop(0, length // 512)
        def _(i):
            rows = pl.ds(pl.multiple_of(i * 512, 512), 512)
            keys[rows, :LANES] = k_ref[0, rows, :]
            keys[rows, LANES:] = kmark_ref[rows, :]
            v = v_ref[0, rows, :]
            one = jnp.ones_like(v)
            vals[0, rows, :] = jnp.where(lane < 64, v, one)
            vals[1, rows, :] = jnp.where(lane < 64, one, v)

    first = lax.broadcasted_iota(jnp.int32, (bq, LANES), 1) < 64
    q = q_ref[0]
    mark = qmark_ref[...]
    zero = jnp.zeros_like(q)
    queries = (
        jnp.concatenate([jnp.where(first, q, zero), mark], axis=1),
        jnp.concatenate([jnp.where(first, zero, q), mark], axis=1),
    )

    def body(j, carry):
        rows = pl.ds(pl.multiple_of(stored_block(j, own, per_part // bk) * bk, bk), bk)
        block = keys[rows, :]
        new = []
        for head in range(2):
            peak, total = carry[head]
            scores = lax.dot_general(queries[head], block, NT, preferred_element_type=F32)
            cuts = [scores[:, k * LANES : (k + 1) * LANES] for k in range(bk // LANES)]
            tallest = functools.reduce(jnp.maximum, cuts)
            higher = jnp.maximum(peak, jnp.max(tallest, axis=1, keepdims=True))
            weights = jnp.concatenate([jnp.exp2(cut - higher).astype(BF) for cut in cuts], axis=1)
            total = total * jnp.exp2(peak - higher) + jnp.dot(
                weights, vals[head, rows, :], preferred_element_type=F32
            )
            new.append((higher, total))
        return tuple(new)

    init = (jnp.full((bq, LANES), -3e38, F32), jnp.zeros((bq, LANES), F32))
    (peak_a, sum_a), (peak_b, sum_b) = lax.fori_loop(low_ref[step], high_ref[step], body, (init, init))
    weight_sum = pltpu.roll(jnp.where(first, sum_b, sum_a), 64, 1)
    ctx_ref[0] = (jnp.where(first, sum_a, sum_b) / weight_sum).astype(BF)
    lse_ref[...] = jnp.where(first, peak_a, peak_b) + jnp.log2(weight_sum)


def attend(qkv, pair, qmark, kmark, own, low, high, bq, bk, per_part):
    length = qmark.shape[0]
    row = lambda i, *_: (i, 0)
    whole = lambda i, *_: (0, 0)
    return pl.pallas_call(
        functools.partial(attend_kernel, bq=bq, bk=bk, per_part=per_part),
        grid_spec=pltpu.PrefetchScalarGridSpec(
            num_scalar_prefetch=3,
            grid=(length // bq,),
            in_specs=[
                pl.BlockSpec((1, bq, LANES), lambda i, *_: (3 * pair, i, 0)),
                pl.BlockSpec((1, length, LANES), lambda i, *_: (3 * pair + 1, 0, 0)),
                pl.BlockSpec((1, length, LANES), lambda i, *_: (3 * pair + 2, 0, 0)),
                pl.BlockSpec((bq, LANES), row),
                pl.BlockSpec((length, LANES), whole),
            ],
            out_specs=[
                pl.BlockSpec((1, bq, LANES), lambda i, *_: (i // (per_part // bq), i % (per_part // bq), 0)),
                pl.BlockSpec((bq, LANES), row),
            ],
            scratch_shapes=[pltpu.VMEM((length, 2 * LANES), BF), pltpu.VMEM((2, length, LANES), BF)],
        ),
        out_shape=[
            jax.ShapeDtypeStruct((length // per_part, per_part, LANES), BF),
            jax.ShapeDtypeStruct((length, LANES), F32),
        ],
        compiler_params=pltpu.CompilerParams(
            dimension_semantics=("arbitrary",), vmem_limit_bytes=48 * MIB
        ),
        cost_estimate=cost(35),
        name="attend",
    )(own, low, high, qkv, qkv, qkv, qmark, kmark)


def three_parts(value):
    high = value.astype(BF).astype(F32)
    rest = value - high
    middle = rest.astype(BF).astype(F32)
    return high, middle, (rest - middle).astype(BF).astype(F32)


def attend_back_kernel(
    own_ref, low_ref, high_ref, q_ref, k_ref, v_ref, do_ref, ctx_ref, lse_ref, qmark_ref, kmark_ref, cos_ref,
    sin_ref, out_ref, keys, vals, key_heads, query_heads, grad_heads, dq_sum,
    *, bq, bk, utt, per_part,
):
    length = kmark_ref.shape[0]
    own = own_ref[0]
    pb = 512
    lane = lax.broadcasted_iota(jnp.int32, (pb, LANES), 1)
    first = lane < 64

    @pl.loop(0, length // pb)
    def _(i):
        rows = pl.ds(pl.multiple_of(i * pb, pb), pb)
        at, within = i // (per_part // pb), pl.ds(pl.multiple_of(i % (per_part // pb) * pb, pb), pb)
        k = k_ref[0, rows, :]
        zero = jnp.zeros_like(k)
        mark = kmark_ref[rows, :]
        keys[rows, :LANES] = k
        keys[rows, LANES:] = mark
        vals[rows, :LANES] = v_ref[0, rows, :]
        vals[rows, LANES:] = mark
        q = q_ref[0, rows, :]
        grad = do_ref[at, within, :]
        qmark = qmark_ref[rows, :].astype(F32)
        lse = lse_ref[rows, :]
        product = grad.astype(F32) * ctx_ref[at, within, :].astype(F32)
        for head in range(2):
            mine = first if head == 0 else jnp.logical_not(first)
            key_heads[head, rows, :] = jnp.where(mine, k, zero)
            query_heads[head, rows, :LANES] = jnp.where(mine, q, zero)
            grad_heads[head, rows, :LANES] = jnp.where(mine, grad, zero)
            high, middle, low = three_parts(-lse[:, 64 * head : 64 * head + 1])
            query_heads[head, rows, LANES:] = jnp.where(
                lane == utt, high, jnp.where(lane == utt + 1, middle, jnp.where(lane == utt + 2, low, qmark))
            ).astype(BF)
            delta = jnp.sum(jnp.where(mine, product, 0.0), axis=1, keepdims=True)
            high, middle, low = three_parts(-delta)
            grad_heads[head, rows, LANES:] = jnp.where(
                lane == utt, high, jnp.where(lane == utt + 1, middle, jnp.where(lane == utt + 2, low, 0.0))
            ).astype(BF)
        dq_sum[rows, :] = jnp.zeros((pb, LANES), F32)

    @pl.loop(0, length // bk)
    def _(j):
        key_rows = pl.ds(pl.multiple_of(j * bk, bk), bk)
        key_block = keys[key_rows, :]
        value_block = vals[key_rows, :]

        def body(i, carry):
            dk, dv = carry
            rows = pl.ds(pl.multiple_of(stored_block(i, own, per_part // bq) * bq, bq), bq)
            dq = dq_sum[rows, :]
            for head in range(2):
                query = query_heads[head, rows, :]
                grad = grad_heads[head, rows, :]
                probs = jnp.exp2(lax.dot_general(key_block, query, NT, preferred_element_type=F32))
                pulled = lax.dot_general(value_block, grad, NT, preferred_element_type=F32)
                grad_scores = (probs * pulled).astype(BF)
                dv = dv + jnp.dot(probs.astype(BF), grad[:, :LANES], preferred_element_type=F32)
                dk = dk + jnp.dot(grad_scores, query[:, :LANES], preferred_element_type=F32)
                dq = dq + lax.dot_general(
                    grad_scores, key_heads[head, key_rows, :], TN, preferred_element_type=F32
                )
            dq_sum[rows, :] = dq
            return dk, dv

        zero = jnp.zeros((bk, LANES), F32)
        dk, dv = lax.fori_loop(low_ref[j], high_ref[j], body, (zero, zero))
        at, within = j // (per_part // bk), pl.ds(pl.multiple_of(j % (per_part // bk) * bk, bk), bk)
        out_ref[at, 2, within, :] = dv.astype(BF)
        dk = dk * (1.0 / LOG2E)
        out_ref[at, 1, within, :] = (dk * cos_ref[key_rows, :] - swap_halves(dk) * sin_ref[key_rows, :]).astype(BF)

    @pl.loop(0, length // pb)
    def _(i):
        rows = pl.ds(pl.multiple_of(i * pb, pb), pb)
        at, within = i // (per_part // pb), pl.ds(pl.multiple_of(i % (per_part // pb) * pb, pb), pb)
        dq = dq_sum[rows, :] * HEAD_DIM**-0.5
        out_ref[at, 0, within, :] = (dq * cos_ref[rows, :] - swap_halves(dq) * sin_ref[rows, :]).astype(BF)


def attend_back(
    qkv, pair, grad, ctx, lse, qmark, kmark, cosine, sine, own, low, high, bq, bk, utt, per_part
):
    length = qmark.shape[0]
    in_smem = pl.BlockSpec(memory_space=pltpu.SMEM)
    whole = pl.BlockSpec((length, LANES), lambda i: (0, 0))
    parts = length // per_part
    by_part = pl.BlockSpec((parts, per_part, LANES), lambda i: (0, 0, 0))
    cut = lambda kind: pl.BlockSpec((1, length, LANES), lambda i: (3 * pair + kind, 0, 0))
    wide = pltpu.VMEM((length, 2 * LANES), BF)
    return pl.pallas_call(
        functools.partial(attend_back_kernel, bq=bq, bk=bk, utt=utt, per_part=per_part),
        grid=(1,),
        in_specs=[in_smem] * 3 + [cut(0), cut(1), cut(2)] + [by_part] * 2 + [whole] * 5,
        out_specs=pl.BlockSpec((parts, 3, per_part, LANES), lambda i: (0, 0, 0, 0)),
        out_shape=jax.ShapeDtypeStruct((parts, 3, per_part, LANES), BF),
        scratch_shapes=[
            wide,
            wide,
            pltpu.VMEM((2, length, LANES), BF),
            pltpu.VMEM((2, length, 2 * LANES), BF),
            pltpu.VMEM((2, length, 2 * LANES), BF),
            pltpu.VMEM((length, LANES), F32),
        ],
        compiler_params=pltpu.CompilerParams(vmem_limit_bytes=56 * MIB),
        cost_estimate=cost(66),
        name="attend_back",
    )(own, low, high, qkv, qkv, qkv, grad, ctx, lse, qmark, kmark, cosine, sine)


def frame_marks(lengths, places, utt):
    ends = jnp.cumsum(lengths)
    starts = ends - lengths
    segment = jnp.sum((places[:, None] >= ends[None, :]).astype(jnp.int32), axis=1, dtype=jnp.int32)
    member = segment[:, None] == jnp.arange(utt, dtype=jnp.int32)[None, :]
    offsets = jnp.sum(jnp.where(member, starts[None, :], 0), axis=1, dtype=jnp.int32)
    return segment, member, offsets


def block_ranges(lengths, blocks, size, other):
    ends = jnp.cumsum(lengths)
    starts = ends - lengths
    at_first = blocks * size
    at_last = at_first + (size - 1)
    index = jnp.arange(lengths.shape[0], dtype=jnp.int32)
    seg_first = jnp.sum((at_first[:, None] >= ends[None]).astype(jnp.int32), axis=1)
    seg_last = jnp.sum((at_last[:, None] >= ends[None]).astype(jnp.int32), axis=1)
    low = jnp.sum(jnp.where(index[None] == seg_first[:, None], starts[None], 0), axis=1)
    high = jnp.sum(jnp.where(index[None] == seg_last[:, None], ends[None], 0), axis=1)
    return (low // other).astype(jnp.int32), ((high + other - 1) // other).astype(jnp.int32)


def feed_kernel(
    x_own_ref, cot_own_ref, cot_other_ref, weights_ref, heads_hbm,
    out_own_ref, out_other_ref, gin_own_ref, gin_other_ref, grads_ref, heads_out_hbm,
    x_other_ref, out_sum, gin_sum, local, sems, *, parts,
):
    step = pl.program_id(0)
    last = pl.num_programs(0) - 1
    d, z, core, half = mesh_spot(parts)
    beside = partner_of(d, z, half, half)

    eighth = d // 2 % 4 + 4 * core

    def heads_part(k):
        if k < parts:
            cut = heads_out_hbm.at[eighth, z]
            return remote_copy(cut, cut, sems, PIECES + k, (d, z ^ k))
        size = 1 << (k - parts)
        cut = heads_out_hbm.at[pl.ds(eighth // size * size, size)]
        return remote_copy(cut, cut, sems, PIECES + k, (d ^ (2, 4)[k - parts], z))

    @pl.when(step == 0)
    def _():
        greet([(d ^ bit, z) for bit in (1, 2, 4)] + [(d, z ^ k) for k in range(1, parts)])
        remote_copy(x_own_ref, x_other_ref, sems, 0, beside).start()
        copy = pltpu.make_async_copy(heads_hbm.at[:, eighth], heads_out_hbm.at[eighth, z], local)
        copy.start()
        copy.wait()
        for k in range(1, parts):
            heads_part(k).start()

    @pl.when(step == 1)
    def _():
        for k in range(1, parts):
            heads_part(k).wait()
        heads_part(parts).start()

    @pl.when(step == 2)
    def _():
        heads_part(parts).wait()
        heads_part(parts + 1).start()

    chunk, depth = weights_ref.shape[0] * weights_ref.shape[2], weights_ref.shape[3]
    up = weights_ref[:, 0].reshape(chunk, depth)
    down = weights_ref[:, 1].reshape(chunk, depth)
    root = math.sqrt(2.0 / math.pi)
    gup = gdown = None
    for side, (x_ref, cot_ref) in enumerate(((x_own_ref, cot_own_ref), (x_other_ref, cot_other_ref))):
        if side == 1:

            @pl.when(step == 0)
            def _():
                remote_copy(x_own_ref, x_other_ref, sems, 0, beside).wait()

        x = x_ref[...]
        cot = cot_ref[...]
        before = lax.dot_general(x, up, NT, preferred_element_type=F32)
        grad_act = lax.dot_general(cot, down, NT, preferred_element_type=F32)
        square = before * before
        bend = jnp.tanh(root * before * (1.0 + 0.044715 * square))
        half = 0.5 * (1.0 + bend)
        activated = (before * half).astype(BF)
        slope = half + 0.5 * before * (1.0 - bend * bend) * (root + (3.0 * 0.044715 * root) * square)
        grad_before = (grad_act * slope).astype(BF)
        out = jnp.dot(activated, down, preferred_element_type=F32)
        gin = jnp.dot(grad_before, up, preferred_element_type=F32)
        gd = lax.dot_general(activated, cot, TN, preferred_element_type=F32)
        gu = lax.dot_general(grad_before, x, TN, preferred_element_type=F32)
        gup = gu if side == 0 else gup + gu
        gdown = gd if side == 0 else gdown + gd

        out_to, gin_to = (out_own_ref, gin_own_ref) if side == 0 else (out_sum, gin_sum)

        @pl.when(step == 0)
        def _():
            out_to[...] = out
            gin_to[...] = gin

        @pl.when(step > 0)
        def _():
            out_to[...] += out
            gin_to[...] += gin

    per = weights_ref.shape[2]
    grads_ref[:, :per] = gup.astype(BF).reshape(-1, per, depth)
    grads_ref[:, per : 2 * per] = gdown.astype(BF).reshape(-1, per, depth)
    grads_ref[:, 2 * per :] = jnp.zeros(grads_ref[:, 2 * per :].shape, BF)

    @pl.when(step == last)
    def _():
        out_other_ref[...] = out_sum[...].astype(BF)
        gin_other_ref[...] = gin_sum[...].astype(BF)

        heads_part(parts + 1).wait()


def feed(x_own, cot_own, cot_other, weights, heads, spare, parts):
    frames, depth = x_own.shape
    groups, _, per, _ = weights.shape
    chunk = 512
    whole = pl.BlockSpec((frames, depth), lambda j: (0, 0), pipeline_mode=pl.Buffered(1))
    cut = pl.BlockSpec((chunk // per, 2, per, depth), lambda j: (j, 0, 0, 0))
    grads = pl.BlockSpec((chunk // per, 2 * per + spare, depth), lambda j: (j, 0, 0))
    shape = lambda *s: jax.ShapeDtypeStruct(*s)
    anywhere = pl.BlockSpec(memory_space=pl.ANY)
    return pl.pallas_call(
        functools.partial(feed_kernel, parts=parts),
        grid=(groups * per // chunk,),
        in_specs=[whole] * 3 + [cut, anywhere],
        out_specs=[whole] * 4 + [grads, anywhere],
        out_shape=[
            shape((frames, depth), F32),
            shape((frames, depth), BF),
            shape((frames, depth), F32),
            shape((frames, depth), BF),
            shape((groups, 2 * per + spare, depth), BF),
            shape((8, parts) + heads.shape[:1] + heads.shape[2:], BF),
        ],
        scratch_shapes=[
            pltpu.VMEM((frames, depth), BF),
            pltpu.VMEM((frames, depth), F32),
            pltpu.VMEM((frames, depth), F32),
            pltpu.SemaphoreType.DMA,
            pltpu.SemaphoreType.DMA((2 * (PIECES + parts + 3),)),
        ],
        compiler_params=pltpu.CompilerParams(
            dimension_semantics=("arbitrary",), vmem_limit_bytes=60 * MIB, collective_id=3, has_side_effects=True
        ),
        cost_estimate=cost(84),
        name="feed",
    )(x_own, cot_own, cot_other, weights, heads)


def spread(segment, table):
    masks = [segment == u for u in range(1, table.shape[0])]
    columns = []
    for k in range(table.shape[1] // LANES):
        cut = table[:, k * LANES : (k + 1) * LANES]
        out = jnp.broadcast_to(cut[0:1], segment.shape)
        for u, mask in enumerate(masks):
            out = jnp.where(mask, cut[u + 1 : u + 2], out)
        columns.append(out)
    return jnp.concatenate(columns, axis=1)


def collect(segment, values, utt):
    rows = []
    for u in range(utt):
        mask = segment == u
        rows.append(
            jnp.concatenate(
                [
                    jnp.sum(jnp.where(mask, values[:, k * LANES : (k + 1) * LANES], 0.0), axis=0, keepdims=True)
                    for k in range(values.shape[1] // LANES)
                ],
                axis=1,
            )
        )
    return jnp.concatenate(rows, axis=0)


def unit_norm(hidden):
    center = hidden - jnp.mean(hidden, axis=-1, keepdims=True)
    inverse = lax.rsqrt(jnp.mean(center * center, axis=-1, keepdims=True) + norm_epsilon)
    return center * inverse, inverse


def pull_norm(unit, inverse, grad, gain):
    pulled = grad * gain
    return (
        pulled
        - jnp.mean(pulled, axis=-1, keepdims=True)
        - unit * jnp.mean(pulled * unit, axis=-1, keepdims=True)
    ) * inverse


def join_kernel(*refs, pairs, parts):
    ctx_refs, refs = refs[: (pairs - 1) * parts], refs[(pairs - 1) * parts :]
    (
        last_hbm, w_out_ref, base_ref, base_in_ref, segment_ref, shift_ref, scale_ref,
        hidden_ref, normed_ref, last_out_hbm, last, local, sems,
    ) = refs
    step = pl.program_id(0)
    steps = pl.num_programs(0)
    d, z, core, half = mesh_spot(parts)
    part = core * half + z % half
    stays = z // half == core
    rows = hidden_ref.shape[0]

    def chunk(b, k):
        here = pl.ds(pl.multiple_of(k * rows, rows), rows)
        return remote_copy(
            last_hbm.at[b, here, :], last.at[b, here, :], sems, k * parts + b, partner_of(d, z, b, half)
        )

    own = pltpu.make_async_copy(last_hbm.at[0], last.at[0], local)

    @pl.when(step == 0)
    def _():
        own.start()
        greet([partner_of(d, z, b, half) for b in range(1, parts)])

        @pl.loop(0, steps)
        def _(k):
            for b in range(1, parts):
                chunk(b, k).start()

    hidden = jnp.where(stays, base_ref[...], base_in_ref[...]).astype(F32)
    for b in range(parts):
        for pair in range(pairs - 1):
            weights = w_out_ref[:, part ^ b].reshape(pairs * LANES, -1)[pair * LANES : (pair + 1) * LANES]
            hidden = hidden + jnp.dot(ctx_refs[pair * parts + b][...], weights, preferred_element_type=F32)

    @pl.when(step == 0)
    def _():
        own.wait()

    for b in range(1, parts):
        chunk(b, step).wait()
    here = pl.ds(pl.multiple_of(step * rows, rows), rows)
    for b in range(parts):
        weights = w_out_ref[:, part ^ b].reshape(pairs * LANES, -1)[(pairs - 1) * LANES :]
        hidden = hidden + jnp.dot(last[b, here, :], weights, preferred_element_type=F32)
    hidden_ref[...] = hidden
    unit, _ = unit_norm(hidden)
    segment = segment_ref[...]
    normed_ref[...] = (unit * (1.0 + spread(segment, scale_ref[...])) + spread(segment, shift_ref[...])).astype(BF)

    @pl.when(step == steps - 1)
    def _():
        copy = pltpu.make_async_copy(last, last_out_hbm, local)
        copy.start()
        copy.wait()


def join(ctx_blocks, last, w_out, base, base_in, segment, shift, scale, pairs, parts):
    frames, depth = base.shape
    rows = 256
    row = lambda i: (i, 0)
    wide = pl.BlockSpec((rows, depth), row)
    thin = pl.BlockSpec((rows, LANES), row)
    table = pl.BlockSpec(shift.shape, lambda i: (0, 0))
    anywhere = pl.BlockSpec(memory_space=pl.ANY)
    return pl.pallas_call(
        functools.partial(join_kernel, pairs=pairs, parts=parts),
        grid=(frames // rows,),
        in_specs=[thin] * len(ctx_blocks)
        + [anywhere, pl.BlockSpec(w_out.shape, lambda i: (0, 0, 0, 0)), wide, wide, thin]
        + [table] * 2,
        out_specs=[wide, wide, anywhere],
        out_shape=[
            jax.ShapeDtypeStruct((frames, depth), F32),
            jax.ShapeDtypeStruct((frames, depth), BF),
            jax.ShapeDtypeStruct(last.shape, BF),
        ],
        scratch_shapes=[
            pltpu.VMEM(last.shape, BF),
            pltpu.SemaphoreType.DMA,
            pltpu.SemaphoreType.DMA((2 * parts * (frames // rows),)),
        ],
        compiler_params=pltpu.CompilerParams(
            dimension_semantics=("arbitrary",), vmem_limit_bytes=40 * MIB, collective_id=5, has_side_effects=True
        ),
        cost_estimate=cost(18),
        name="join",
    )(*ctx_blocks, last, w_out, base, base_in, segment, shift, scale)


def turn_kernel(
    own_ref, gin_own_ref, gin_in_ref, out_own_ref, out_in_ref, hidden_ref, cot_ref, skips_ref, segment_ref, scale_ref,
    w_out_ref, grad_hidden_ref, low_ref, block_out_ref, sums_ref, *grad_context_refs, pairs, parts, utt,
):
    own = own_ref[0]
    hidden = hidden_ref[...]
    unit, inverse = unit_norm(hidden)
    segment = segment_ref[...]
    block_out_ref[0] = (hidden + out_own_ref[...] + out_in_ref[...].astype(F32)).astype(BF)
    block_out_ref[1] = skips_ref[...]
    grad = gin_own_ref[...] + gin_in_ref[...].astype(F32)
    grad_hidden = cot_ref[...].astype(F32) + pull_norm(unit, inverse, grad, 1.0 + spread(segment, scale_ref[...]))
    grad_hidden_ref[...] = grad_hidden
    low = grad_hidden.astype(BF)
    low_ref[...] = low
    for b in range(parts):
        part = lax.dot_general(low, w_out_ref[:, own ^ b].reshape(pairs * LANES, -1), NT, preferred_element_type=F32).astype(BF)
        for pair in range(pairs):
            grad_context_refs[b][pair] = part[:, pair * LANES : (pair + 1) * LANES]
    sums = jnp.concatenate([collect(segment, grad, utt), collect(segment, grad * unit, utt)], axis=0)

    @pl.when(pl.program_id(0) == 0)
    def _():
        sums_ref[...] = sums

    @pl.when(pl.program_id(0) > 0)
    def _():
        sums_ref[...] += sums


def turn(own, gin_own, gin_in, out_own, out_in, hidden, cot, skips, segment, scale, w_out, pairs, parts):
    frames, depth = hidden.shape
    utt = scale.shape[0]
    rows = 256
    row = lambda i, *_: (i, 0)
    wide = pl.BlockSpec((rows, depth), row)
    thin = pl.BlockSpec((rows, LANES), row)
    shape = lambda *s: jax.ShapeDtypeStruct(*s)
    return pl.pallas_call(
        functools.partial(turn_kernel, pairs=pairs, parts=parts, utt=utt),
        grid_spec=pltpu.PrefetchScalarGridSpec(
            num_scalar_prefetch=1,
            grid=(frames // rows,),
            in_specs=[wide] * 7
            + [thin, pl.BlockSpec(scale.shape, lambda i, *_: (0, 0)), pl.BlockSpec(w_out.shape, lambda i, *_: (0, 0, 0, 0))],
            out_specs=[wide] * 2
            + [pl.BlockSpec((2, rows, depth), lambda i, *_: (0, i, 0)), pl.BlockSpec((2 * utt, depth), lambda i, *_: (0, 0))]
            + [pl.BlockSpec((pairs, rows, LANES), lambda i, *_: (0, i, 0))] * parts,
        ),
        out_shape=[
            shape((frames, depth), F32),
            shape((frames, depth), BF),
            shape((2, frames, depth), BF),
            shape((2 * utt, depth), F32),
        ]
        + [shape((pairs, frames, LANES), BF)] * parts,
        compiler_params=pltpu.CompilerParams(
            dimension_semantics=("arbitrary",), vmem_limit_bytes=48 * MIB
        ),
        cost_estimate=cost(15),
        name="turn",
    )(own, gin_own, gin_in, out_own, out_in, hidden, cot, skips, segment, scale, w_out)


def out_grad_kernel(*refs, pairs, parts, columns, at_row):
    low_ref, ctx_refs, (last_ref, _, out_hbm, held, landing, local, sems) = refs[0], refs[1:-7], refs[-7:]
    d, z, core, half = mesh_spot(parts)
    part = core * half + z % half
    beside = partner_of(d, z, half, half)
    per = pairs * LANES // (2 * columns)
    greet([beside])
    if per < held.shape[3]:
        held[...] = jnp.zeros_like(held)
    low = low_ref[...]
    for b in range(parts):
        for pair in range(pairs):
            ctx = last_ref[b] if pair == pairs - 1 else ctx_refs[pair * parts + b][...]
            grad = lax.dot_general(ctx, low, TN, preferred_element_type=F32)
            for k in range(LANES // per):
                spot = pair * (LANES // per) + k
                held[spot % 2, spot // 2, part ^ b, :per, :] = grad[k * per : (k + 1) * per].astype(BF)
    remote(held.at[1 - core], landing, sems, 0, beside).wait()

    @pl.loop(0, columns)
    def _(i):
        held[core, i] = (held[core, i].astype(F32) + landing[i].astype(F32)).astype(BF)

    copies = []
    for i in range(columns):
        copy = pltpu.make_async_copy(
            held.at[core, i], out_hbm.at[i * parts : (i + 1) * parts, at_row:, :], local.at[i]
        )
        copy.start()
        copies.append(copy)
    for copy in copies:
        copy.wait()


def out_grad(low, ctx_blocks, last, grad_feed, at_row, pairs, parts, columns):
    depth = low.shape[1]
    spare = grad_feed.shape[1] - at_row
    vmem = pl.BlockSpec(memory_space=pltpu.VMEM)
    anywhere = pl.BlockSpec(memory_space=pl.ANY)
    return pl.pallas_call(
        functools.partial(out_grad_kernel, pairs=pairs, parts=parts, columns=columns, at_row=at_row),
        in_specs=[vmem] * (2 + len(ctx_blocks)) + [anywhere],
        out_specs=anywhere,
        out_shape=jax.ShapeDtypeStruct(grad_feed.shape, BF),
        scratch_shapes=[
            pltpu.VMEM((2, columns, parts, spare, depth), BF),
            pltpu.VMEM((columns, parts, spare, depth), BF),
            pltpu.SemaphoreType.DMA((columns,)),
            pltpu.SemaphoreType.DMA((2,)),
        ],
        input_output_aliases={2 + len(ctx_blocks): 0},
        compiler_params=pltpu.CompilerParams(
            collective_id=4, has_side_effects=True, vmem_limit_bytes=32 * MIB
        ),
        cost_estimate=cost(9),
        name="out_grad",
    )(low, *ctx_blocks, last, grad_feed)


class Sender:
    def __init__(self, sems, used=0):
        self.sems, self.used = sems, used
        self.d, self.z = lax.axis_index("dp"), lax.axis_index("tensor")

    def device(self, axis, bit):
        return (self.d ^ bit, self.z) if axis == "dp" else (self.d, self.z ^ bit)

    def side(self, axis, bit):
        return ((self.d if axis == "dp" else self.z) // bit) % 2

    def take(self, count):
        self.used += count
        return self.used - count

    def send(self, source, target, axis, bit):
        return remote(source, target, self.sems, self.take(1), self.device(axis, bit))


def rows_at(start, size):
    return pl.ds(pl.multiple_of(start, 16), size)


def few_rows(size):
    while size > 128:
        size //= 2
    return size


def add_rows(target, start, landing, landing_at, size):
    step = few_rows(size)

    @pl.loop(0, size // step)
    def _(i):
        here = rows_at(start + i * step, step)
        there = landing[rows_at(landing_at + i * step, step), :].astype(F32)
        target[here, :] = (target[here, :].astype(F32) + there).astype(target.dtype)


def sum_tree(sender, buffer, landing, down, turn_round, up, out, offset):
    size = buffer.shape[0] // 2
    starts, begin, kept = [0, size], [0, size], []
    for step in range(len(down[0])):
        kept.append(list(starts))
        size //= 2
        copies = []
        for side in range(2):
            axis, bit = down[side][step]
            upper = sender.side(axis, bit)
            lose = starts[side] + (1 - upper) * size
            copies.append(
                sender.send(buffer.at[rows_at(lose, size), :], landing.at[rows_at(begin[side], size), :], axis, bit)
            )
            starts[side] = starts[side] + upper * size
        yield
        for side in range(2):
            copies[side].wait()
            add_rows(buffer, starts[side], landing, begin[side], size)
            begin[side] += size
    yield from turn_round(starts, size)
    for step in reversed(range(len(down[0]))):
        copies = []
        for side in range(2):
            mine = out.at[rows_at(offset + starts[side], size), :]
            copies.append(sender.send(mine, mine, *up[side][step]))
        yield
        for side in range(2):
            copies[side].wait()
        starts = kept[step]
        size *= 2


def gather_rows(sender, own_hbm, out, semaphore):
    columns = out.shape[0] // 2
    slot = sender.d // 2 + columns * (sender.d % 2)
    copy = pltpu.make_async_copy(own_hbm, out.at[slot], semaphore)
    copy.start()
    yield
    copy.wait()
    size = 1
    while size < 2 * columns:
        cut = out.at[pl.ds(slot // size * size, size)]
        copy = sender.send(cut, cut, "dp", 2 * size if size < columns else 1)
        yield
        copy.wait()
        size *= 2


def spread_sums(sender, own, held, out, parts):
    half = parts // 2
    slot = (sender.d // 2) * 2 + sender.z // half
    held[0] = own
    group = [("dp", 1)] + [("tensor", 1 << k) for k in range(parts.bit_length() - 2)]
    for at, (axis, bit) in enumerate(group):
        copy = sender.send(held.at[2 * at], held.at[2 * at + 1], axis, bit)
        yield
        copy.wait()
        held[2 * at + 2] = held[2 * at] + held[2 * at + 1]
    out[pl.ds(slot, 1)] = held[pl.ds(2 * len(group), 1)]
    size = 1
    rows_all = out.shape[0]
    for axis, bit in [("tensor", half)] + [("dp", 1 << k) for k in range(1, rows_all.bit_length() - 1)]:
        mine = out.at[pl.ds(slot // size * size, size)]
        copy = sender.send(mine, mine, axis, bit)
        yield
        copy.wait()
        size *= 2


def run_all(running):
    for work in list(running):
        try:
            next(work)
        except StopIteration:
            running.remove(work)


def bits_of(rows_all, parts):
    dp_bits = [1 << k for k in range(1, rows_all.bit_length() - 1)]
    return dp_bits, [1 << k for k in reversed(range(parts.bit_length() - 1))]


def finish_kernel(*refs, pairs, parts, utt, rows_all):
    cut = (pairs - 1) * parts
    prev_hbm, refs = refs[:cut], refs[cut:]
    own_hbm, refs = refs[:pairs], refs[pairs:]
    (
        normed_hbm, weight_hbm, base_hbm, base_in_hbm, grad_hbm, inputs_hbm, shard_hbm, segment_ref, scale_ref,
        grad_base_ref, qkv_ref, sums_ref, shards_ref, inputs_in_hbm,
        prev, own, normed, weight, base, grad_hidden, arrived, total, qkv_held, qkv_in, loads, sems,
    ) = refs
    d, z, core, half = mesh_spot(parts)
    part = core * half + z % half
    stays = z // half == core
    frames = normed.shape[1]
    width = pairs * LANES

    there = ((d - core) + z // half, core * half + z % half)
    dp_bits, _ = bits_of(rows_all, parts)
    near = [partner_of(d, z, b, half) for b in range(1, parts)] + [(d, z ^ half)] + [(d ^ bit, z) for bit in dp_bits]
    barrier = pltpu.get_barrier_semaphore()
    for device in near:
        pl.semaphore_signal(barrier, inc=1, device_id=device, device_id_type=pl.DeviceIdType.MESH)

    @pl.when(jnp.logical_not(stays))
    def _():
        pl.semaphore_signal(barrier, inc=1, device_id=there, device_id_type=pl.DeviceIdType.MESH)
        pl.semaphore_wait(barrier, len(near) + 1)

    @pl.when(stays)
    def _():
        pl.semaphore_wait(barrier, len(near))

    sends = []
    order = [b for b in range(1, parts) if b % half] + [b for b in range(1, parts) if b % half == 0]
    for b in order:
        sends.append(
            (b, remote(own_hbm[-1].at[b], arrived.at[b - 1], sems, b - 1, partner_of(d, z, b, half)))
        )

    @pl.when(jnp.logical_not(stays))
    def _():
        for copy in in_pieces(inputs_hbm, inputs_in_hbm, sems, parts, there):
            copy.start()

    def load(at, source, target):
        copy = pltpu.make_async_copy(source, target, loads.at[at])
        copy.start()
        return copy

    first = [load(0, normed_hbm, normed)]
    for pair in range(pairs):
        first.append(load(1 + pair, own_hbm[pair], own.at[pair]))
    at = 1 + pairs
    four = pl.ds(core * 4, 4)
    second = [
        load(at, weight_hbm.at[four], weight.at[four]),
        remote(weight_hbm.at[four], weight.at[four], sems, parts - 1, (d ^ 1, z)),
    ]
    for k in range(cut):
        second.append(load(at + 1 + k, prev_hbm[k], prev.at[k]))
    at += 1 + cut
    third = [load(at, grad_hbm, grad_hidden)]

    @pl.when(stays)
    def _():
        pltpu.make_async_copy(base_hbm, base, loads.at[at + 1]).start()

    @pl.when(jnp.logical_not(stays))
    def _():
        pltpu.make_async_copy(base_in_hbm, base, loads.at[at + 1]).start()

    sender = Sender(sems, parts + PIECES)
    running = [gather_rows(sender, shard_hbm, shards_ref, loads.at[len(own_hbm) + cut + 4])]
    run_all(running)
    for copy in first:
        copy.wait()
    run_all(running)
    for kind in range(3):
        for pair in range(pairs):

            def gather(b, carry):
                return carry + lax.dot_general(own[pair, b, kind], normed[b], TN, preferred_element_type=F32)

            grad = lax.fori_loop(0, parts, gather, jnp.zeros((LANES, normed.shape[2]), F32)).astype(BF)
            wide = qkv_held.shape[1]
            for k in range(normed.shape[2] // wide):
                at_row = k * 3 * width + kind * width + pair * LANES
                qkv_held[at_row : at_row + LANES, :] = grad[:, k * wide : (k + 1) * wide]

    down = [
        [("dp", bit) for bit in dp_bits] + [("tensor", half)],
        [("dp", bit) for bit in reversed(dp_bits)] + [("tensor", half)],
    ]

    def go_home(starts, size):
        at_sem = sender.take(2)

        def copies():
            return [
                remote_copy(
                    qkv_held.at[rows_at(starts[side], size), :],
                    qkv_ref.at[rows_at(starts[side], size), :],
                    sems,
                    at_sem + side,
                    there,
                )
                for side in range(2)
            ]

        @pl.when(stays)
        def _():
            for side in range(2):
                here = rows_at(starts[side], size)
                qkv_ref[here, :] = qkv_held[here, :]

        @pl.when(jnp.logical_not(stays))
        def _():
            for copy in copies():
                copy.start()

        yield

        @pl.when(jnp.logical_not(stays))
        def _():
            for copy in copies():
                copy.wait()

        for side in range(2):
            starts[side] = starts[side] + (core - z // half) * size

    up = [line[:-1] + [("dp", 1)] for line in down]
    running.append(sum_tree(sender, qkv_held, qkv_in, down, go_home, up, qkv_ref, 0))
    run_all(running)

    for copy in second:
        copy.wait()
    rows = 256

    def add_block(source, b, pair, fresh):
        weights = jnp.concatenate(
            [weight[:, part ^ b, kind * pairs + pair].reshape(LANES, -1) for kind in range(3)],
            axis=0,
        )

        @pl.loop(0, frames // rows)
        def _(i):
            here = pl.ds(pl.multiple_of(i * rows, rows), rows)
            block = jnp.concatenate([source[kind, here, :] for kind in range(3)], axis=1)
            term = jnp.dot(block, weights, preferred_element_type=F32)
            if fresh:
                total[here, :] = term
            else:
                total[here, :] += term

    add_block(own.at[pairs - 1, 0], 0, pairs - 1, True)
    run_all(running)
    for pair in range(pairs - 1):
        for b in range(parts):
            add_block(prev.at[pair * parts + b], b, pair, False)
            if b % 2:
                run_all(running)
    for b, copy in sorted(sends, key=lambda item: (item[0] % half, item[0])):
        copy.wait()
        add_block(arrived.at[b - 1], b, pairs - 1, False)
        run_all(running)

    for copy in third:
        copy.wait()
    pltpu.make_async_copy(base_hbm, base, loads.at[at + 1]).wait()
    sums_ref[...] = jnp.zeros_like(sums_ref)

    @pl.loop(0, frames // rows)
    def _(i):
        here = pl.ds(pl.multiple_of(i * rows, rows), rows)
        unit, inverse = unit_norm(base[here, :].astype(F32))
        grad = total[here, :]
        segment = segment_ref[here, :]
        pulled = pull_norm(unit, inverse, grad, 1.0 + spread(segment, scale_ref[...]))
        grad_base_ref[here, :] = (grad_hidden[here, :] + pulled).astype(BF)
        sums_ref[...] += jnp.concatenate([collect(segment, grad, utt), collect(segment, grad * unit, utt)], axis=0)

    while running:
        run_all(running)

    @pl.when(jnp.logical_not(stays))
    def _():
        for copy in in_pieces(inputs_hbm, inputs_in_hbm, sems, parts, there):
            copy.wait()


def finish(
    prev, own, normed_all, weight, base, base_in, grad_hidden, inputs, shard, segment, scale, pairs, parts, rows_all
):
    frames, depth = base.shape
    utt = scale.shape[0]
    units = 3 * pairs * LANES
    wide = depth
    while units * depth // wide % (16 * rows_all * 2):
        wide //= 2
    qkv_shape = (units * depth // wide, wide)
    copies = parts + 2 + PIECES + 6 * rows_all.bit_length() + parts.bit_length()
    anywhere = pl.BlockSpec(memory_space=pl.ANY)
    vmem = pl.BlockSpec(memory_space=pltpu.VMEM)
    shape = lambda *s: jax.ShapeDtypeStruct(*s)
    block = (3, frames, LANES)
    return pl.pallas_call(
        functools.partial(finish_kernel, pairs=pairs, parts=parts, utt=utt, rows_all=rows_all),
        in_specs=[anywhere] * (len(prev) + pairs + 7) + [vmem] * 2,
        out_specs=[vmem] * 4 + [anywhere],
        out_shape=[
            shape((frames, depth), BF),
            shape(qkv_shape, BF),
            shape((2 * utt, depth), F32),
            shape((rows_all,) + shard.shape, BF),
            shape((frames, depth), BF),
        ],
        scratch_shapes=[
            pltpu.VMEM((max(len(prev), 1),) + block, BF),
            pltpu.VMEM((pairs, parts) + block, BF),
            pltpu.VMEM(normed_all.shape, BF),
            pltpu.VMEM(weight.shape, BF),
            pltpu.VMEM((frames, depth), BF),
            pltpu.VMEM((frames, depth), F32),
            pltpu.VMEM((parts - 1,) + block, BF),
            pltpu.VMEM((frames, depth), F32),
            pltpu.VMEM(qkv_shape, BF),
            pltpu.VMEM(qkv_shape, BF),
            pltpu.SemaphoreType.DMA((5 + pairs + len(prev),)),
            pltpu.SemaphoreType.DMA((2 * copies,)),
        ],
        compiler_params=pltpu.CompilerParams(
            collective_id=1, has_side_effects=True, vmem_limit_bytes=56 * MIB
        ),
        cost_estimate=cost(60),
        name="finish",
    )(*prev, *own, normed_all, weight, base, base_in, grad_hidden, inputs, shard, segment, scale)


def sums_kernel(
    inputs_hbm, inputs_in_hbm, skips_hbm, skips_in_hbm, grad_ref, sums_ref, skip_out_ref, sums_out_ref, grad_in_hbm,
    frames_in, away, held, first_in, half_in, sums_in, loads, sems, *, rows_all, parts,
):
    d, z, core, half = mesh_spot(parts)
    stays = z // half == core
    leaves = jnp.logical_not(stays)
    dp_bits, z_bits = bits_of(rows_all, parts)
    there = ((d - core) + z // half, core * half + z % half)
    depth = grad_ref.shape[1]
    half_rows, width = held.shape

    for at, (source, source_in) in enumerate(((inputs_hbm, inputs_in_hbm), (skips_hbm, skips_in_hbm))):
        slot = frames_in.at[1 - core if at == 0 else core]

        @pl.when(stays)
        def _():
            pltpu.make_async_copy(source, slot, loads.at[at]).start()

        @pl.when(leaves)
        def _():
            pltpu.make_async_copy(source_in, slot, loads.at[at]).start()

    sender = Sender(sems, PIECES)
    near = [("dp", 1)] + [("dp", bit) for bit in dp_bits] + [("tensor", bit) for bit in z_bits]
    barrier = pltpu.get_barrier_semaphore()
    for axis, bit in near:
        pl.semaphore_signal(
            barrier, inc=1, device_id=sender.device(axis, bit), device_id_type=pl.DeviceIdType.MESH
        )

    @pl.when(leaves)
    def _():
        pl.semaphore_signal(barrier, inc=1, device_id=there, device_id_type=pl.DeviceIdType.MESH)
        pl.semaphore_wait(barrier, len(near) + 1)

    @pl.when(stays)
    def _():
        pl.semaphore_wait(barrier, len(near))

    def start_move(k):
        @pl.when(leaves)
        def _():
            in_pieces(grad_ref, grad_in_hbm, sems, 0, there, [k])[0].start()

    def settle(starts, size):
        for side in range(2):
            skip_out_ref[rows_at(offset + starts[side], size), :] = held[rows_at(starts[side], size), :]
        yield

    offset = core * half_rows

    def skips():
        for slot in range(2):
            pltpu.make_async_copy(inputs_hbm, frames_in.at[slot], loads.at[slot]).wait()
        for slot, target in ((0, away), (1, held)):

            @pl.loop(0, depth // 256)
            def _(i):
                cut = frames_in[slot, :, pl.ds(pl.multiple_of(i * 256, 256), 256)]
                grad = lax.dot_general(cut, grad_ref[...], TN, preferred_element_type=F32).astype(BF)
                for k in range(depth // width):
                    target[rows_at(k * depth + i * 256, 256), :] = grad[:, k * width : (k + 1) * width]

            if slot == 0:
                copy = sender.send(away, first_in, "dp", 1)
                yield
        copy.wait()
        add_rows(held, 0, first_in, 0, half_rows)
        down = [
            [("dp", bit) for bit in dp_bits] + [("tensor", bit) for bit in z_bits],
            [("dp", bit) for bit in reversed(dp_bits)] + [("tensor", bit) for bit in z_bits],
        ]
        yield from sum_tree(sender, held, half_in, down, settle, down, skip_out_ref, offset)
        mine = skip_out_ref.at[rows_at(offset, half_rows), :]
        copy = sender.send(mine, mine, "dp", 1)
        yield
        copy.wait()

    running = [skips(), spread_sums(sender, sums_ref[...], sums_in, sums_out_ref, parts)]
    rounds = 0
    later = 1 + len(dp_bits) + 2 * len(z_bits) + 1
    while running:
        if rounds in (0, 1, later, later + 1):
            start_move(rounds if rounds < 2 else rounds - later + 2)
        rounds += 1
        run_all(running)

    @pl.when(leaves)
    def _():
        for copy in in_pieces(grad_ref, grad_in_hbm, sems, 0, there):
            copy.wait()


def sums(inputs, inputs_in, skips, skips_in, grad_base, utterance_sums, rows_all, parts):
    frames, depth = inputs.shape
    devices = rows_all * parts
    width = min(depth, depth * depth // (16 * devices))
    half_rows = depth * depth // width
    stages = rows_all.bit_length() + parts.bit_length() - 3
    copies = PIECES + 2 + 4 * stages + rows_all.bit_length() + parts.bit_length()
    vmem = pl.BlockSpec(memory_space=pltpu.VMEM)
    anywhere = pl.BlockSpec(memory_space=pl.ANY)
    shape = lambda *s: jax.ShapeDtypeStruct(*s)
    skip_sum, all_sums, grad_base_in = pl.pallas_call(
        functools.partial(sums_kernel, rows_all=rows_all, parts=parts),
        in_specs=[anywhere] * 4 + [vmem] * 2,
        out_specs=[vmem] * 2 + [anywhere],
        out_shape=[
            shape((2 * half_rows, width), BF),
            shape((rows_all,) + utterance_sums.shape, F32),
            shape((frames, depth), BF),
        ],
        scratch_shapes=[pltpu.VMEM((2, frames, depth), BF)]
        + [pltpu.VMEM((half_rows, width), BF)] * 4
        + [
            pltpu.VMEM((2 * parts.bit_length() - 1,) + utterance_sums.shape, F32),
            pltpu.SemaphoreType.DMA((2,)),
            pltpu.SemaphoreType.DMA((2 * copies,)),
        ],
        compiler_params=pltpu.CompilerParams(
            collective_id=0, has_side_effects=True, vmem_limit_bytes=56 * MIB
        ),
        cost_estimate=cost(100),
        name="sums",
    )(inputs, inputs_in, skips, skips_in, grad_base, utterance_sums)
    skip_sum = skip_sum.reshape(2, depth // width, depth, width)
    skip_sum = jnp.transpose(skip_sum, (0, 2, 1, 3)).reshape(2, depth, depth)
    return skip_sum, all_sums, grad_base_in


def spread_out_kernel(shard_ref, up_ref, down_ref):
    per = down_ref.shape[0]
    rows = shard_ref[0].astype(F32)
    up_ref[...] = rows[:per].T
    down_ref[...] = rows[per : 2 * per]


def spread_out(shards, per):
    count, _, depth = shards.shape
    units = count * per
    if per % LANES:
        up = jnp.transpose(shards[:, :per].reshape(units, depth)).astype(F32)
        return up, shards[:, per : 2 * per].reshape(units, depth).astype(F32)
    return pl.pallas_call(
        spread_out_kernel,
        grid=(count,),
        in_specs=[pl.BlockSpec((1,) + shards.shape[1:], lambda i: (i, 0, 0))],
        out_specs=[pl.BlockSpec((depth, per), lambda i: (0, i)), pl.BlockSpec((per, depth), lambda i: (i, 0))],
        out_shape=[jax.ShapeDtypeStruct((depth, units), F32), jax.ShapeDtypeStruct((units, depth), F32)],
        compiler_params=pltpu.CompilerParams(vmem_limit_bytes=24 * MIB),
        cost_estimate=cost(4),
        name="spread_out",
    )(shards)


def front_kernel(
    ends_ref, inputs_ref, skips_ref, w_in_ref, w_res_ref, segment_ref, shift_ref, scale_ref, rate_ref, weight_hbm, w_out_ref,
    base_ref, out_ref, cos_ref, sin_ref, qmark_ref, kmark_ref, weight_in_hbm, w_out_all_ref, away, local, sems,
    *, parts, utt,
):
    d, z, core, half = mesh_spot(parts)
    stays = z // half == core
    leaves = jnp.logical_not(stays)
    there = ((d - core) + z // half, core * half + z % half)
    frames = base_ref.shape[0]
    rows = 256
    chunks = frames // rows

    barrier = pltpu.get_barrier_semaphore()
    near = [partner_of(d, z, b, half) for b in range(1, half + 1)] + [(d ^ bit, z) for bit in (2, 4, 6)]
    near += [(d, z ^ k) for k in range(half, parts)]
    for device in near:
        pl.semaphore_signal(barrier, inc=1, device_id=device, device_id_type=pl.DeviceIdType.MESH)

    @pl.when(leaves)
    def _():
        pl.semaphore_signal(barrier, inc=1, device_id=there, device_id_type=pl.DeviceIdType.MESH)
        pl.semaphore_wait(barrier, len(near) + 1)

    @pl.when(stays)
    def _():
        pl.semaphore_wait(barrier, len(near))

    def here(k):
        return pl.ds(pl.multiple_of(k * rows, rows), rows)

    def copy(kind, k, source, target, device):
        at = kind * chunks + k
        return pltpu.make_async_remote_copy(
            src_ref=source,
            dst_ref=target,
            send_sem=sems.at[2 * at],
            recv_sem=sems.at[2 * at + 1],
            device_id=device,
            device_id_type=pl.DeviceIdType.MESH,
        )

    def moving(k):
        return copy(0, k, away.at[here(k), :], out_ref.at[0, here(k), :], there)

    quarter = weight_hbm.shape[0] // 4
    column = d // 2 % 4

    def weight_part(k):
        cut = pl.ds(pl.multiple_of((column ^ k) * quarter, 16), quarter)
        if k == 0:
            return copy(parts, 0, weight_hbm.at[cut, :], weight_in_hbm.at[cut, :], there)
        own = pl.ds(pl.multiple_of(column * quarter, 16), quarter)
        return copy(parts, k, weight_in_hbm.at[own, :], weight_in_hbm.at[own, :], (d ^ (2 * k), z))

    @pl.when(leaves)
    def _():
        weight_part(0).start()

    @pl.when(stays)
    def _():
        pltpu.make_async_copy(weight_hbm, weight_in_hbm, local).start()

    eighth = d // 2 % 4 + 4 * core
    per = w_out_all_ref.shape[2]
    w_out_all_ref[eighth, z] = w_out_ref[pl.ds(pl.multiple_of(eighth * per, 16), per), :]

    def w_out_part(k):
        if k < parts:
            cut = w_out_all_ref.at[eighth, z]
            return copy(parts, 3 + k, cut, cut, (d, z ^ k))
        size = 1 << (k - parts)
        cut = w_out_all_ref.at[pl.ds(eighth // size * size, size)]
        return copy(parts, 3 + k, cut, cut, (d ^ (2, 4, 1)[k - parts], z))

    for k in range(1, parts):
        w_out_part(k).start()

    def across(b, k):
        return copy(b, k, out_ref.at[0, here(k), :], out_ref.at[b, here(k), :], partner_of(d, z, b, half))

    def beside(b, k):
        return copy(
            half + b, k, out_ref.at[b, here(k), :], out_ref.at[half + b, here(k), :], partner_of(d, z, half, half)
        )

    def spread_own(k):
        for b in range(1, half):
            across(b, k).start()
        beside(0, k).start()

    @pl.loop(0, chunks)
    def _(k):
        at = here(k)
        base = jnp.dot(inputs_ref[at, :], w_in_ref[...], preferred_element_type=F32)
        base = base + jnp.dot(skips_ref[at, :], w_res_ref[...], preferred_element_type=F32)
        base_ref[at, :] = base.astype(BF)
        unit, _ = unit_norm(base)
        segment = segment_ref[at, :]
        normed = (unit * (1.0 + spread(segment, scale_ref[...])) + spread(segment, shift_ref[...])).astype(BF)

        @pl.when(stays)
        def _():
            out_ref[0, at, :] = normed
            spread_own(k)

        @pl.when(leaves)
        def _():
            away[at, :] = normed
            moving(k).start()

    part = core * half + z % half

    @pl.loop(0, parts * chunks)
    def _(i):
        at = here(i)
        place = (part ^ (i // chunks)) * frames + (i % chunks) * rows
        place = place + lax.broadcasted_iota(jnp.int32, (rows, LANES), 0)
        lane = lax.broadcasted_iota(jnp.int32, (rows, LANES), 1)
        segment = jnp.zeros((rows, LANES), jnp.int32)
        start = jnp.zeros((rows, LANES), jnp.int32)
        for u in range(utt - 1):
            past = place >= ends_ref[u]
            segment = jnp.where(past, u + 1, segment)
            start = jnp.where(past, ends_ref[u], start)
        angle = (place - start).astype(F32) * rate_ref[0:1, :]
        cos_ref[at, :] = jnp.cos(angle)
        sin_ref[at, :] = jnp.sin(angle) * rate_ref[1:2, :]
        other = jnp.logical_and(lane < utt, lane != segment)
        qmark_ref[at, :] = jnp.where(other, MASKED, 0.0).astype(BF)
        shown = jnp.where(lane < utt + 3, 1.0, 0.0)
        kmark_ref[at, :] = jnp.where(other, 0.0, shown).astype(BF)

    for k in range(1, parts):
        w_out_part(k).wait()
    w_out_part(parts).start()

    @pl.when(leaves)
    def _():
        weight_part(0).wait()
        for k in range(1, 4):
            weight_part(k).start()

        @pl.loop(0, chunks)
        def _(k):
            moving(k).wait_recv()
            spread_own(k)

    w_out_part(parts).wait()
    w_out_part(parts + 1).start()

    @pl.loop(0, chunks)
    def _(k):
        for b in range(1, half):
            across(b, k).wait_recv()
            beside(b, k).start()

    w_out_part(parts + 1).wait()
    w_out_part(parts + 2).start()

    @pl.loop(0, chunks)
    def _(k):
        for b in range(half):
            beside(b, k).wait_recv()
            beside(b, k).wait_send()
        for b in range(1, half):
            across(b, k).wait_send()

    @pl.when(leaves)
    def _():
        @pl.loop(0, chunks)
        def _(k):
            moving(k).wait_send()

        for k in range(1, 4):
            weight_part(k).wait()

    @pl.when(stays)
    def _():
        pltpu.make_async_copy(weight_hbm, weight_in_hbm, local).wait()

    w_out_part(parts + 2).wait()


def front(ends, inputs, skips, w_in, w_res, segment, shift, scale, rate, weight, w_out, parts):
    frames, depth = inputs.shape
    utt = ends.shape[0]
    vmem = pl.BlockSpec(memory_space=pltpu.VMEM)
    return pl.pallas_call(
        functools.partial(front_kernel, parts=parts, utt=utt),
        in_specs=[pl.BlockSpec(memory_space=pltpu.SMEM)] + [vmem] * 8 + [pl.BlockSpec(memory_space=pl.ANY), vmem],
        out_specs=[vmem] * 6 + [pl.BlockSpec(memory_space=pl.ANY), vmem],
        out_shape=[
            jax.ShapeDtypeStruct((frames, depth), BF),
            jax.ShapeDtypeStruct((parts, frames, depth), BF),
            jax.ShapeDtypeStruct((parts * frames, LANES), F32),
            jax.ShapeDtypeStruct((parts * frames, LANES), F32),
            jax.ShapeDtypeStruct((parts * frames, LANES), BF),
            jax.ShapeDtypeStruct((parts * frames, LANES), BF),
            jax.ShapeDtypeStruct(weight.shape, BF),
            jax.ShapeDtypeStruct((8, parts, w_out.shape[0] // 8, depth), BF),
        ],
        scratch_shapes=[
            pltpu.VMEM((frames, depth), BF),
            pltpu.SemaphoreType.DMA,
            pltpu.SemaphoreType.DMA((2 * (parts * (frames // 256) + 6 + parts),)),
        ],
        compiler_params=pltpu.CompilerParams(
            collective_id=2, has_side_effects=True, vmem_limit_bytes=48 * MIB
        ),
        cost_estimate=cost(75),
        name="front",
    )(ends, inputs, skips, w_in, w_res, segment, shift, scale, rate, weight, w_out)


def dot(a, b, dims=(((1,), (0,)), ((), ()))):
    return lax.dot_general(a, b, dims, preferred_element_type=F32)


def after(value, token):
    return lax.optimization_barrier((value, token))[0]


def on_device(
    inputs, skip_input, lengths, time_steps, w_skip_in, w_skip_res, w_ada, w_qkv, w_out, w_up, w_down, cotangent
):
    parts = lax.axis_size("tensor")
    rows_all = lax.axis_size("dp")
    half = parts // 2
    columns = rows_all // 2
    d = lax.axis_index("dp")
    z = lax.axis_index("tensor")
    core, column = d % 2, d // 2
    stays = z // half == core
    part = core * half + z % half
    inputs, skip_input, cotangent = inputs[0], skip_input[0], cotangent[0]
    frames, depth = inputs.shape
    length = frames * parts
    ws = w_qkv.shape[2]
    pairs = ws // LANES
    utt = lengths.shape[1]
    both = ("dp", "tensor")

    def moved(value):
        pattern = [
            (i * parts + j, ((i // 2) * 2 + j // half) * parts + (i % 2) * half + j % half)
            for i in range(rows_all)
            for j in range(parts)
            if i % 2 != j // half
        ]
        return lax.ppermute(value, both, pattern)

    def partner(value, b):
        pattern = [
            (i * parts + j, (i ^ (b // half)) * parts + (j // half) * half + ((j % half) ^ (b % half)))
            for i in range(rows_all)
            for j in range(parts)
        ]
        return lax.ppermute(value, both, pattern)

    def exchange(blocks):
        return [blocks[0]] + [partner(blocks[b], b) for b in range(1, parts)]

    same_core = [[2 * i + k for i in range(columns)] for k in range(2)]

    other_lengths = partner(lengths, half)
    other_steps = partner(time_steps, half)
    lengths_work = jnp.where(stays, lengths, other_lengths)[0]
    steps_work = jnp.where(stays, time_steps, other_steps)[0]

    time_rate = jnp.exp(
        -math.log(10000.0) * (jnp.arange(w_ada.shape[0] // 2, dtype=F32) / (w_ada.shape[0] // 2))
    )

    def embed(steps):
        phases = steps.astype(F32)[:, None] * time_rate
        return jax.nn.silu(jnp.concatenate([jnp.sin(phases), jnp.cos(phases)], axis=-1)).astype(BF)

    def wide_segment(row_lengths, places):
        segment, _, _ = frame_marks(row_lengths, places, utt)
        return jnp.broadcast_to(segment[:, None], (places.shape[0], LANES))

    spot = jnp.arange(frames, dtype=jnp.int32)
    mods_home = dot(embed(time_steps[0]), w_ada[:, : 2 * depth])
    qkv_rows = jnp.transpose(w_qkv, (0, 2, 1)).reshape(3 * ws, depth)
    rotary_rate = jnp.exp(-math.log(10000.0) * (2.0 * jnp.arange(HEAD_DIM // 2, dtype=F32) / HEAD_DIM))
    sign = jnp.where(jnp.arange(LANES) % HEAD_DIM < HEAD_DIM // 2, -1.0, 1.0).astype(F32)
    base_home, normed_all, cosine, sine, qmark, kmark, w_mine, w_out_all = front(
        jnp.cumsum(lengths_work, dtype=jnp.int32),
        inputs,
        skip_input,
        w_skip_in,
        w_skip_res,
        wide_segment(lengths[0], z * frames + spot),
        mods_home[:, :depth],
        mods_home[:, depth:],
        jnp.stack([jnp.tile(rotary_rate, 4), sign]),
        qkv_rows,
        w_out,
        parts,
    )

    per_q, per_o = 3 * ws // rows_all, ws // rows_all
    units = w_down.shape[0]
    per_u = units // rows_all
    slice_feed = jnp.concatenate(
        [
            jnp.transpose(lax.dynamic_slice_in_dim(w_up, d * per_u, per_u, 1)),
            lax.dynamic_slice_in_dim(w_down, d * per_u, per_u, 0),
        ]
    )
    feed_rows = lax.all_gather(slice_feed, "tensor")
    feed_rows = lax.all_gather(after(feed_rows, base_home), "dp", axis_index_groups=same_core)
    feed_rows = feed_rows.reshape(columns * parts, 2, per_u, depth)

    cotangent = after(cotangent, base_home)
    cot = jnp.where(stays, cotangent, moved(cotangent))
    base_in = moved(after(base_home, cot))

    silu_work = embed(steps_work)
    mods = dot(silu_work, w_ada)
    shift_one, scale_one, shift_two, scale_two = [mods[:, k * depth : (k + 1) * depth] for k in range(4)]
    segment_here = wide_segment(lengths_work, part * frames + spot)

    qkv = project(normed_all.reshape(length, depth), w_mine, cosine, sine, pairs)

    def ranges(size, other):
        per = frames // size
        stored = jnp.arange(length // size, dtype=jnp.int32)
        natural = (part ^ (stored // per)) * per + stored % per
        return block_ranges(lengths_work, natural, size, other)

    own = jnp.stack([part.astype(jnp.int32), stays.astype(jnp.int32)])
    wide = min(frames, 1024)
    low, high = ranges(wide, wide)
    bq, bk = 512, 512
    low_back, high_back = ranges(bk, bq)
    ctx_pairs, lse_pairs, ctx_mine = [], [], []
    for pair in range(pairs):
        ctx, lse = attend(
            after(qkv, cot) if pair == pairs - 1 else qkv, pair, qmark, kmark, own, low, high, wide, wide, frames
        )
        ctx_pairs.append(ctx)
        lse_pairs.append(lse)
        if pair < pairs - 1:
            ctx_mine += exchange([ctx[b] for b in range(parts)])
    hidden, ffn_in, ctx_last = join(
        ctx_mine, ctx_pairs[-1], w_out_all, base_home, base_in, segment_here, shift_two, scale_two, pairs, parts
    )

    cot_other = partner(cot, half)
    spare = max(per_o, 16)
    heads = qkv_rows.reshape(3 * pairs, 8, LANES // 8, depth)
    out_own, out_send, gin_own, gin_send, grad_feed, w_heads = feed(
        ffn_in, cot, cot_other, feed_rows, heads, spare, parts
    )
    grad_hidden, low_grad, block_out, sums_two, *grad_context = turn(
        own, gin_own, partner(gin_send, half), out_own, partner(out_send, half), hidden, cot, skip_input, segment_here,
        scale_two,
        w_out_all, pairs, parts,
    )

    grad_feed = out_grad(low_grad, ctx_mine, ctx_last, grad_feed, 2 * per_u, pairs, parts, columns)
    grad_feed = grad_feed.reshape(columns, parts, 2 * per_u + spare, depth)
    feed_sum = lax.psum_scatter(grad_feed, "dp", scatter_dimension=0, axis_index_groups=same_core)
    feed_shard = lax.psum_scatter(feed_sum, "tensor", scatter_dimension=0)

    grad_parts = exchange(grad_context)
    grad_mine = []
    for pair in range(pairs):
        grad = jnp.stack([block[pair] for block in grad_parts])
        if pair == pairs - 1 and pairs > 1:
            grad = after(grad, feed_sum)
        grads = attend_back(
            qkv, pair, grad, ctx_pairs[pair], lse_pairs[pair], qmark, kmark, cosine, sine, own,
            low_back, high_back, bq, bk, utt, frames,
        )
        grad_mine.append(grads)

    returned = []
    for grads in grad_mine[:-1]:
        returned += exchange([grads[b] for b in range(parts)])
    block_out_in, skips_in = moved(block_out)
    grad_base, grad_qkv, sums_one, shards, inputs_in = finish(
        returned, grad_mine, normed_all, w_heads, base_home, base_in, grad_hidden, inputs, feed_shard.reshape(-1, depth), segment_here,
        scale_one, pairs, parts, rows_all,
    )
    shards = jnp.transpose(shards.reshape((2, columns) + shards.shape[1:]), (1, 0, 2, 3))
    grad_up, grad_down = spread_out(shards.reshape((rows_all,) + shards.shape[2:]), per_u)
    grad_out = shards[:, :, 2 * per_u : 2 * per_u + per_o].reshape(ws, depth).astype(F32)
    silu_rows = jnp.pad(silu_work.astype(F32) * (1.0 / parts), ((0, 0), (0, depth - silu_work.shape[1])))
    skip_sum, all_sums, grad_base_in = sums(
        inputs, inputs_in, skip_input, skips_in, grad_base, jnp.concatenate([sums_one, sums_two, silu_rows]),
        rows_all, parts,
    )
    grad_qkv = grad_qkv.reshape(-1, 3, ws, grad_qkv.shape[1])
    grad_qkv = jnp.transpose(grad_qkv, (1, 0, 3, 2)).reshape(3, depth, ws).astype(F32)
    grad_skip = skip_sum.astype(F32)
    grad_base_home = jnp.where(stays, grad_base, grad_base_in)
    grad_inputs = dot(grad_base_home, w_skip_in, NT)
    grad_skips = dot(grad_base_home, w_skip_res, NT)
    block_out = jnp.where(stays, block_out[0], block_out_in).astype(F32)

    all_sums = all_sums.reshape(rows_all, 5, utt, depth)
    silu_all = all_sums[:, 4, :, : w_ada.shape[0]].reshape(rows_all * utt, w_ada.shape[0])
    all_sums = jnp.concatenate([all_sums[:, k] for k in range(4)], axis=-1).reshape(rows_all * utt, 4 * depth)
    grad_ada = jnp.einsum("ut,um->tm", silu_all, all_sums, precision=lax.Precision.HIGHEST)

    return (
        block_out[None],
        grad_inputs[None],
        grad_skips[None],
        grad_skip[0],
        grad_skip[1],
        grad_ada,
        grad_qkv,
        grad_out,
        grad_up,
        grad_down,
    )


def solution(mesh):
    placed = (
        P("dp", "tensor", None),
        P("dp", "tensor", None),
        P("dp", None),
        P("dp", None),
        P(),
        P(),
        P(),
        P(None, None, "tensor"),
        P("tensor", None),
        P(None, "tensor"),
        P("tensor", None),
        P("dp", "tensor", None),
    )
    return jax.shard_map(
        on_device,
        mesh=mesh,
        in_specs=placed,
        out_specs=(
            P("dp", "tensor", None),
            P("dp", "tensor", None),
            P("dp", "tensor", None),
            P(),
            P(),
            P(),
            P(None, None, "tensor"),
            P("tensor", None),
            P(None, "tensor"),
            P("tensor", None),
        ),
        check_vma=False,
    )
```
